32 devices in a mesh: dom: 2 (over core), gx: 4 (over z), yz: 4 (over y, x).
Axes of the slice: x: 2, y: 2, z: 4, core: 2. Of those that a mesh axis runs over, the one named last changes fastest.
Arguments:
- field_state: float32 [2, 8, 64, 64, 128], P('dom', None, 'gx', 'yz'), as said below
- shell_owner: int32 [4, 4, 8], P('gx'), may hold values from 0 to 3, as said below
- block_sources: int32 [4, 4, 2, 4], P('gx', 'yz'), may hold values from -1 to 7, as said below
- block_targets: int32 [4, 4, 2], P('gx', 'yz'), may hold values from -1 to 63, as said below
- interp_weights: bfloat16 [4, 4, 2, 4, 512, 512], P('gx', 'yz'), as said below
Outputs:
- new_state: float32 [2, 8, 64, 64, 128], P('dom', None, 'gx', 'yz')
The draws below stay inside these ranges and needn't reach their ends.
Inputs may be any that keep to these rules, and one draw needn't show every extreme that they name: `shell_owner`: entry [g, t, b] is the yz index of the heliosphere device, at the same gx index g, that owns shell block b of the corona device (g, t). No corona device gives more than 2 of its blocks to one owner, and in every gx index some owner receives exactly 2 blocks from each corona device of that gx index. `block_sources`: the live entries of device (g, y) come first in slot order and are the positions 0 to R - 1 of its owned list, each exactly once, R being the number of shell blocks it owns; the rest are -1. `block_targets`: live slots of one device name distinct local blocks; a slot is -1 exactly when all its sources are -1. `field_state`: each cell holds conserved variables of a state with positive density and pressure. `interp_weights`: for every target cell the entries over all 4 source blocks and their cells sum to less than one.
All inputs are finite; a program needn't handle non-finite values.
Results may differ from the reference program's by a relative error of at most 0.002.
Values may be sent and summed in bfloat16 or wider, within the bound.
No kernel may reach another device: no remote copies, remote signals or barrier semaphores. Data moves between devices by JAX's collectives and lax.ppermute only.
A program may use at most 64 MiB of HBM per device.

```python
import jax
import jax.numpy as jnp
from jax import lax

NCOMP = 8
BLK = 8
LX = 16
LY = 16
LZ = 128
SR = 2
CAP = 2
K = 4
SB = 8
BC = 512
NBD = 2
NX = 64
NY = 64
NS = 128
N_GX = 4
N_YZ = 4


HEAT_RATIO = 5.0 / 3.0


def routing(key):
    base_key = jax.random.fold_in(key, 11)
    hot_key = jax.random.fold_in(base_key, 1)
    pick_key = jax.random.fold_in(base_key, 2)
    order_key = jax.random.fold_in(base_key, 3)
    rank_key = jax.random.fold_in(base_key, 4)
    place_key = jax.random.fold_in(base_key, 5)
    hot_owner = jax.random.randint(hot_key, (N_GX,), 0, N_YZ).astype(jnp.int32)
    pool_size = (N_YZ - 1) * CAP

    def sender_row(sender_index):
        hot_one = hot_owner[sender_index // N_YZ]
        owner_pool = (hot_one + 1 + jnp.arange(pool_size, dtype=jnp.int32) // CAP) % N_YZ
        chosen = jax.random.permutation(jax.random.fold_in(pick_key, sender_index), owner_pool)[:SB - CAP]
        entries = jnp.concatenate([jnp.full((CAP,), hot_one, jnp.int32), chosen.astype(jnp.int32)])
        return jax.random.permutation(jax.random.fold_in(order_key, sender_index), entries).astype(jnp.int32)
    owner_table = jax.vmap(sender_row)(jnp.arange(N_GX * N_YZ, dtype=jnp.int32)).reshape(N_GX, N_YZ, SB)
    slot_total = NBD * K
    block_total = LX // BLK * (LY // BLK) * (LZ // BLK)

    def receiver_row(device_index):
        column_owners = owner_table[device_index // N_YZ].reshape(-1)
        yz_index = device_index % N_YZ
        owned_count = jnp.sum((column_owners == yz_index).astype(jnp.int32))
        scores = jax.random.permutation(jax.random.fold_in(rank_key, device_index), slot_total).astype(jnp.int32)
        positions = jnp.arange(slot_total, dtype=jnp.int32)
        live_entry = positions < owned_count
        sort_order = jnp.argsort(jnp.where(live_entry, scores, slot_total + positions), stable=True).astype(jnp.int32)
        sources = jnp.where(live_entry, sort_order, -1).astype(jnp.int32).reshape(NBD, K)
        block_perm = jax.random.permutation(jax.random.fold_in(place_key, device_index), block_total)[:NBD].astype(jnp.int32)
        block_perm = jnp.where(block_perm == block_total - 1, block_perm[0], block_perm)
        block_perm = block_perm.at[0].set(block_total - 1)
        live_slot = jnp.arange(NBD, dtype=jnp.int32) * K < owned_count
        targets = jnp.where(live_slot, block_perm, -1).astype(jnp.int32)
        return (sources, targets)
    sources, targets = jax.vmap(receiver_row)(jnp.arange(N_GX * N_YZ, dtype=jnp.int32))
    return (owner_table, sources.reshape(N_GX, N_YZ, NBD, K), targets.reshape(N_GX, N_YZ, NBD))


def draw_shell_owner(key, part):
    return routing(key)[0]


def draw_block_sources(key, part):
    return routing(key)[1]


def draw_block_targets(key, part):
    return routing(key)[2]


def draw_interp_weights(key, part):
    perm_key = jax.random.fold_in(key, 31)
    share_key = jax.random.fold_in(key, 32)
    rest_key = jax.random.fold_in(key, 33)
    share_low = 0.5
    share_high = 1.5
    share_unit = 0.13
    rest_total = 0.17
    block_count = N_GX * N_YZ * NBD * K

    def one_block(block_index):
        target_source = jax.random.permutation(jax.random.fold_in(perm_key, block_index), BC).astype(jnp.int32)
        share = jax.random.uniform(jax.random.fold_in(share_key, block_index), (BC,), jnp.float32, share_low, share_high) * share_unit
        spread = jax.random.uniform(jax.random.fold_in(rest_key, block_index), (BC, BC), jnp.float32, 0.0, 2.0 * rest_total / (K * BC))
        source_spots = jnp.arange(BC, dtype=jnp.int32)
        leading = jnp.where(source_spots[:, None] == target_source[None, :], share[None, :], 0.0)
        return (spread + leading).astype(jnp.bfloat16)
    blocks = lax.map(one_block, jnp.arange(block_count, dtype=jnp.int32))
    return blocks.reshape(N_GX, N_YZ, NBD, K, BC, BC)


def draw_field_state(key, part):
    grid_shape = (2, NX, NY, LZ)
    density_key = jax.random.fold_in(key, 21)
    velocity_key = jax.random.fold_in(key, 22)
    magnetic_key = jax.random.fold_in(key, 23)
    pressure_key = jax.random.fold_in(key, 24)
    density = jnp.exp(jax.random.uniform(density_key, grid_shape, jnp.float32, jnp.log(0.5), jnp.log(2.0)))
    velocity = jax.random.uniform(velocity_key, (3,) + grid_shape, jnp.float32, -1.0, 1.0)
    magnetic = jax.random.uniform(magnetic_key, (3,) + grid_shape, jnp.float32, -1.0, 1.0)
    pressure = jnp.exp(jax.random.uniform(pressure_key, grid_shape, jnp.float32, jnp.log(0.5), jnp.log(2.0)))
    energy = pressure / (HEAT_RATIO - 1.0) + 0.5 * density * jnp.sum(velocity * velocity, axis=0)
    energy = energy + 0.5 * jnp.sum(magnetic * magnetic, axis=0)
    parts_list = [density, density * velocity[0], density * velocity[1], density * velocity[2], magnetic[0], magnetic[1], magnetic[2], energy]
    return jnp.stack(parts_list, axis=1).astype(jnp.float32)


def setup_inputs(seed: int = 0) -> dict:
    streams_of = jax.random.split(jax.random.key(seed), 6)
    field_state = draw_field_state(jax.random.fold_in(streams_of[5], 71), 0)
    shell_owner = draw_shell_owner(jax.random.fold_in(streams_of[5], 71), 0)
    block_sources = draw_block_sources(jax.random.fold_in(streams_of[5], 71), 0)
    block_targets = draw_block_targets(jax.random.fold_in(streams_of[5], 71), 0)
    interp_weights = draw_interp_weights(jax.random.fold_in(streams_of[5], 71), 0)
    return dict(field_state=field_state, shell_owner=shell_owner, block_sources=block_sources, block_targets=block_targets, interp_weights=interp_weights)


HEAT_RATIO = 5.0 / 3.0
CORONA_RATIO = 0.04
HELIO_RATIO = 0.03

def direction_flux(grid_cells, direction):
    density = grid_cells[0]
    momentum = grid_cells[1:4]
    magnetic = grid_cells[4:7]
    energy = grid_cells[7]
    velocity = momentum / density
    field_sq = lax.optimization_barrier(jnp.sum(magnetic * magnetic, axis=0))
    pressure = (HEAT_RATIO - 1.0) * (energy - 0.5 * lax.optimization_barrier(jnp.sum(momentum * velocity, axis=0)) - 0.5 * field_sq)
    total_pressure = pressure + 0.5 * field_sq
    normal_speed = velocity[direction]
    normal_field = magnetic[direction]
    velocity_dot = lax.optimization_barrier(jnp.sum(velocity * magnetic, axis=0))
    flux_list = [momentum[direction]]
    for other in range(3):
        term = momentum[other] * normal_speed - magnetic[other] * normal_field
        if other == direction:
            term = term + total_pressure
        flux_list.append(term)
    for other in range(3):
        flux_list.append(normal_speed * magnetic[other] - normal_field * velocity[other])
    flux_list.append((energy + total_pressure) * normal_speed - normal_field * velocity_dot)
    wave_speed = jnp.abs(normal_speed) + jnp.sqrt((HEAT_RATIO * pressure + field_sq) / density)
    return (jnp.stack(flux_list), wave_speed)

def interface_change(padded_line, direction):
    phys_flux, wave_speed = direction_flux(padded_line, direction)
    array_dim = direction + 1
    cell_count = padded_line.shape[array_dim]
    low_cells = lax.slice_in_dim(padded_line, 0, cell_count - 1, axis=array_dim)
    high_cells = lax.slice_in_dim(padded_line, 1, cell_count, axis=array_dim)
    low_flux = lax.slice_in_dim(phys_flux, 0, cell_count - 1, axis=array_dim)
    high_flux = lax.slice_in_dim(phys_flux, 1, cell_count, axis=array_dim)
    low_speed = lax.slice_in_dim(wave_speed, 0, cell_count - 1, axis=direction)
    high_speed = lax.slice_in_dim(wave_speed, 1, cell_count, axis=direction)
    fastest = jnp.maximum(low_speed, high_speed)
    face_flux = 0.5 * (low_flux + high_flux) - 0.5 * fastest[None] * (high_cells - low_cells)
    upper_face = lax.slice_in_dim(face_flux, 1, cell_count - 1, axis=array_dim)
    lower_face = lax.slice_in_dim(face_flux, 0, cell_count - 2, axis=array_dim)
    return upper_face - lower_face

def advance(line_set, inner_cells, step_ratio):
    change = interface_change(line_set[0], 0) + interface_change(line_set[1], 1)
    change = change + interface_change(line_set[2], 2)
    return inner_cells - step_ratio * change

def evolve(domain_grid, wrap_x, step_ratio):
    if wrap_x:
        padded = jnp.pad(domain_grid, ((0, 0), (1, 1), (0, 0), (0, 0)), mode='wrap')
    else:
        padded = jnp.pad(domain_grid, ((0, 0), (1, 1), (0, 0), (0, 0)), mode='edge')
    padded = jnp.pad(padded, ((0, 0), (0, 0), (1, 1), (1, 1)), mode='edge')

    def slab_update(slab_index):
        slab_cells = lax.dynamic_slice_in_dim(padded, slab_index * LX, LX + 2, 1)
        line_set = (slab_cells[:, :, 1:-1, 1:-1], slab_cells[:, 1:-1, :, 1:-1], slab_cells[:, 1:-1, 1:-1, :])
        return advance(line_set, slab_cells[:, 1:-1, 1:-1, 1:-1], step_ratio)
    slab_stack = lax.map(slab_update, jnp.arange(N_GX, dtype=jnp.int32))
    return jnp.transpose(slab_stack, (1, 0, 2, 3, 4)).reshape(NCOMP, NX, NY, LZ)

def reference(field_state, shell_owner, block_sources, block_targets, interp_weights):
    corona = field_state[0]
    helio_grid = field_state[1]
    per_x = LX // BLK
    per_y = LY // BLK
    per_z = LZ // BLK
    shell_cells = corona[:, :, :, LZ - SR * BLK:]
    shell_cells = shell_cells.reshape(NCOMP, N_GX, per_x, BLK, N_YZ, per_y, BLK, SR, BLK)
    shell_cells = shell_cells.transpose(1, 4, 2, 5, 7, 0, 3, 6, 8).reshape(NS, NCOMP, BC).astype(jnp.bfloat16)

    def owned_list(device_index):
        column_owners = shell_owner[device_index // N_YZ].reshape(-1)
        yz_index = device_index % N_YZ
        all_spots = jnp.arange(N_YZ * SB, dtype=jnp.int32)
        sort_keys = jnp.where(column_owners == yz_index, all_spots, N_YZ * SB + all_spots)
        sort_order = jnp.argsort(sort_keys, stable=True).astype(jnp.int32)
        return device_index // N_YZ * (N_YZ * SB) + sort_order
    owned_ids = jax.vmap(owned_list)(jnp.arange(N_GX * N_YZ, dtype=jnp.int32))
    raw_sources = block_sources.reshape(N_GX * N_YZ, NBD * K)
    global_ids = jnp.take_along_axis(owned_ids, jnp.maximum(raw_sources, 0), axis=1)
    global_ids = jnp.where(raw_sources >= 0, global_ids, -1).reshape(-1, K)
    flat_weights = interp_weights.reshape(-1, K, BC, BC)

    def one_slot(slot_item):
        slot_sources, slot_weights = slot_item
        picked = shell_cells[jnp.maximum(slot_sources, 0)]
        picked = jnp.where((slot_sources >= 0)[:, None, None], picked, jnp.zeros_like(picked))
        return jnp.einsum('kcs,kst->ct', picked.astype(jnp.float32), slot_weights.astype(jnp.float32), precision=lax.Precision.HIGHEST)
    boundary_blocks = lax.map(one_slot, (global_ids, flat_weights))
    slot_index = jnp.arange(N_GX * N_YZ * NBD, dtype=jnp.int32)
    device_index = slot_index // NBD
    target_block = block_targets.reshape(-1).astype(jnp.int32)
    block_spot = jnp.maximum(target_block, 0)
    base_x = device_index // N_YZ * LX + block_spot // (per_y * per_z) * BLK
    base_y = device_index % N_YZ * LY + block_spot // per_z % per_y * BLK
    base_z = block_spot % per_z * BLK
    offsets = jnp.arange(BC, dtype=jnp.int32)
    cell_x = base_x[:, None] + offsets[None, :] // (BLK * BLK)
    cell_y = base_y[:, None] + offsets[None, :] // BLK % BLK
    cell_z = base_z[:, None] + offsets[None, :] % BLK
    cell_x = jnp.where(target_block[:, None] >= 0, cell_x, NX)
    helio_grid = helio_grid.at[:, cell_x, cell_y, cell_z].set(jnp.transpose(boundary_blocks, (1, 0, 2)), mode='drop')
    new_corona = evolve(corona, True, CORONA_RATIO)
    new_helio = evolve(helio_grid, False, HELIO_RATIO)
    return jnp.stack([new_corona, new_helio])
```

```python
import functools

import jax
import jax.numpy as jnp
from jax import lax
from jax.experimental import pallas as pl
from jax.experimental.pallas import tpu as pltpu
from jax.sharding import PartitionSpec as P

BLK = 8
SR = 2
CAP = 2
LANES = 128

HEAT_RATIO = 5.0 / 3.0
CORONA_RATIO = 0.04
HELIO_RATIO = 0.03

VM = pl.BlockSpec(memory_space=pltpu.VMEM)
SM = pl.BlockSpec(memory_space=pltpu.SMEM)


def partner(index, step, count):
    if count & (count - 1) == 0:
        return index ^ step
    return (index + step) % count


def sender(index, step, count):
    if count & (count - 1) == 0:
        return index ^ step
    return (index - step + count) % count


def pack_kernel(dims, owner_ref, grid_ref, *rest):
    ncomp, len_x, len_y, len_z, n_yz, shells = dims
    outs, (blocks, send) = rest[:n_yz], rest[n_yz:]
    me = lax.axis_index("yz")

    @pl.when(lax.axis_index("dom") == 0)
    def _():
        n_bx, n_by, half = len_x // BLK, len_y // BLK, BLK // 2
        plane = len_x * len_y
        z_from = len_z - SR * BLK
        row_z = lax.broadcasted_iota(jnp.int32, (LANES, SR * LANES), 0) + (len_z - LANES)
        column = lax.broadcasted_iota(jnp.int32, (LANES, SR * LANES), 1)
        hit = row_z == z_from + column // LANES * BLK + column % BLK
        place = column % LANES // BLK
        total = jnp.zeros((n_bx * n_by * half * ncomp, SR * LANES), jnp.float32)
        for ap in range(2):
            for cy in range(BLK):
                pieces = []
                for bx in range(n_bx):
                    for by in range(n_by):
                        for a2 in range(half):
                            first = (bx * BLK + a2 * 2 + ap) * len_y + by * BLK + cy
                            pieces.append(grid_ref[pl.ds(first, ncomp, stride=plane), :])
                cells = jnp.concatenate(pieces, axis=0).astype(jnp.bfloat16)
                pick = jnp.where(hit & (place == ap * BLK + cy), 1.0, 0.0).astype(jnp.bfloat16)
                total = total + jnp.dot(cells, pick, preferred_element_type=jnp.float32)
        rows = half * ncomp
        for column_block in range(n_bx * n_by):
            for br in range(SR):
                blocks[column_block * SR + br] = total[
                    column_block * rows : (column_block + 1) * rows, br * LANES : (br + 1) * LANES
                ].astype(jnp.bfloat16)
        send[...] = jnp.zeros_like(send)
        for b in range(shells):
            owner = owner_ref[me * shells + b]
            rank = jnp.int32(0)
            for other in range(b):
                rank = rank + jnp.where(owner_ref[me * shells + other] == owner, 1, 0)
            if n_yz & (n_yz - 1) == 0:
                step = owner ^ me
            else:
                step = lax.rem(owner - me + n_yz, n_yz)
            spot = jnp.clip(step * CAP + rank, 0, n_yz * CAP - 1)
            send[spot] = blocks[b]
        for step in range(n_yz):
            for slot in range(CAP):
                outs[step][slot * rows : (slot + 1) * rows, :] = send[step * CAP + slot]


def fill_kernel(dims, owner_ref, source_ref, target_ref, weight_ref, grid_ref, *rest):
    ncomp, len_x, len_y, len_z, n_yz, shells, slots, depth = dims
    got = rest[:n_yz]
    filled, x_low, x_high, y_low, y_high, held, result, table = rest[n_yz:]
    me = lax.axis_index("yz")
    half = BLK // 2
    rows = half * ncomp
    plane = len_x * len_y

    filled[...] = grid_ref[...]

    @pl.when(lax.axis_index("dom") == 1)
    def _():
        for step in range(n_yz):
            for slot in range(CAP):
                held[step * CAP + slot] = got[step][slot * rows : (slot + 1) * rows, :].astype(jnp.float32)
        position = jnp.int32(0)
        for t in range(n_yz):
            if n_yz & (n_yz - 1) == 0:
                step = t ^ me
            else:
                step = lax.rem(me - t + n_yz, n_yz)
            rank = jnp.int32(0)
            for b in range(shells):
                table[jnp.minimum(position, n_yz * CAP)] = step * CAP + jnp.minimum(rank, CAP - 1)
                mine = jnp.where(owner_ref[t * shells + b] == me, 1, 0)
                position = position + mine
                rank = rank + mine
        lines = []
        for j in range(slots):
            total = jnp.zeros((ncomp, BLK * BLK * BLK), jnp.float32)
            for k in range(depth):
                entry = source_ref[j * depth + k]
                live = entry >= 0
                spot = jnp.where(live, table[jnp.clip(entry, 0, n_yz * CAP)], 0)
                block = held[spot]
                cells = jnp.concatenate(
                    [block[a2 * ncomp : (a2 + 1) * ncomp, :] for a2 in range(half)], axis=1
                )
                cells = jnp.where(live, cells, 0.0).astype(jnp.bfloat16)
                total = total + jnp.dot(
                    cells, weight_ref[j * depth + k], preferred_element_type=jnp.float32
                )
            lines += [total[:, a2 * LANES : (a2 + 1) * LANES] for a2 in range(half)]
        lines = jnp.concatenate(lines, axis=0)
        top = lines.astype(jnp.bfloat16)
        rest = lines - top.astype(jnp.float32)
        middle = rest.astype(jnp.bfloat16)
        bottom = (rest - middle.astype(jnp.float32)).astype(jnp.bfloat16)
        lines = jnp.concatenate([top, middle, bottom], axis=0)
        count = slots * rows
        from_lane = lax.broadcasted_iota(jnp.int32, (LANES, LANES), 0)
        to_lane = lax.broadcasted_iota(jnp.int32, (LANES, LANES), 1)
        same = from_lane % BLK == to_lane % BLK
        for m in range(2 * BLK):
            spread = jnp.where(same & (from_lane // BLK == m), 1.0, 0.0).astype(jnp.bfloat16)
            parts = jnp.dot(lines, spread, preferred_element_type=jnp.float32)
            result[m] = parts[:count] + parts[count : 2 * count] + parts[2 * count :]
        lane = lax.broadcasted_iota(jnp.int32, (ncomp, LANES), 1)
        per_y, per_z = len_y // BLK, len_z // BLK
        for j in range(slots):
            target = target_ref[j]

            @pl.when(target >= 0)
            def _():
                block_x = target // (per_y * per_z)
                block_y = target // per_z % per_y
                z_from = target % per_z * BLK
                inside = (lane >= z_from) & (lane < z_from + BLK)
                first = block_x * BLK * len_y + block_y * BLK
                for a in range(BLK):
                    for cy in range(BLK):
                        spot = pl.ds(first + a * len_y + cy, ncomp, stride=plane)
                        row = j * rows + a // 2 * ncomp
                        new = result[a % 2 * BLK + cy, row : row + ncomp, :]
                        filled[spot, :] = jnp.where(inside, new, filled[spot, :])

    for c in range(ncomp):
        x_low[c * len_y : (c + 1) * len_y, :] = filled[c * plane : c * plane + len_y, :]
        x_high[c * len_y : (c + 1) * len_y, :] = filled[(c + 1) * plane - len_y : (c + 1) * plane, :]
        y_low[c * len_x : (c + 1) * len_x, :] = filled[pl.ds(c * plane, len_x, stride=len_y), :]
        y_high[c * len_x : (c + 1) * len_x, :] = filled[
            pl.ds(c * plane + len_y - 1, len_x, stride=len_y), :
        ]


def primitives(cells):
    density, energy = cells[0], cells[7]
    momentum, magnetic = cells[1:4], cells[4:7]
    inverse = 1.0 / density
    velocity = [m * inverse for m in momentum]
    field_sq = magnetic[0] * magnetic[0] + magnetic[1] * magnetic[1] + magnetic[2] * magnetic[2]
    kinetic = momentum[0] * velocity[0] + momentum[1] * velocity[1] + momentum[2] * velocity[2]
    pressure = (HEAT_RATIO - 1.0) * (energy - 0.5 * kinetic - 0.5 * field_sq)
    total_pressure = pressure + 0.5 * field_sq
    dot = velocity[0] * magnetic[0] + velocity[1] * magnetic[1] + velocity[2] * magnetic[2]
    fast = jnp.sqrt((HEAT_RATIO * pressure + field_sq) * inverse)
    return velocity, total_pressure, energy + total_pressure, dot, fast


def flux_of(cells, prims, direction):
    velocity, total_pressure, enthalpy, dot, fast = prims
    momentum, magnetic = cells[1:4], cells[4:7]
    speed, field = velocity[direction], magnetic[direction]
    flux = [momentum[direction]]
    for other in range(3):
        term = momentum[other] * speed - magnetic[other] * field
        flux.append(term + total_pressure if other == direction else term)
    for other in range(3):
        if other == direction:
            flux.append(None)
        else:
            flux.append(speed * magnetic[other] - field * velocity[other])
    flux.append(enthalpy * speed - field * dot)
    return flux, jnp.abs(speed) + fast


def face_sum(low, high):
    fastest = jnp.maximum(low[2], high[2])
    out = []
    for u_low, u_high, f_low, f_high in zip(low[0], high[0], low[1], high[1]):
        face = fastest * (u_high - u_low)
        out.append(face if f_low is None else face - (f_low + f_high))
    return out


def inner_kernel(dims, filled, out):
    ncomp, len_x, len_y, len_z = dims
    plane = len_x * len_y
    half_ratio = jnp.where(lax.axis_index("dom") == 0, 0.5 * CORONA_RATIO, 0.5 * HELIO_RATIO).astype(jnp.float32)
    shape = (len_y, LANES)
    row = lax.broadcasted_iota(jnp.int32, shape, 0)
    lane = lax.broadcasted_iota(jnp.int32, shape, 1)

    def load(x):
        return [filled[pl.ds(pl.multiple_of(c * plane + x * len_y, BLK), len_y), :] for c in range(ncomp)]

    def shift_up(values, axis, size):
        return [None if v is None else pltpu.roll(v, size - 1, axis) for v in values]

    def step(x, carry, last):
        cells, prims, flux_x, speed_x, low_x = carry
        if last:
            high_x = [jnp.zeros(shape, jnp.float32)] * ncomp
            next_carry = None
        else:
            next_cells = load(x + 1)
            next_prims = primitives(next_cells)
            next_flux, next_speed = flux_of(next_cells, next_prims, 0)
            high_x = face_sum((cells, flux_x, speed_x), (next_cells, next_flux, next_speed))
            next_carry = (next_cells, next_prims, next_flux, next_speed, high_x)
        total = [high - low for high, low in zip(high_x, low_x)]
        flux, speed = flux_of(cells, prims, 1)
        beside = (shift_up(cells, 0, len_y), shift_up(flux, 0, len_y), pltpu.roll(speed, len_y - 1, 0))
        for c, face in enumerate(face_sum((cells, flux, speed), beside)):
            face = jnp.where(row == len_y - 1, 0.0, face)
            total[c] = total[c] + (face - pltpu.roll(face, 1, 0))
        flux, speed = flux_of(cells, prims, 2)
        beside = (shift_up(cells, 1, LANES), shift_up(flux, 1, LANES), pltpu.roll(speed, LANES - 1, 1))
        for c, face in enumerate(face_sum((cells, flux, speed), beside)):
            own = jnp.zeros(shape, jnp.float32) if flux[c] is None else -2.0 * flux[c]
            face = jnp.where(lane == LANES - 1, own, face)
            below = jnp.where(lane == 0, own, pltpu.roll(face, 1, 1))
            total[c] = total[c] + (face - below)
        for c in range(ncomp):
            spot = pl.ds(pl.multiple_of(c * plane + x * len_y, BLK), len_y)
            out[spot, :] = cells[c] + half_ratio * total[c]
        return next_carry

    cells = load(0)
    prims = primitives(cells)
    flux, speed = flux_of(cells, prims, 0)
    flux[4] = None
    zero = [jnp.zeros(shape, jnp.float32)] * ncomp
    carry = (cells, prims, flux, speed, zero)

    def pack(carry):
        cells, prims, flux, speed, low = carry
        return cells, prims, [f for f in flux if f is not None], speed, low

    def unpack(carry):
        cells, prims, flux, speed, low = carry
        return cells, prims, flux[:4] + [None] + flux[4:], speed, low

    carry = lax.fori_loop(
        0, len_x - 1, lambda x, carry: pack(step(x, unpack(carry), False)), pack(carry)
    )
    step(len_x - 1, unpack(carry), True)


def edge_kernel(dims, part, x_low, x_high, y_low, y_high, from_x_low, from_x_high, from_y_low, from_y_high, out):
    ncomp, len_x, len_y, len_z = dims
    plane = len_x * len_y
    helio = lax.axis_index("dom") == 1
    column, line = lax.axis_index("gx"), lax.axis_index("yz")
    half_ratio = jnp.where(helio, 0.5 * HELIO_RATIO, 0.5 * CORONA_RATIO).astype(jnp.float32)
    out[...] = part[...]

    def state(cells, direction):
        flux, speed = flux_of(cells, primitives(cells), direction)
        return cells, flux, speed

    def faces(own_ref, other_ref, at_end, direction, upper, size):
        own = [own_ref[c * size : (c + 1) * size, :] for c in range(ncomp)]
        other = [other_ref[c * size : (c + 1) * size, :] for c in range(ncomp)]
        other = [jnp.where(at_end, u, v) for u, v in zip(own, other)]
        own, other = state(own, direction), state(other, direction)
        if upper:
            return [half_ratio * f for f in face_sum(own, other)]
        return [-half_ratio * f for f in face_sum(other, own)]

    low_end = helio & (column == 0)
    high_end = helio & (column == lax.axis_size("gx") - 1)
    for c, change in enumerate(faces(x_low, from_x_low, low_end, 0, False, len_y)):
        spot = pl.ds(c * plane, len_y)
        out[spot, :] = out[spot, :] + change
    for c, change in enumerate(faces(x_high, from_x_high, high_end, 0, True, len_y)):
        spot = pl.ds((c + 1) * plane - len_y, len_y)
        out[spot, :] = out[spot, :] + change
    low_end = line == 0
    high_end = line == lax.axis_size("yz") - 1
    for c, change in enumerate(faces(y_low, from_y_low, low_end, 1, False, len_x)):
        spot = pl.ds(c * plane, len_x, stride=len_y)
        out[spot, :] = out[spot, :] + change
    for c, change in enumerate(faces(y_high, from_y_high, high_end, 1, True, len_x)):
        spot = pl.ds(c * plane + len_y - 1, len_x, stride=len_y)
        out[spot, :] = out[spot, :] + change


def local(field_state, shell_owner, block_sources, block_targets, interp_weights):
    _, ncomp, len_x, len_y, len_z = field_state.shape
    n_gx, n_yz = lax.axis_size("gx"), lax.axis_size("yz")
    shells = shell_owner.shape[2]
    slots, depth = block_sources.shape[2:]
    volume = BLK * BLK * BLK
    cell_rows = ncomp * len_x * len_y
    grid = field_state.reshape(cell_rows, len_z)
    owners = shell_owner.reshape(-1)
    sources = block_sources.reshape(-1)
    targets = block_targets.reshape(-1)
    weights = interp_weights.reshape(slots * depth, volume, volume)
    rows = BLK // 2 * ncomp
    dims = (ncomp, len_x, len_y, len_z)

    packed = pl.pallas_call(
        functools.partial(pack_kernel, dims + (n_yz, shells)),
        out_shape=[jax.ShapeDtypeStruct((CAP * rows, LANES), jnp.bfloat16)] * n_yz,
        in_specs=[SM, VM],
        out_specs=[VM] * n_yz,
        scratch_shapes=[
            pltpu.VMEM((shells, rows, LANES), jnp.bfloat16),
            pltpu.VMEM((n_yz * CAP, rows, LANES), jnp.bfloat16),
        ],
        name="pack_shell",
    )(owners, grid)

    moved = []
    for step in range(n_yz):
        pairs = [(t, n_yz + partner(t, step, n_yz)) for t in range(n_yz)]
        pairs = pairs + [(b, a) for a, b in pairs]
        moved.append(lax.ppermute(packed[step], ("dom", "yz"), pairs))

    face_x = jax.ShapeDtypeStruct((ncomp * len_y, len_z), jnp.float32)
    face_y = jax.ShapeDtypeStruct((ncomp * len_x, len_z), jnp.float32)
    filled, x_low, x_high, y_low, y_high = pl.pallas_call(
        functools.partial(fill_kernel, dims + (n_yz, shells, slots, depth)),
        out_shape=[jax.ShapeDtypeStruct((cell_rows, len_z), jnp.float32), face_x, face_x, face_y, face_y],
        in_specs=[SM, SM, SM, VM, VM] + [VM] * n_yz,
        out_specs=[VM] * 5,
        scratch_shapes=[
            pltpu.VMEM((n_yz * CAP, rows, LANES), jnp.float32),
            pltpu.VMEM((2 * BLK, slots * rows, LANES), jnp.float32),
            pltpu.SMEM((n_yz * CAP + 1,), jnp.int32),
        ],
        compiler_params=pltpu.CompilerParams(vmem_limit_bytes=24 * 2**20),
        name="fill_blocks",
    )(owners, sources, targets, weights, grid, *moved)

    up_x = [(i, (i + 1) % n_gx) for i in range(n_gx)]
    down_x = [(b, a) for a, b in up_x]
    up_y = [(i, (i + 1) % n_yz) for i in range(n_yz)]
    down_y = [(b, a) for a, b in up_y]
    from_x_low = lax.ppermute(x_high, "gx", up_x)
    from_x_high = lax.ppermute(x_low, "gx", down_x)
    from_y_low = lax.ppermute(y_high, "yz", up_y)
    from_y_high = lax.ppermute(y_low, "yz", down_y)

    part = pl.pallas_call(
        functools.partial(inner_kernel, dims),
        out_shape=jax.ShapeDtypeStruct((cell_rows, len_z), jnp.float32),
        in_specs=[VM],
        out_specs=VM,
        cost_estimate=pl.CostEstimate(flops=300 * cell_rows * len_z, bytes_accessed=8 * cell_rows * len_z, transcendentals=0),
        name="inner_faces",
    )(filled)

    updated = pl.pallas_call(
        functools.partial(edge_kernel, dims),
        out_shape=jax.ShapeDtypeStruct((cell_rows, len_z), jnp.float32),
        in_specs=[VM] * 9,
        out_specs=VM,
        name="edge_faces",
    )(part, x_low, x_high, y_low, y_high, from_x_low, from_x_high, from_y_low, from_y_high)
    return updated.reshape(1, ncomp, len_x, len_y, len_z)


def solution(mesh):
    placed = (
        P("dom", None, "gx", "yz", None),
        P("gx", None, None),
        P("gx", "yz", None, None),
        P("gx", "yz", None),
        P("gx", "yz", None, None, None, None),
    )
    return jax.shard_map(
        local,
        mesh=mesh,
        in_specs=placed,
        out_specs=P("dom", None, "gx", "yz", None),
        check_vma=False,
    )
```

```python
import functools

import jax
import jax.numpy as jnp
from jax import lax
from jax.experimental import pallas as pl
from jax.experimental.pallas import tpu as pltpu
from jax.sharding import PartitionSpec as P

BLK = 8
SR = 2
CAP = 2
LANES = 128
MIB = 2**20
VMEM_BYTES = 64 * MIB

HEAT_RATIO = 5.0 / 3.0
CORONA_RATIO = 0.04
HELIO_RATIO = 0.03

VM = pl.BlockSpec(memory_space=pltpu.VMEM)
HB = pl.BlockSpec(memory_space=pltpu.HBM)


def partner(index, step, count):
    if count & (count - 1) == 0:
        return index ^ step
    return (index + step) % count


def pack_kernel(dims, owner_hbm, source_hbm, target_hbm, grid_hbm, *rest):
    ncomp, len_x, len_y, len_z, n_yz, shells, slots, depth = dims
    outs, plan = rest[:n_yz], rest[n_yz]
    grid_ref, owner_ref, source_ref, target_ref, table, blocks, send, sems = rest[n_yz + 1 :]
    me = lax.axis_index("yz")
    grid_copy = pltpu.make_async_copy(grid_hbm, grid_ref, sems.at[0])
    copies = [
        pltpu.make_async_copy(owner_hbm, owner_ref, sems.at[1]),
        pltpu.make_async_copy(source_hbm, source_ref, sems.at[2]),
        pltpu.make_async_copy(target_hbm, target_ref, sems.at[3]),
    ]

    @pl.when(lax.axis_index("dom") == 1)
    def _():
        for copy in copies:
            copy.start()
        for copy in copies:
            copy.wait()
        position = jnp.int32(0)
        for t in range(n_yz):
            if n_yz & (n_yz - 1) == 0:
                step = t ^ me
            else:
                step = lax.rem(me - t + n_yz, n_yz)
            rank = jnp.int32(0)
            for b in range(shells):
                table[jnp.minimum(position, n_yz * CAP)] = step * CAP + jnp.minimum(rank, CAP - 1)
                mine = jnp.where(owner_ref[0, t, b] == me, 1, 0)
                position = position + mine
                rank = rank + mine
        for j in range(slots):
            for k in range(depth):
                entry = source_ref[0, 0, j, k]
                spot = jnp.where(entry >= 0, table[jnp.clip(entry, 0, n_yz * CAP)], -1)
                plan[j * depth + k : j * depth + k + 1, :] = jnp.full((1, LANES), spot, jnp.int32)
            plan[slots * depth + j : slots * depth + j + 1, :] = jnp.full((1, LANES), target_ref[0, 0, j], jnp.int32)

    @pl.when(lax.axis_index("dom") == 0)
    def _():
        grid_copy.start()
        copies[0].start()
        grid_copy.wait()
        copies[0].wait()
        n_bx, n_by, half = len_x // BLK, len_y // BLK, BLK // 2
        plane = len_x * len_y
        z_from = len_z - SR * BLK
        row_z = lax.broadcasted_iota(jnp.int32, (LANES, SR * LANES), 0) + (len_z - LANES)
        column = lax.broadcasted_iota(jnp.int32, (LANES, SR * LANES), 1)
        hit = row_z == z_from + column // LANES * BLK + column % BLK
        place = column % LANES // BLK
        total = jnp.zeros((n_bx * n_by * half * ncomp, SR * LANES), jnp.float32)
        for ap in range(2):
            for cy in range(BLK):
                pieces = []
                for bx in range(n_bx):
                    for by in range(n_by):
                        for a2 in range(half):
                            first = (bx * BLK + a2 * 2 + ap) * len_y + by * BLK + cy
                            pieces.append(grid_ref[pl.ds(first, ncomp, stride=plane), :])
                cells = jnp.concatenate(pieces, axis=0).astype(jnp.bfloat16)
                pick = jnp.where(hit & (place == ap * BLK + cy), 1.0, 0.0).astype(jnp.bfloat16)
                total = total + jnp.dot(cells, pick, preferred_element_type=jnp.float32)
        rows = half * ncomp
        for column_block in range(n_bx * n_by):
            for br in range(SR):
                blocks[column_block * SR + br] = total[
                    column_block * rows : (column_block + 1) * rows, br * LANES : (br + 1) * LANES
                ].astype(jnp.bfloat16)
        send[...] = jnp.zeros_like(send)
        for b in range(shells):
            owner = owner_ref[0, me, b]
            rank = jnp.int32(0)
            for other in range(b):
                rank = rank + jnp.where(owner_ref[0, me, other] == owner, 1, 0)
            if n_yz & (n_yz - 1) == 0:
                step = owner ^ me
            else:
                step = lax.rem(owner - me + n_yz, n_yz)
            spot = jnp.clip(step * CAP + rank, 0, n_yz * CAP - 1)
            send[spot] = blocks[b]
        for step in range(n_yz):
            for slot in range(CAP):
                outs[step][slot * rows : (slot + 1) * rows, :] = send[step * CAP + slot]


def stage_kernel(count, *refs):
    sems = refs[-1]
    copies = [pltpu.make_async_copy(refs[i], refs[count + i], sems.at[i]) for i in range(count)]
    for copy in copies:
        copy.start()
    for copy in copies:
        copy.wait()


def fill_kernel(dims, plan_vmem, weight_ref, grid_ref, *rest):
    ncomp, len_x, len_y, len_z, n_yz, slots, depth = dims
    got = rest[:n_yz]
    filled, x_low, x_high, y_low, y_high, held, result, plan, sem = rest[n_yz:]
    half = BLK // 2
    rows = half * ncomp
    plane = len_x * len_y

    @pl.when(lax.axis_index("dom") == 1)
    def _():
        copy = pltpu.make_async_copy(plan_vmem, plan, sem)
        copy.start()
        for step in range(n_yz):
            for slot in range(CAP):
                held[step * CAP + slot] = got[step][slot * rows : (slot + 1) * rows, :].astype(jnp.float32)
        copy.wait()
        lines = []
        for j in range(slots):
            total = jnp.zeros((ncomp, BLK * BLK * BLK), jnp.float32)
            for k in range(depth):
                spot = plan[j * depth + k, 0]
                live = spot >= 0
                block = held[jnp.maximum(spot, 0)]
                cells = jnp.concatenate(
                    [block[a2 * ncomp : (a2 + 1) * ncomp, :] for a2 in range(half)], axis=1
                )
                cells = jnp.where(live, cells, 0.0).astype(jnp.bfloat16)
                total = total + jnp.dot(
                    cells, weight_ref[j * depth + k], preferred_element_type=jnp.float32
                )
            lines += [total[:, a2 * LANES : (a2 + 1) * LANES] for a2 in range(half)]
        lines = jnp.concatenate(lines, axis=0)
        top = lines.astype(jnp.bfloat16)
        rest = lines - top.astype(jnp.float32)
        middle = rest.astype(jnp.bfloat16)
        bottom = (rest - middle.astype(jnp.float32)).astype(jnp.bfloat16)
        lines = jnp.concatenate([top, middle, bottom], axis=0)
        count = slots * rows
        from_lane = lax.broadcasted_iota(jnp.int32, (LANES, LANES), 0)
        to_lane = lax.broadcasted_iota(jnp.int32, (LANES, LANES), 1)
        same = from_lane % BLK == to_lane % BLK
        for m in range(2 * BLK):
            spread = jnp.where(same & (from_lane // BLK == m), 1.0, 0.0).astype(jnp.bfloat16)
            parts = jnp.dot(lines, spread, preferred_element_type=jnp.float32)
            result[m] = parts[:count] + parts[count : 2 * count] + parts[2 * count :]
        lane = lax.broadcasted_iota(jnp.int32, (ncomp, LANES), 1)
        per_y, per_z = len_y // BLK, len_z // BLK
        for j in range(slots):
            target = plan[slots * depth + j, 0]

            @pl.when(target >= 0)
            def _():
                block_x = target // (per_y * per_z)
                block_y = target // per_z % per_y
                z_from = target % per_z * BLK
                inside = (lane >= z_from) & (lane < z_from + BLK)
                first = block_x * BLK * len_y + block_y * BLK
                for a in range(BLK):
                    for cy in range(BLK):
                        spot = pl.ds(first + a * len_y + cy, ncomp, stride=plane)
                        row = j * rows + a // 2 * ncomp
                        new = result[a % 2 * BLK + cy, row : row + ncomp, :]
                        filled[spot, :] = jnp.where(inside, new, filled[spot, :])

    for c in range(ncomp):
        x_low[c * len_y : (c + 1) * len_y, :] = filled[c * plane : c * plane + len_y, :]
        x_high[c * len_y : (c + 1) * len_y, :] = filled[(c + 1) * plane - len_y : (c + 1) * plane, :]
        y_low[c * len_x : (c + 1) * len_x, :] = filled[pl.ds(c * plane, len_x, stride=len_y), :]
        y_high[c * len_x : (c + 1) * len_x, :] = filled[
            pl.ds(c * plane + len_y - 1, len_x, stride=len_y), :
        ]


def primitives(cells):
    density, energy = cells[0], cells[7]
    momentum, magnetic = cells[1:4], cells[4:7]
    inverse = 1.0 / density
    velocity = [m * inverse for m in momentum]
    field_sq = magnetic[0] * magnetic[0] + magnetic[1] * magnetic[1] + magnetic[2] * magnetic[2]
    kinetic = momentum[0] * velocity[0] + momentum[1] * velocity[1] + momentum[2] * velocity[2]
    pressure = (HEAT_RATIO - 1.0) * (energy - 0.5 * kinetic - 0.5 * field_sq)
    total_pressure = pressure + 0.5 * field_sq
    dot = velocity[0] * magnetic[0] + velocity[1] * magnetic[1] + velocity[2] * magnetic[2]
    fast = jnp.sqrt((HEAT_RATIO * pressure + field_sq) * inverse)
    return velocity, total_pressure, energy + total_pressure, dot, fast


def flux_of(cells, prims, direction):
    velocity, total_pressure, enthalpy, dot, fast = prims
    momentum, magnetic = cells[1:4], cells[4:7]
    speed, field = velocity[direction], magnetic[direction]
    flux = [momentum[direction]]
    for other in range(3):
        term = momentum[other] * speed - magnetic[other] * field
        flux.append(term + total_pressure if other == direction else term)
    for other in range(3):
        if other == direction:
            flux.append(None)
        else:
            flux.append(speed * magnetic[other] - field * velocity[other])
    flux.append(enthalpy * speed - field * dot)
    return flux, jnp.abs(speed) + fast


def face_sum(low, high):
    fastest = jnp.maximum(low[2], high[2])
    out = []
    for u_low, u_high, f_low, f_high in zip(low[0], high[0], low[1], high[1]):
        face = fastest * (u_high - u_low)
        out.append(face if f_low is None else face - (f_low + f_high))
    return out


def inner_kernel(dims, filled, out):
    ncomp, len_x, len_y, len_z = dims
    plane = len_x * len_y
    half_ratio = jnp.where(lax.axis_index("dom") == 0, 0.5 * CORONA_RATIO, 0.5 * HELIO_RATIO).astype(jnp.float32)
    shape = (len_y, LANES)
    row = lax.broadcasted_iota(jnp.int32, shape, 0)
    lane = lax.broadcasted_iota(jnp.int32, shape, 1)

    def load(x):
        return [filled[pl.ds(pl.multiple_of(c * plane + x * len_y, BLK), len_y), :] for c in range(ncomp)]

    def shift_up(values, axis, size):
        return [None if v is None else pltpu.roll(v, size - 1, axis) for v in values]

    def step(x, carry, last):
        cells, prims, flux_x, speed_x, low_x = carry
        if last:
            high_x = [jnp.zeros(shape, jnp.float32)] * ncomp
            next_carry = None
        else:
            next_cells = load(x + 1)
            next_prims = primitives(next_cells)
            next_flux, next_speed = flux_of(next_cells, next_prims, 0)
            high_x = face_sum((cells, flux_x, speed_x), (next_cells, next_flux, next_speed))
            next_carry = (next_cells, next_prims, next_flux, next_speed, high_x)
        total = [high - low for high, low in zip(high_x, low_x)]
        flux, speed = flux_of(cells, prims, 1)
        beside = (shift_up(cells, 0, len_y), shift_up(flux, 0, len_y), pltpu.roll(speed, len_y - 1, 0))
        for c, face in enumerate(face_sum((cells, flux, speed), beside)):
            face = jnp.where(row == len_y - 1, 0.0, face)
            total[c] = total[c] + (face - pltpu.roll(face, 1, 0))
        flux, speed = flux_of(cells, prims, 2)
        beside = (shift_up(cells, 1, LANES), shift_up(flux, 1, LANES), pltpu.roll(speed, LANES - 1, 1))
        for c, face in enumerate(face_sum((cells, flux, speed), beside)):
            own = jnp.zeros(shape, jnp.float32) if flux[c] is None else -2.0 * flux[c]
            face = jnp.where(lane == LANES - 1, own, face)
            below = jnp.where(lane == 0, own, pltpu.roll(face, 1, 1))
            total[c] = total[c] + (face - below)
        for c in range(ncomp):
            spot = pl.ds(pl.multiple_of(c * plane + x * len_y, BLK), len_y)
            out[spot, :] = cells[c] + half_ratio * total[c]
        return next_carry

    cells = load(0)
    prims = primitives(cells)
    flux, speed = flux_of(cells, prims, 0)
    flux[4] = None
    zero = [jnp.zeros(shape, jnp.float32)] * ncomp
    carry = (cells, prims, flux, speed, zero)

    def pack(carry):
        cells, prims, flux, speed, low = carry
        return cells, prims, [f for f in flux if f is not None], speed, low

    def unpack(carry):
        cells, prims, flux, speed, low = carry
        return cells, prims, flux[:4] + [None] + flux[4:], speed, low

    carry = lax.fori_loop(
        0, len_x - 1, lambda x, carry: pack(step(x, unpack(carry), False)), pack(carry)
    )
    step(len_x - 1, unpack(carry), True)


def edge_kernel(dims, part, x_low, x_high, y_low, y_high, from_x_low, from_x_high, from_y_low, from_y_high, out):
    ncomp, len_x, len_y, len_z = dims
    plane = len_x * len_y
    helio = lax.axis_index("dom") == 1
    column, line = lax.axis_index("gx"), lax.axis_index("yz")
    half_ratio = jnp.where(helio, 0.5 * HELIO_RATIO, 0.5 * CORONA_RATIO).astype(jnp.float32)
    out[...] = part[...]

    def state(cells, direction):
        flux, speed = flux_of(cells, primitives(cells), direction)
        return cells, flux, speed

    def faces(own_ref, other_ref, at_end, direction, upper, size):
        own = [own_ref[c * size : (c + 1) * size, :] for c in range(ncomp)]
        other = [other_ref[c * size : (c + 1) * size, :] for c in range(ncomp)]
        other = [jnp.where(at_end, u, v) for u, v in zip(own, other)]
        own, other = state(own, direction), state(other, direction)
        if upper:
            return [half_ratio * f for f in face_sum(own, other)]
        return [-half_ratio * f for f in face_sum(other, own)]

    low_end = helio & (column == 0)
    high_end = helio & (column == lax.axis_size("gx") - 1)
    for c, change in enumerate(faces(x_low, from_x_low, low_end, 0, False, len_y)):
        spot = pl.ds(c * plane, len_y)
        out[spot, :] = out[spot, :] + change
    for c, change in enumerate(faces(x_high, from_x_high, high_end, 0, True, len_y)):
        spot = pl.ds((c + 1) * plane - len_y, len_y)
        out[spot, :] = out[spot, :] + change
    low_end = line == 0
    high_end = line == lax.axis_size("yz") - 1
    for c, change in enumerate(faces(y_low, from_y_low, low_end, 1, False, len_x)):
        spot = pl.ds(c * plane, len_x, stride=len_y)
        out[spot, :] = out[spot, :] + change
    for c, change in enumerate(faces(y_high, from_y_high, high_end, 1, True, len_x)):
        spot = pl.ds(c * plane + len_y - 1, len_x, stride=len_y)
        out[spot, :] = out[spot, :] + change


def local(field_state, shell_owner, block_sources, block_targets, interp_weights):
    _, ncomp, len_x, len_y, len_z = field_state.shape
    n_gx, n_yz = lax.axis_size("gx"), lax.axis_size("yz")
    shells = shell_owner.shape[2]
    slots, depth = block_sources.shape[2:]
    volume = BLK * BLK * BLK
    cell_rows = ncomp * len_x * len_y
    grid = field_state.reshape(cell_rows, len_z)
    weights = interp_weights.reshape(slots * depth, volume, volume)
    rows = BLK // 2 * ncomp
    dims = (ncomp, len_x, len_y, len_z)

    plan_rows = -(-slots * (depth + 1) // BLK) * BLK
    *packed, plan = pl.pallas_call(
        functools.partial(pack_kernel, dims + (n_yz, shells, slots, depth)),
        out_shape=[jax.ShapeDtypeStruct((CAP * rows, LANES), jnp.bfloat16)] * n_yz
        + [jax.ShapeDtypeStruct((plan_rows, LANES), jnp.int32)],
        in_specs=[HB] * 4,
        out_specs=[VM] * (n_yz + 1),
        scratch_shapes=[
            pltpu.VMEM((cell_rows, len_z), jnp.float32),
            pltpu.SMEM(shell_owner.shape, jnp.int32),
            pltpu.SMEM(block_sources.shape, jnp.int32),
            pltpu.SMEM(block_targets.shape, jnp.int32),
            pltpu.SMEM((n_yz * CAP + 1,), jnp.int32),
            pltpu.VMEM((shells, rows, LANES), jnp.bfloat16),
            pltpu.VMEM((n_yz * CAP, rows, LANES), jnp.bfloat16),
            pltpu.SemaphoreType.DMA((4,)),
        ],
        compiler_params=pltpu.CompilerParams(vmem_limit_bytes=VMEM_BYTES - 8 * MIB),
        name="pack_shell",
    )(shell_owner, block_sources, block_targets, grid)

    moved = []
    for step in range(n_yz):
        pairs = [(t, n_yz + partner(t, step, n_yz)) for t in range(n_yz)]
        pairs = pairs + [(b, a) for a, b in pairs]
        moved.append(lax.ppermute(packed[step], ("dom", "yz"), pairs))

    staged = (weights, grid, plan)
    staged_bytes = sum(x.size * x.dtype.itemsize for x in staged)
    weights, grid, plan = pl.pallas_call(
        functools.partial(stage_kernel, len(staged)),
        out_shape=[jax.ShapeDtypeStruct(x.shape, x.dtype) for x in staged],
        in_specs=[HB] * 3,
        out_specs=[VM] * 3,
        scratch_shapes=[pltpu.SemaphoreType.DMA((3,))],
        compiler_params=pltpu.CompilerParams(vmem_limit_bytes=VMEM_BYTES - 13 * staged_bytes // 4),
        cost_estimate=pl.CostEstimate(flops=0, bytes_accessed=4 * interp_weights.size, transcendentals=0),
        name="stage_operands",
    )(*staged)

    face_x = jax.ShapeDtypeStruct((ncomp * len_y, len_z), jnp.float32)
    face_y = jax.ShapeDtypeStruct((ncomp * len_x, len_z), jnp.float32)
    filled, x_low, x_high, y_low, y_high = pl.pallas_call(
        functools.partial(fill_kernel, dims + (n_yz, slots, depth)),
        out_shape=[jax.ShapeDtypeStruct((cell_rows, len_z), jnp.float32), face_x, face_x, face_y, face_y],
        in_specs=[VM, VM, VM] + [VM] * n_yz,
        out_specs=[VM] * 5,
        scratch_shapes=[
            pltpu.VMEM((n_yz * CAP, rows, LANES), jnp.float32),
            pltpu.VMEM((2 * BLK, slots * rows, LANES), jnp.float32),
            pltpu.SMEM((plan_rows, LANES), jnp.int32),
            pltpu.SemaphoreType.DMA,
        ],
        input_output_aliases={2: 0},
        compiler_params=pltpu.CompilerParams(vmem_limit_bytes=16 * MIB),
        name="fill_blocks",
    )(plan, weights, grid, *moved)

    up_x = [(i, (i + 1) % n_gx) for i in range(n_gx)]
    down_x = [(b, a) for a, b in up_x]
    up_y = [(i, (i + 1) % n_yz) for i in range(n_yz)]
    down_y = [(b, a) for a, b in up_y]
    from_x_low = lax.ppermute(x_high, "gx", up_x)
    from_x_high = lax.ppermute(x_low, "gx", down_x)
    from_y_low = lax.ppermute(y_high, "yz", up_y)
    from_y_high = lax.ppermute(y_low, "yz", down_y)

    part = pl.pallas_call(
        functools.partial(inner_kernel, dims),
        out_shape=jax.ShapeDtypeStruct((cell_rows, len_z), jnp.float32),
        in_specs=[VM],
        out_specs=VM,
        cost_estimate=pl.CostEstimate(flops=300 * cell_rows * len_z, bytes_accessed=8 * cell_rows * len_z, transcendentals=0),
        compiler_params=pltpu.CompilerParams(vmem_limit_bytes=8 * MIB),
        name="inner_faces",
    )(filled)

    updated = pl.pallas_call(
        functools.partial(edge_kernel, dims),
        out_shape=jax.ShapeDtypeStruct((cell_rows, len_z), jnp.float32),
        in_specs=[VM] * 9,
        out_specs=VM,
        compiler_params=pltpu.CompilerParams(vmem_limit_bytes=8 * MIB),
        name="edge_faces",
    )(part, x_low, x_high, y_low, y_high, from_x_low, from_x_high, from_y_low, from_y_high)
    return updated.reshape(1, ncomp, len_x, len_y, len_z)


def solution(mesh):
    placed = (
        P("dom", None, "gx", "yz", None),
        P("gx", None, None),
        P("gx", "yz", None, None),
        P("gx", "yz", None),
        P("gx", "yz", None, None, None, None),
    )
    return jax.shard_map(
        local,
        mesh=mesh,
        in_specs=placed,
        out_specs=P("dom", None, "gx", "yz", None),
        check_vma=False,
    )
```

```python
import functools

import jax
import jax.numpy as jnp
from jax import lax
from jax.experimental import pallas as pl
from jax.experimental.pallas import tpu as pltpu
from jax.sharding import PartitionSpec as P

BLK = 8
SR = 2
CAP = 2
LANES = 128
MIB = 2**20
VMEM_BYTES = 64 * MIB

HEAT_RATIO = 5.0 / 3.0
CORONA_RATIO = 0.04
HELIO_RATIO = 0.03

VM = pl.BlockSpec(memory_space=pltpu.VMEM)
HB = pl.BlockSpec(memory_space=pltpu.HBM)


def partner(index, step, count):
    if count & (count - 1) == 0:
        return index ^ step
    return (index + step) % count


def cycle(count):
    pairs = [(count + i, count + i + 1) for i in range(count - 1)] + [(2 * count - 1, count - 1)]
    return pairs + [(i + 1, i) for i in range(count - 1)] + [(0, count)]


def wrap_pairs(count):
    pairs = [(0, count - 1)]
    pairs += [(i, i + 1) for i in range(1, count - 2, 2)]
    pairs += [(count + i, count + i + 1) for i in range(0, count - 1, 2)]
    return pairs + [(b, a) for a, b in pairs]


def pack_kernel(dims, owner_hbm, source_hbm, target_hbm, grid_hbm, *rest):
    ncomp, len_x, len_y, len_z, n_yz, shells, slots, depth = dims
    outs, plan, wrap = rest[:n_yz], rest[n_yz], rest[n_yz + 1]
    grid_ref, owner_ref, source_ref, target_ref, table, spread, send, sems = rest[n_yz + 2 :]
    me = lax.axis_index("yz")
    plane = len_x * len_y
    grid_copies = [
        pltpu.make_async_copy(
            grid_hbm.at[pl.ds(c * plane, plane), :], grid_ref.at[pl.ds(c * plane, plane), :], sems.at[3 + c]
        )
        for c in range(ncomp)
    ]
    copies = [
        pltpu.make_async_copy(owner_hbm, owner_ref, sems.at[0]),
        pltpu.make_async_copy(source_hbm, source_ref, sems.at[1]),
        pltpu.make_async_copy(target_hbm, target_ref, sems.at[2]),
    ]

    @pl.when(lax.axis_index("dom") == 1)
    def _():
        for copy in copies:
            copy.start()
        for copy in copies:
            copy.wait()
        position = jnp.int32(0)
        for t in range(n_yz):
            if n_yz & (n_yz - 1) == 0:
                step = t ^ me
            else:
                step = lax.rem(me - t + n_yz, n_yz)
            rank = jnp.int32(0)
            for b in range(shells):
                table[jnp.minimum(position, n_yz * CAP)] = step * CAP + jnp.minimum(rank, CAP - 1)
                mine = jnp.where(owner_ref[0, t, b] == me, 1, 0)
                position = position + mine
                rank = rank + mine
        for j in range(slots):
            for k in range(depth):
                entry = source_ref[0, 0, j, k]
                spot = jnp.where(entry >= 0, table[jnp.clip(entry, 0, n_yz * CAP)], -1)
                plan[j * depth + k : j * depth + k + 1, :] = jnp.full((1, LANES), spot, jnp.int32)
            plan[slots * depth + j : slots * depth + j + 1, :] = jnp.full((1, LANES), target_ref[0, 0, j], jnp.int32)

    @pl.when(lax.axis_index("dom") == 0)
    def _():
        copies[0].start()
        for copy in grid_copies:
            copy.start()
        n_bx, n_by, half = len_x // BLK, len_y // BLK, BLK // 2
        z_from = len_z - SR * BLK
        row_z = lax.broadcasted_iota(jnp.int32, (LANES, SR * LANES), 0) + (len_z - LANES)
        column = lax.broadcasted_iota(jnp.int32, (LANES, SR * LANES), 1)
        hit = row_z == z_from + column // LANES * BLK + column % BLK
        place = jnp.where(hit, column % LANES // BLK, -1)
        for m in range(2 * BLK):
            spread[m] = jnp.where(place == m, 1.0, 0.0).astype(jnp.bfloat16)
        send[...] = jnp.zeros_like(send)
        copies[0].wait()
        spots = []
        for b in range(shells):
            owner = owner_ref[0, me, b]
            rank = jnp.int32(0)
            for other in range(b):
                rank = rank + jnp.where(owner_ref[0, me, other] == owner, 1, 0)
            if n_yz & (n_yz - 1) == 0:
                step = owner ^ me
            else:
                step = lax.rem(owner - me + n_yz, n_yz)
            spots.append(jnp.clip(step * CAP + rank, 0, n_yz * CAP - 1))
        for copy in grid_copies:
            copy.wait()
        total = jnp.zeros((n_bx * n_by * half * ncomp, SR * LANES), jnp.float32)
        for ap in range(2):
            for cy in range(BLK):
                pieces = []
                for bx in range(n_bx):
                    for by in range(n_by):
                        for a2 in range(half):
                            first = (bx * BLK + a2 * 2 + ap) * len_y + by * BLK + cy
                            pieces.append(grid_ref[pl.ds(first, ncomp, stride=plane), :])
                cells = jnp.concatenate(pieces, axis=0).astype(jnp.bfloat16)
                total = total + jnp.dot(cells, spread[ap * BLK + cy], preferred_element_type=jnp.float32)
        rows = half * ncomp
        total = total.astype(jnp.bfloat16)
        for b in range(shells):
            column_block, br = b // SR, b % SR
            send[spots[b]] = total[
                column_block * rows : (column_block + 1) * rows, br * LANES : (br + 1) * LANES
            ]
        for step in range(n_yz):
            for slot in range(CAP):
                outs[step][slot * rows : (slot + 1) * rows, :] = send[step * CAP + slot]
        end = jnp.where(lax.axis_index("gx") == 0, 0, plane - len_y)
        for c in range(ncomp):
            wrap[c * len_y : (c + 1) * len_y, :] = grid_ref[
                pl.ds(pl.multiple_of(c * plane + end, BLK), len_y), :
            ]


def stage_kernel(weight_hbm, grid_hbm, plan_hbm, weight_ref, grid_ref, plan_ref, sems):
    blocks = weight_ref.shape[0]
    grid_copy = pltpu.make_async_copy(grid_hbm, grid_ref, sems.at[blocks])
    copies = [pltpu.make_async_copy(weight_hbm.at[i], weight_ref.at[i], sems.at[i]) for i in range(blocks)]
    copies.append(pltpu.make_async_copy(plan_hbm, plan_ref, sems.at[blocks + 1]))
    grid_copy.start()

    @pl.when(lax.axis_index("dom") == 1)
    def _():
        for copy in copies:
            copy.start()
        for copy in copies:
            copy.wait()

    grid_copy.wait()


def fill_kernel(dims, plan_vmem, weight_ref, grid_ref, *rest):
    ncomp, len_x, len_y, len_z, n_yz, slots, depth = dims
    got = rest[:n_yz]
    filled, x_one, x_two, y_one, y_two, result, plan, sem = rest[n_yz:]
    half = BLK // 2
    rows = half * ncomp
    plane = len_x * len_y

    helio = lax.axis_index("dom") == 1

    @pl.when(helio)
    def _():
        copy = pltpu.make_async_copy(plan_vmem, plan, sem)
        copy.start()
        held = [
            got[step][slot * rows : (slot + 1) * rows, :].astype(jnp.float32)
            for step in range(n_yz)
            for slot in range(CAP)
        ]
        lines = []
        for j in range(slots):
            total = jnp.zeros((ncomp, BLK * BLK * BLK), jnp.float32)
            for k in range(depth):
                entry = j * depth + k
                spot = jnp.broadcast_to(plan_vmem[entry : entry + 1, :], (rows, LANES))
                block = jnp.zeros((rows, LANES), jnp.float32)
                for place, candidate in enumerate(held):
                    block = jnp.where(spot == place, candidate, block)
                cells = jnp.concatenate(
                    [block[a2 * ncomp : (a2 + 1) * ncomp, :] for a2 in range(half)], axis=1
                ).astype(jnp.bfloat16)
                total = total + jnp.dot(cells, weight_ref[entry], preferred_element_type=jnp.float32)
            lines += [total[:, a2 * LANES : (a2 + 1) * LANES] for a2 in range(half)]
        lines = jnp.concatenate(lines, axis=0)
        top = lines.astype(jnp.bfloat16)
        rest = lines - top.astype(jnp.float32)
        middle = rest.astype(jnp.bfloat16)
        bottom = (rest - middle.astype(jnp.float32)).astype(jnp.bfloat16)
        lines = jnp.concatenate([top, middle, bottom], axis=0)
        count = slots * rows
        from_lane = lax.broadcasted_iota(jnp.int32, (LANES, LANES), 0)
        to_lane = lax.broadcasted_iota(jnp.int32, (LANES, LANES), 1)
        same = from_lane % BLK == to_lane % BLK
        for m in range(2 * BLK):
            spread = jnp.where(same & (from_lane // BLK == m), 1.0, 0.0).astype(jnp.bfloat16)
            parts = jnp.dot(lines, spread, preferred_element_type=jnp.float32)
            result[m] = parts[:count] + parts[count : 2 * count] + parts[2 * count :]
        copy.wait()
        lane = lax.broadcasted_iota(jnp.int32, (ncomp, LANES), 1)
        per_y, per_z = len_y // BLK, len_z // BLK
        for j in range(slots):
            target = plan[slots * depth + j, 0]

            @pl.when(target >= 0)
            def _():
                block_x = target // (per_y * per_z)
                block_y = target // per_z % per_y
                z_from = target % per_z * BLK
                inside = (lane >= z_from) & (lane < z_from + BLK)
                first = block_x * BLK * len_y + block_y * BLK
                for a in range(BLK):
                    spots = [pl.ds(first + a * len_y + cy, ncomp, stride=plane) for cy in range(BLK)]
                    row = j * rows + a // 2 * ncomp
                    old = [filled[spot, :] for spot in spots]
                    new = [result[a % 2 * BLK + cy, row : row + ncomp, :] for cy in range(BLK)]
                    for spot, before, after in zip(spots, old, new):
                        filled[spot, :] = jnp.where(inside, after, before)

    def faces(x_low, x_high, y_low, y_high):
        for c in range(ncomp):
            x_low[c * len_y : (c + 1) * len_y, :] = filled[c * plane : c * plane + len_y, :]
            x_high[c * len_y : (c + 1) * len_y, :] = filled[(c + 1) * plane - len_y : (c + 1) * plane, :]
            y_low[c * len_x : (c + 1) * len_x, :] = filled[pl.ds(c * plane, len_x, stride=len_y), :]
            y_high[c * len_x : (c + 1) * len_x, :] = filled[
                pl.ds(c * plane + len_y - 1, len_x, stride=len_y), :
            ]

    @pl.when(helio)
    def _():
        faces(x_two, x_one, y_two, y_one)

    @pl.when(jnp.logical_not(helio))
    def _():
        faces(x_one, x_two, y_one, y_two)


def primitives(cells):
    density, energy = cells[0], cells[7]
    momentum, magnetic = cells[1:4], cells[4:7]
    inverse = 1.0 / density
    velocity = [m * inverse for m in momentum]
    field_sq = magnetic[0] * magnetic[0] + magnetic[1] * magnetic[1] + magnetic[2] * magnetic[2]
    kinetic = momentum[0] * velocity[0] + momentum[1] * velocity[1] + momentum[2] * velocity[2]
    pressure = (HEAT_RATIO - 1.0) * (energy - 0.5 * kinetic - 0.5 * field_sq)
    total_pressure = pressure + 0.5 * field_sq
    dot = velocity[0] * magnetic[0] + velocity[1] * magnetic[1] + velocity[2] * magnetic[2]
    fast = jnp.sqrt((HEAT_RATIO * pressure + field_sq) * inverse)
    return velocity, total_pressure, energy + total_pressure, dot, fast


def flux_of(cells, prims, direction):
    velocity, total_pressure, enthalpy, dot, fast = prims
    momentum, magnetic = cells[1:4], cells[4:7]
    speed, field = velocity[direction], magnetic[direction]
    flux = [momentum[direction]]
    for other in range(3):
        term = momentum[other] * speed - magnetic[other] * field
        flux.append(term + total_pressure if other == direction else term)
    for other in range(3):
        if other == direction:
            flux.append(None)
        else:
            flux.append(speed * magnetic[other] - field * velocity[other])
    flux.append(enthalpy * speed - field * dot)
    return flux, jnp.abs(speed) + fast


def face_sum(low, high):
    fastest = jnp.maximum(low[2], high[2])
    out = []
    for u_low, u_high, f_low, f_high in zip(low[0], high[0], low[1], high[1]):
        face = fastest * (u_high - u_low)
        out.append(face if f_low is None else face - (f_low + f_high))
    return out


def inner_kernel(dims, filled, out):
    ncomp, len_x, len_y, len_z = dims
    plane = len_x * len_y
    half_ratio = jnp.where(lax.axis_index("dom") == 0, 0.5 * CORONA_RATIO, 0.5 * HELIO_RATIO).astype(jnp.float32)
    shape = (len_y, LANES)
    row = lax.broadcasted_iota(jnp.int32, shape, 0)
    lane = lax.broadcasted_iota(jnp.int32, shape, 1)

    def load(x):
        return [filled[pl.ds(pl.multiple_of(c * plane + x * len_y, BLK), len_y), :] for c in range(ncomp)]

    def shift_up(values, axis, size):
        return [None if v is None else pltpu.roll(v, size - 1, axis) for v in values]

    def step(x, carry, last):
        cells, prims, flux_x, speed_x, low_x = carry
        if last:
            high_x = [jnp.zeros(shape, jnp.float32)] * ncomp
            next_carry = None
        else:
            next_cells = load(x + 1)
            next_prims = primitives(next_cells)
            next_flux, next_speed = flux_of(next_cells, next_prims, 0)
            high_x = face_sum((cells, flux_x, speed_x), (next_cells, next_flux, next_speed))
            next_carry = (next_cells, next_prims, next_flux, next_speed, high_x)
        total = [high - low for high, low in zip(high_x, low_x)]
        flux, speed = flux_of(cells, prims, 1)
        beside = (shift_up(cells, 0, len_y), shift_up(flux, 0, len_y), pltpu.roll(speed, len_y - 1, 0))
        for c, face in enumerate(face_sum((cells, flux, speed), beside)):
            face = jnp.where(row == len_y - 1, 0.0, face)
            total[c] = total[c] + (face - pltpu.roll(face, 1, 0))
        flux, speed = flux_of(cells, prims, 2)
        beside = (shift_up(cells, 1, LANES), shift_up(flux, 1, LANES), pltpu.roll(speed, LANES - 1, 1))
        for c, face in enumerate(face_sum((cells, flux, speed), beside)):
            own = jnp.zeros(shape, jnp.float32) if flux[c] is None else -2.0 * flux[c]
            face = jnp.where(lane == LANES - 1, own, face)
            below = jnp.where(lane == 0, own, pltpu.roll(face, 1, 1))
            total[c] = total[c] + (face - below)
        for c in range(ncomp):
            spot = pl.ds(pl.multiple_of(c * plane + x * len_y, BLK), len_y)
            out[spot, :] = cells[c] + half_ratio * total[c]
        return next_carry

    cells = load(0)
    prims = primitives(cells)
    flux, speed = flux_of(cells, prims, 0)
    flux[4] = None
    zero = [jnp.zeros(shape, jnp.float32)] * ncomp
    carry = (cells, prims, flux, speed, zero)

    def pack(carry):
        cells, prims, flux, speed, low = carry
        return cells, prims, [f for f in flux if f is not None], speed, low

    def unpack(carry):
        cells, prims, flux, speed, low = carry
        return cells, prims, flux[:4] + [None] + flux[4:], speed, low

    carry = lax.fori_loop(
        0, len_x - 1, lambda x, carry: pack(step(x, unpack(carry), False)), pack(carry)
    )
    step(len_x - 1, unpack(carry), True)


def edge_kernel(dims, part, x_one, x_two, y_one, y_two, from_x_one, from_x_two, from_y_one, from_y_two, wrap, out):
    ncomp, len_x, len_y, len_z = dims
    plane = len_x * len_y
    helio = lax.axis_index("dom") == 1
    half_ratio = jnp.where(helio, 0.5 * HELIO_RATIO, 0.5 * CORONA_RATIO).astype(jnp.float32)
    out[...] = part[...]

    def state(cells, direction):
        flux, speed = flux_of(cells, primitives(cells), direction)
        return cells, flux, speed

    def faces(own_ref, other_ref, end, end_ref, direction, upper, size):
        own = [own_ref[c * size : (c + 1) * size, :] for c in range(ncomp)]
        other = [other_ref[c * size : (c + 1) * size, :] for c in range(ncomp)]
        at_end = own if end_ref is None else [end_ref[c * size : (c + 1) * size, :] for c in range(ncomp)]
        other = [jnp.where(end, u, v) for u, v in zip(at_end, other)]
        own, other = state(own, direction), state(other, direction)
        if upper:
            return [half_ratio * f for f in face_sum(own, other)]
        return [-half_ratio * f for f in face_sum(other, own)]

    def both(x_low, x_high, y_low, y_high, from_x_low, from_x_high, from_y_low, from_y_high, x_end):
        column, line = lax.axis_index("gx"), lax.axis_index("yz")
        low_end, high_end = column == 0, column == lax.axis_size("gx") - 1
        for c, change in enumerate(faces(x_low, from_x_low, low_end, x_end, 0, False, len_y)):
            spot = pl.ds(c * plane, len_y)
            out[spot, :] = out[spot, :] + change
        for c, change in enumerate(faces(x_high, from_x_high, high_end, x_end, 0, True, len_y)):
            spot = pl.ds((c + 1) * plane - len_y, len_y)
            out[spot, :] = out[spot, :] + change
        low_end, high_end = line == 0, line == lax.axis_size("yz") - 1
        for c, change in enumerate(faces(y_low, from_y_low, low_end, None, 1, False, len_x)):
            spot = pl.ds(c * plane, len_x, stride=len_y)
            out[spot, :] = out[spot, :] + change
        for c, change in enumerate(faces(y_high, from_y_high, high_end, None, 1, True, len_x)):
            spot = pl.ds(c * plane + len_y - 1, len_x, stride=len_y)
            out[spot, :] = out[spot, :] + change

    @pl.when(helio)
    def _():
        both(x_two, x_one, y_two, y_one, from_x_one, from_x_two, from_y_one, from_y_two, None)

    @pl.when(jnp.logical_not(helio))
    def _():
        both(x_one, x_two, y_one, y_two, from_x_two, from_x_one, from_y_two, from_y_one, wrap)


def local(field_state, shell_owner, block_sources, block_targets, interp_weights):
    _, ncomp, len_x, len_y, len_z = field_state.shape
    n_gx, n_yz = lax.axis_size("gx"), lax.axis_size("yz")
    shells = shell_owner.shape[2]
    slots, depth = block_sources.shape[2:]
    volume = BLK * BLK * BLK
    cell_rows = ncomp * len_x * len_y
    grid = field_state.reshape(cell_rows, len_z)
    weights = interp_weights.reshape(slots * depth, volume, volume)
    rows = BLK // 2 * ncomp
    dims = (ncomp, len_x, len_y, len_z)

    plan_rows = -(-slots * (depth + 1) // BLK) * BLK
    face_x = jax.ShapeDtypeStruct((ncomp * len_y, len_z), jnp.float32)
    face_y = jax.ShapeDtypeStruct((ncomp * len_x, len_z), jnp.float32)
    *packed, plan, wrap = pl.pallas_call(
        functools.partial(pack_kernel, dims + (n_yz, shells, slots, depth)),
        out_shape=[jax.ShapeDtypeStruct((CAP * rows, LANES), jnp.bfloat16)] * n_yz
        + [jax.ShapeDtypeStruct((plan_rows, LANES), jnp.int32), face_x],
        in_specs=[HB] * 4,
        out_specs=[VM] * (n_yz + 2),
        scratch_shapes=[
            pltpu.VMEM((cell_rows, len_z), jnp.float32),
            pltpu.SMEM(shell_owner.shape, jnp.int32),
            pltpu.SMEM(block_sources.shape, jnp.int32),
            pltpu.SMEM(block_targets.shape, jnp.int32),
            pltpu.SMEM((n_yz * CAP + 1,), jnp.int32),
            pltpu.VMEM((2 * BLK, LANES, SR * LANES), jnp.bfloat16),
            pltpu.VMEM((n_yz * CAP, rows, LANES), jnp.bfloat16),
            pltpu.SemaphoreType.DMA((3 + ncomp,)),
        ],
        compiler_params=pltpu.CompilerParams(vmem_limit_bytes=VMEM_BYTES - 8 * MIB),
        name="pack_shell",
    )(shell_owner, block_sources, block_targets, grid)

    moved = []
    for step in range(n_yz):
        pairs = [(t, n_yz + partner(t, step, n_yz)) for t in range(n_yz)]
        pairs = pairs + [(b, a) for a, b in pairs]
        moved.append(lax.ppermute(packed[step], ("dom", "yz"), pairs))
    wrap = lax.ppermute(wrap, ("dom", "gx"), wrap_pairs(n_gx))

    staged = (weights, grid, plan)
    staged_bytes = sum(x.size * x.dtype.itemsize for x in staged)
    weights, grid, plan = pl.pallas_call(
        stage_kernel,
        out_shape=[jax.ShapeDtypeStruct(x.shape, x.dtype) for x in staged],
        in_specs=[HB] * 3,
        out_specs=[VM] * 3,
        scratch_shapes=[pltpu.SemaphoreType.DMA((slots * depth + 2,))],
        compiler_params=pltpu.CompilerParams(vmem_limit_bytes=VMEM_BYTES - 13 * staged_bytes // 4),
        cost_estimate=pl.CostEstimate(flops=0, bytes_accessed=4 * interp_weights.size, transcendentals=0),
        name="stage_operands",
    )(*staged)

    filled, x_one, x_two, y_one, y_two = pl.pallas_call(
        functools.partial(fill_kernel, dims + (n_yz, slots, depth)),
        out_shape=[jax.ShapeDtypeStruct((cell_rows, len_z), jnp.float32), face_x, face_x, face_y, face_y],
        in_specs=[VM, VM, VM] + [VM] * n_yz,
        out_specs=[VM] * 5,
        scratch_shapes=[
            pltpu.VMEM((2 * BLK, slots * rows, LANES), jnp.float32),
            pltpu.SMEM((plan_rows, LANES), jnp.int32),
            pltpu.SemaphoreType.DMA,
        ],
        input_output_aliases={2: 0},
        compiler_params=pltpu.CompilerParams(vmem_limit_bytes=16 * MIB),
        name="fill_blocks",
    )(plan, weights, grid, *moved)

    once_x, once_y = cycle(n_gx), cycle(n_yz)
    from_x_one = lax.ppermute(x_one, ("dom", "gx"), once_x)
    from_x_two = lax.ppermute(x_two, ("dom", "gx"), [(b, a) for a, b in once_x])
    from_y_one = lax.ppermute(y_one, ("dom", "yz"), once_y)
    from_y_two = lax.ppermute(y_two, ("dom", "yz"), [(b, a) for a, b in once_y])

    part = pl.pallas_call(
        functools.partial(inner_kernel, dims),
        out_shape=jax.ShapeDtypeStruct((cell_rows, len_z), jnp.float32),
        in_specs=[VM],
        out_specs=VM,
        cost_estimate=pl.CostEstimate(flops=300 * cell_rows * len_z, bytes_accessed=8 * cell_rows * len_z, transcendentals=0),
        compiler_params=pltpu.CompilerParams(vmem_limit_bytes=8 * MIB),
        name="inner_faces",
    )(filled)

    updated = pl.pallas_call(
        functools.partial(edge_kernel, dims),
        out_shape=jax.ShapeDtypeStruct((cell_rows, len_z), jnp.float32),
        in_specs=[VM] * 10,
        out_specs=VM,
        compiler_params=pltpu.CompilerParams(vmem_limit_bytes=8 * MIB),
        name="edge_faces",
    )(part, x_one, x_two, y_one, y_two, from_x_one, from_x_two, from_y_one, from_y_two, wrap)
    return updated.reshape(1, ncomp, len_x, len_y, len_z)


def solution(mesh):
    placed = (
        P("dom", None, "gx", "yz", None),
        P("gx", None, None),
        P("gx", "yz", None, None),
        P("gx", "yz", None),
        P("gx", "yz", None, None, None, None),
    )
    return jax.shard_map(
        local,
        mesh=mesh,
        in_specs=placed,
        out_specs=P("dom", None, "gx", "yz", None),
        check_vma=False,
    )
```

```python
import functools

import jax
import jax.numpy as jnp
from jax import lax
from jax.experimental import pallas as pl
from jax.experimental.pallas import tpu as pltpu
from jax.sharding import PartitionSpec as P

BLK = 8
SR = 2
CAP = 2
LANES = 128
MIB = 2**20
VMEM_BYTES = 64 * MIB

HEAT_RATIO = 5.0 / 3.0
CORONA_RATIO = 0.04
HELIO_RATIO = 0.03

VM = pl.BlockSpec(memory_space=pltpu.VMEM)
HB = pl.BlockSpec(memory_space=pltpu.HBM)


def partner(index, step, count):
    if count & (count - 1) == 0:
        return index ^ step
    return (index + step) % count


def cycle(count):
    pairs = [(count + i, count + i + 1) for i in range(count - 1)] + [(2 * count - 1, count - 1)]
    return pairs + [(i + 1, i) for i in range(count - 1)] + [(0, count)]


def wrap_pairs(count):
    pairs = [(0, count - 1)]
    pairs += [(i, i + 1) for i in range(1, count - 2, 2)]
    pairs += [(count + i, count + i + 1) for i in range(0, count - 1, 2)]
    return pairs + [(b, a) for a, b in pairs]


def pack_kernel(dims, owner_hbm, source_hbm, target_hbm, grid_hbm, *rest):
    ncomp, len_x, len_y, len_z, n_yz, shells, slots, depth = dims
    outs, carried, wrap = rest[:n_yz], rest[n_yz], rest[n_yz + 1]
    grid_ref, owner_ref, source_ref, target_ref, table, plan, spread, send, sems = rest[n_yz + 2 :]
    me = lax.axis_index("yz")
    plane = len_x * len_y
    cell_rows = ncomp * plane
    grid_copies = [
        pltpu.make_async_copy(
            grid_hbm.at[pl.ds(c * plane, plane), :], grid_ref.at[pl.ds(c * plane, plane), :], sems.at[5 + c]
        )
        for c in range(ncomp)
    ]
    end = jnp.where(lax.axis_index("gx") == 0, 0, plane - len_y)
    wrap_copies = [
        pltpu.make_async_copy(
            grid_ref.at[pl.ds(pl.multiple_of(c * plane + end, BLK), len_y), :],
            wrap.at[pl.ds(c * len_y, len_y), :],
            sems.at[5 + ncomp + c],
        )
        for c in range(ncomp)
    ]
    onward = [
        pltpu.make_async_copy(
            grid_ref.at[pl.ds(c * plane, plane), :], carried.at[pl.ds(c * plane, plane), :], sems.at[5 + 2 * ncomp + c]
        )
        for c in range(ncomp)
    ]
    copies = [
        pltpu.make_async_copy(owner_hbm, owner_ref, sems.at[0]),
        pltpu.make_async_copy(source_hbm, source_ref, sems.at[1]),
        pltpu.make_async_copy(target_hbm, target_ref, sems.at[2]),
    ]

    @pl.when(lax.axis_index("dom") == 1)
    def _():
        for copy in copies:
            copy.start()
        for copy in grid_copies:
            copy.start()
        for copy in copies:
            copy.wait()
        position = jnp.int32(0)
        for t in range(n_yz):
            if n_yz & (n_yz - 1) == 0:
                step = t ^ me
            else:
                step = lax.rem(me - t + n_yz, n_yz)
            rank = jnp.int32(0)
            for b in range(shells):
                table[jnp.minimum(position, n_yz * CAP)] = step * CAP + jnp.minimum(rank, CAP - 1)
                mine = jnp.where(owner_ref[0, t, b] == me, 1, 0)
                position = position + mine
                rank = rank + mine
        for j in range(slots):
            for k in range(depth):
                entry = source_ref[0, 0, j, k]
                spot = jnp.where(entry >= 0, table[jnp.clip(entry, 0, n_yz * CAP)], -1)
                plan[j * depth + k : j * depth + k + 1, :] = jnp.full((1, LANES), spot.astype(jnp.float32))
            plan[slots * depth + j : slots * depth + j + 1, :] = jnp.full(
                (1, LANES), target_ref[0, 0, j].astype(jnp.float32)
            )
        told = pltpu.make_async_copy(plan, carried.at[pl.ds(cell_rows, plan.shape[0]), :], sems.at[4])
        told.start()
        for arriving, leaving in zip(grid_copies, onward):
            arriving.wait()
            leaving.start()
        told.wait()
        for copy in onward:
            copy.wait()

    @pl.when(lax.axis_index("dom") == 0)
    def _():
        copies[0].start()
        for copy in grid_copies:
            copy.start()
        n_bx, n_by, half = len_x // BLK, len_y // BLK, BLK // 2
        z_from = len_z - SR * BLK
        row_z = lax.broadcasted_iota(jnp.int32, (LANES, SR * LANES), 0) + (len_z - LANES)
        column = lax.broadcasted_iota(jnp.int32, (LANES, SR * LANES), 1)
        hit = row_z == z_from + column // LANES * BLK + column % BLK
        place = jnp.where(hit, column % LANES // BLK, -1)
        for m in range(2 * BLK):
            spread[m] = jnp.where(place == m, 1.0, 0.0).astype(jnp.bfloat16)
        send[...] = jnp.zeros_like(send)
        copies[0].wait()
        spots = []
        for b in range(shells):
            owner = owner_ref[0, me, b]
            rank = jnp.int32(0)
            for other in range(b):
                rank = rank + jnp.where(owner_ref[0, me, other] == owner, 1, 0)
            if n_yz & (n_yz - 1) == 0:
                step = owner ^ me
            else:
                step = lax.rem(owner - me + n_yz, n_yz)
            spots.append(jnp.clip(step * CAP + rank, 0, n_yz * CAP - 1))
        for arriving, leaving, wrapping in zip(grid_copies, onward, wrap_copies):
            arriving.wait()
            leaving.start()
            wrapping.start()
        total = jnp.zeros((n_bx * n_by * half * ncomp, SR * LANES), jnp.float32)
        for ap in range(2):
            for cy in range(BLK):
                pieces = []
                for bx in range(n_bx):
                    for by in range(n_by):
                        for a2 in range(half):
                            first = (bx * BLK + a2 * 2 + ap) * len_y + by * BLK + cy
                            pieces.append(grid_ref[pl.ds(first, ncomp, stride=plane), :])
                cells = jnp.concatenate(pieces, axis=0).astype(jnp.bfloat16)
                total = total + jnp.dot(cells, spread[ap * BLK + cy], preferred_element_type=jnp.float32)
        rows = half * ncomp
        total = total.astype(jnp.bfloat16)
        for b in range(shells):
            column_block, br = b // SR, b % SR
            send[spots[b]] = total[
                column_block * rows : (column_block + 1) * rows, br * LANES : (br + 1) * LANES
            ]
        sends = [
            pltpu.make_async_copy(send.at[pl.ds(step * CAP, CAP)], outs[step], sems.at[5 + 3 * ncomp + step])
            for step in range(n_yz)
        ]
        for copy in sends:
            copy.start()
        for copy in wrap_copies + onward + sends:
            copy.wait()


def stage_kernel(weight_hbm, carried, weight_ref, grid_ref, plan_ref, sems):
    blocks, cell_rows, plan_rows = weight_ref.shape[0], grid_ref.shape[0], plan_ref.shape[0]
    grid_copy = pltpu.make_async_copy(carried.at[pl.ds(0, cell_rows), :], grid_ref, sems.at[blocks])
    copies = [pltpu.make_async_copy(weight_hbm.at[i], weight_ref.at[i], sems.at[i]) for i in range(blocks)]
    copies.append(
        pltpu.make_async_copy(carried.at[pl.ds(cell_rows, plan_rows), :], plan_ref, sems.at[blocks + 1])
    )
    grid_copy.start()

    @pl.when(lax.axis_index("dom") == 1)
    def _():
        for copy in copies:
            copy.start()
        for copy in copies:
            copy.wait()

    grid_copy.wait()


def fill_kernel(dims, plan_vmem, weight_ref, grid_ref, *rest):
    ncomp, len_x, len_y, len_z, n_yz, slots, depth = dims
    got = rest[:n_yz]
    filled, x_one, x_two, y_one, y_two, result, plan, sem = rest[n_yz:]
    half = BLK // 2
    rows = half * ncomp
    plane = len_x * len_y

    helio = lax.axis_index("dom") == 1

    @pl.when(helio)
    def _():
        copy = pltpu.make_async_copy(plan_vmem, plan, sem)
        copy.start()
        held = [
            got[step][slot].astype(jnp.float32)
            for step in range(n_yz)
            for slot in range(CAP)
        ]
        lines = []
        for j in range(slots):
            total = jnp.zeros((ncomp, BLK * BLK * BLK), jnp.float32)
            for k in range(depth):
                entry = j * depth + k
                spot = jnp.broadcast_to(plan_vmem[entry : entry + 1, :], (rows, LANES))
                block = jnp.zeros((rows, LANES), jnp.float32)
                for place, candidate in enumerate(held):
                    block = jnp.where(spot == float(place), candidate, block)
                cells = jnp.concatenate(
                    [block[a2 * ncomp : (a2 + 1) * ncomp, :] for a2 in range(half)], axis=1
                ).astype(jnp.bfloat16)
                total = total + jnp.dot(cells, weight_ref[entry], preferred_element_type=jnp.float32)
            lines += [total[:, a2 * LANES : (a2 + 1) * LANES] for a2 in range(half)]
        lines = jnp.concatenate(lines, axis=0)
        top = lines.astype(jnp.bfloat16)
        rest = lines - top.astype(jnp.float32)
        middle = rest.astype(jnp.bfloat16)
        bottom = (rest - middle.astype(jnp.float32)).astype(jnp.bfloat16)
        lines = jnp.concatenate([top, middle, bottom], axis=0)
        count = slots * rows
        from_lane = lax.broadcasted_iota(jnp.int32, (LANES, LANES), 0)
        to_lane = lax.broadcasted_iota(jnp.int32, (LANES, LANES), 1)
        same = from_lane % BLK == to_lane % BLK
        for m in range(2 * BLK):
            spread = jnp.where(same & (from_lane // BLK == m), 1.0, 0.0).astype(jnp.bfloat16)
            parts = jnp.dot(lines, spread, preferred_element_type=jnp.float32)
            result[m] = parts[:count] + parts[count : 2 * count] + parts[2 * count :]
        copy.wait()
        lane = lax.broadcasted_iota(jnp.int32, (ncomp, LANES), 1)
        per_y, per_z = len_y // BLK, len_z // BLK
        for j in range(slots):
            target = plan[slots * depth + j, 0].astype(jnp.int32)

            @pl.when(target >= 0)
            def _():
                block_x = target // (per_y * per_z)
                block_y = target // per_z % per_y
                z_from = target % per_z * BLK
                inside = (lane >= z_from) & (lane < z_from + BLK)
                first = block_x * BLK * len_y + block_y * BLK
                for a in range(BLK):
                    spots = [pl.ds(first + a * len_y + cy, ncomp, stride=plane) for cy in range(BLK)]
                    row = j * rows + a // 2 * ncomp
                    old = [filled[spot, :] for spot in spots]
                    new = [result[a % 2 * BLK + cy, row : row + ncomp, :] for cy in range(BLK)]
                    for spot, before, after in zip(spots, old, new):
                        filled[spot, :] = jnp.where(inside, after, before)

    def faces(x_low, x_high, y_low, y_high):
        for c in range(ncomp):
            x_low[c * len_y : (c + 1) * len_y, :] = filled[c * plane : c * plane + len_y, :]
            x_high[c * len_y : (c + 1) * len_y, :] = filled[(c + 1) * plane - len_y : (c + 1) * plane, :]
            y_low[c * len_x : (c + 1) * len_x, :] = filled[pl.ds(c * plane, len_x, stride=len_y), :]
            y_high[c * len_x : (c + 1) * len_x, :] = filled[
                pl.ds(c * plane + len_y - 1, len_x, stride=len_y), :
            ]

    @pl.when(helio)
    def _():
        faces(x_two, x_one, y_two, y_one)

    @pl.when(jnp.logical_not(helio))
    def _():
        faces(x_one, x_two, y_one, y_two)


def primitives(cells):
    density, energy = cells[0], cells[7]
    momentum, magnetic = cells[1:4], cells[4:7]
    inverse = 1.0 / density
    velocity = [m * inverse for m in momentum]
    field_sq = magnetic[0] * magnetic[0] + magnetic[1] * magnetic[1] + magnetic[2] * magnetic[2]
    kinetic = momentum[0] * velocity[0] + momentum[1] * velocity[1] + momentum[2] * velocity[2]
    pressure = (HEAT_RATIO - 1.0) * (energy - 0.5 * kinetic - 0.5 * field_sq)
    total_pressure = pressure + 0.5 * field_sq
    dot = velocity[0] * magnetic[0] + velocity[1] * magnetic[1] + velocity[2] * magnetic[2]
    fast = jnp.sqrt((HEAT_RATIO * pressure + field_sq) * inverse)
    return velocity, total_pressure, energy + total_pressure, dot, fast


def flux_of(cells, prims, direction):
    velocity, total_pressure, enthalpy, dot, fast = prims
    momentum, magnetic = cells[1:4], cells[4:7]
    speed, field = velocity[direction], magnetic[direction]
    flux = [momentum[direction]]
    for other in range(3):
        term = momentum[other] * speed - magnetic[other] * field
        flux.append(term + total_pressure if other == direction else term)
    for other in range(3):
        if other == direction:
            flux.append(None)
        else:
            flux.append(speed * magnetic[other] - field * velocity[other])
    flux.append(enthalpy * speed - field * dot)
    return flux, jnp.abs(speed) + fast


def face_sum(low, high):
    fastest = jnp.maximum(low[2], high[2])
    out = []
    for u_low, u_high, f_low, f_high in zip(low[0], high[0], low[1], high[1]):
        face = fastest * (u_high - u_low)
        out.append(face if f_low is None else face - (f_low + f_high))
    return out


def inner_kernel(dims, filled, out, rim_x_low, rim_x_high, rim_y_low, rim_y_high, part, sems):
    ncomp, len_x, len_y, len_z = dims
    plane = len_x * len_y
    half_ratio = jnp.where(lax.axis_index("dom") == 0, 0.5 * CORONA_RATIO, 0.5 * HELIO_RATIO).astype(jnp.float32)
    shape = (len_y, LANES)
    row = lax.broadcasted_iota(jnp.int32, shape, 0)
    lane = lax.broadcasted_iota(jnp.int32, shape, 1)

    def load(x):
        return [filled[pl.ds(pl.multiple_of(c * plane + x * len_y, BLK), len_y), :] for c in range(ncomp)]

    def shift_up(values, axis, size):
        return [None if v is None else pltpu.roll(v, size - 1, axis) for v in values]

    def step(x, carry, last):
        cells, prims, flux_x, speed_x, low_x = carry
        if last:
            high_x = [jnp.zeros(shape, jnp.float32)] * ncomp
            next_carry = None
        else:
            next_cells = load(x + 1)
            next_prims = primitives(next_cells)
            next_flux, next_speed = flux_of(next_cells, next_prims, 0)
            high_x = face_sum((cells, flux_x, speed_x), (next_cells, next_flux, next_speed))
            next_carry = (next_cells, next_prims, next_flux, next_speed, high_x)
        total = [high - low for high, low in zip(high_x, low_x)]
        flux, speed = flux_of(cells, prims, 1)
        beside = (shift_up(cells, 0, len_y), shift_up(flux, 0, len_y), pltpu.roll(speed, len_y - 1, 0))
        for c, face in enumerate(face_sum((cells, flux, speed), beside)):
            face = jnp.where(row == len_y - 1, 0.0, face)
            total[c] = total[c] + (face - pltpu.roll(face, 1, 0))
        flux, speed = flux_of(cells, prims, 2)
        beside = (shift_up(cells, 1, LANES), shift_up(flux, 1, LANES), pltpu.roll(speed, LANES - 1, 1))
        for c, face in enumerate(face_sum((cells, flux, speed), beside)):
            own = jnp.zeros(shape, jnp.float32) if flux[c] is None else -2.0 * flux[c]
            face = jnp.where(lane == LANES - 1, own, face)
            below = jnp.where(lane == 0, own, pltpu.roll(face, 1, 1))
            total[c] = total[c] + (face - below)
        for c in range(ncomp):
            part[c, x] = cells[c] + half_ratio * total[c]
        return next_carry

    def line_copy(x):
        return pltpu.make_async_copy(part.at[:, x], out.at[:, x], sems.at[x])

    cells = load(0)
    prims = primitives(cells)
    flux, speed = flux_of(cells, prims, 0)
    flux[4] = None
    zero = [jnp.zeros(shape, jnp.float32)] * ncomp
    carry = (cells, prims, flux, speed, zero)

    def pack(carry):
        cells, prims, flux, speed, low = carry
        return cells, prims, [f for f in flux if f is not None], speed, low

    def unpack(carry):
        cells, prims, flux, speed, low = carry
        return cells, prims, flux[:4] + [None] + flux[4:], speed, low

    def line(x, carry):
        carry = pack(step(x, unpack(carry), False))

        @pl.when(x > 0)
        def _():
            line_copy(x).start()

        return carry

    carry = lax.fori_loop(0, len_x - 1, line, pack(carry), unroll=3)
    step(len_x - 1, unpack(carry), True)
    for c in range(ncomp):
        rim_x_low[c] = part[c, 0]
        rim_x_high[c] = part[c, len_x - 1]
        rim_y_low[c] = part[c, :, 0, :]
        rim_y_high[c] = part[c, :, len_y - 1, :]
    for x in range(1, len_x - 1):
        line_copy(x).wait()


def edge_kernel(dims, part, rim_x_low, rim_x_high, rim_y_low, rim_y_high, *rest):
    ncomp, len_x, len_y, len_z = dims
    x_one, x_two, y_one, y_two, from_x_one, from_x_two, from_y_one, from_y_two, wrap = rest[:9]
    out, row_x_low, row_x_high, row_y_low, row_y_high, sems = rest[9:]
    helio = lax.axis_index("dom") == 1
    half_ratio = jnp.where(helio, 0.5 * HELIO_RATIO, 0.5 * CORONA_RATIO).astype(jnp.float32)

    def state(cells, direction):
        flux, speed = flux_of(cells, primitives(cells), direction)
        return cells, flux, speed

    def faces(own_ref, other_ref, end, end_ref, direction, upper, size):
        own = [own_ref[c * size : (c + 1) * size, :] for c in range(ncomp)]
        other = [other_ref[c * size : (c + 1) * size, :] for c in range(ncomp)]
        at_end = own if end_ref is None else [end_ref[c * size : (c + 1) * size, :] for c in range(ncomp)]
        other = [jnp.where(end, u, v) for u, v in zip(at_end, other)]
        own, other = state(own, direction), state(other, direction)
        if upper:
            return [half_ratio * f for f in face_sum(own, other)]
        return [-half_ratio * f for f in face_sum(other, own)]

    def both(x_low, x_high, y_low, y_high, from_x_low, from_x_high, from_y_low, from_y_high, x_end):
        column, line = lax.axis_index("gx"), lax.axis_index("yz")
        low_end, high_end = line == 0, line == lax.axis_size("yz") - 1
        y_lows = faces(y_low, from_y_low, low_end, None, 1, False, len_x)
        y_highs = faces(y_high, from_y_high, high_end, None, 1, True, len_x)
        for c in range(ncomp):
            row_y_low[c] = (rim_y_low[c] + y_lows[c])[1 : len_x - 1]
            row_y_high[c] = (rim_y_high[c] + y_highs[c])[1 : len_x - 1]
        inner_x = pl.ds(1, len_x - 2)
        copies = [
            pltpu.make_async_copy(row_y_low, out.at[:, inner_x, 0], sems.at[0]),
            pltpu.make_async_copy(row_y_high, out.at[:, inner_x, len_y - 1], sems.at[1]),
        ]
        copies[0].start()
        copies[1].start()
        low_end, high_end = column == 0, column == lax.axis_size("gx") - 1
        x_lows = faces(x_low, from_x_low, low_end, x_end, 0, False, len_y)
        x_highs = faces(x_high, from_x_high, high_end, x_end, 0, True, len_y)
        for row, rim, changes, x, sem in (
            (row_x_low, rim_x_low, x_lows, 0, 2),
            (row_x_high, rim_x_high, x_highs, len_x - 1, 3),
        ):
            for c in range(ncomp):
                row[c] = rim[c] + changes[c]
                row[c, 0:1] = row[c, 0:1] + y_lows[c][x : x + 1]
                row[c, len_y - 1 : len_y] = row[c, len_y - 1 : len_y] + y_highs[c][x : x + 1]
            copies.append(pltpu.make_async_copy(row, out.at[:, x], sems.at[sem]))
            copies[-1].start()
        for copy in copies:
            copy.wait()

    @pl.when(helio)
    def _():
        both(x_two, x_one, y_two, y_one, from_x_one, from_x_two, from_y_one, from_y_two, None)

    @pl.when(jnp.logical_not(helio))
    def _():
        both(x_one, x_two, y_one, y_two, from_x_two, from_x_one, from_y_two, from_y_one, wrap)


def local(field_state, shell_owner, block_sources, block_targets, interp_weights):
    _, ncomp, len_x, len_y, len_z = field_state.shape
    n_gx, n_yz = lax.axis_size("gx"), lax.axis_size("yz")
    shells = shell_owner.shape[2]
    slots, depth = block_sources.shape[2:]
    volume = BLK * BLK * BLK
    cell_rows = ncomp * len_x * len_y
    grid = field_state.reshape(cell_rows, len_z)
    weights = interp_weights.reshape(slots * depth, volume, volume)
    rows = BLK // 2 * ncomp
    dims = (ncomp, len_x, len_y, len_z)

    plan_rows = -(-slots * (depth + 1) // BLK) * BLK
    face_x = jax.ShapeDtypeStruct((ncomp * len_y, len_z), jnp.float32)
    face_y = jax.ShapeDtypeStruct((ncomp * len_x, len_z), jnp.float32)
    carried_rows = max(cell_rows + plan_rows, 8 * MIB // (4 * LANES))
    *packed, carried, wrap = pl.pallas_call(
        functools.partial(pack_kernel, dims + (n_yz, shells, slots, depth)),
        out_shape=[jax.ShapeDtypeStruct((CAP, rows, LANES), jnp.bfloat16)] * n_yz
        + [jax.ShapeDtypeStruct((carried_rows, LANES), jnp.float32), face_x],
        in_specs=[HB] * 4,
        out_specs=[HB] * (n_yz + 2),
        scratch_shapes=[
            pltpu.VMEM((cell_rows, len_z), jnp.float32),
            pltpu.SMEM(shell_owner.shape, jnp.int32),
            pltpu.SMEM(block_sources.shape, jnp.int32),
            pltpu.SMEM(block_targets.shape, jnp.int32),
            pltpu.SMEM((n_yz * CAP + 1,), jnp.int32),
            pltpu.VMEM((plan_rows, LANES), jnp.float32),
            pltpu.VMEM((2 * BLK, LANES, SR * LANES), jnp.bfloat16),
            pltpu.VMEM((n_yz * CAP, rows, LANES), jnp.bfloat16),
            pltpu.SemaphoreType.DMA((5 + 3 * ncomp + n_yz,)),
        ],
        compiler_params=pltpu.CompilerParams(vmem_limit_bytes=VMEM_BYTES - 8 * MIB),
        name="pack_shell",
    )(shell_owner, block_sources, block_targets, grid)

    moved = []
    for step in range(n_yz):
        pairs = [(t, n_yz + partner(t, step, n_yz)) for t in range(n_yz)]
        pairs = pairs + [(b, a) for a, b in pairs]
        moved.append(lax.ppermute(packed[step], ("dom", "yz"), pairs))
    wrap = lax.ppermute(wrap, ("dom", "gx"), wrap_pairs(n_gx))

    staged = [
        jax.ShapeDtypeStruct(weights.shape, weights.dtype),
        jax.ShapeDtypeStruct((cell_rows, len_z), jnp.float32),
        jax.ShapeDtypeStruct((plan_rows, LANES), jnp.float32),
    ]
    staged_bytes = sum(x.size * x.dtype.itemsize for x in staged)
    weights, grid, plan = pl.pallas_call(
        stage_kernel,
        out_shape=staged,
        in_specs=[HB] * 2,
        out_specs=[VM] * 3,
        scratch_shapes=[pltpu.SemaphoreType.DMA((slots * depth + 2,))],
        compiler_params=pltpu.CompilerParams(vmem_limit_bytes=VMEM_BYTES - 13 * staged_bytes // 4),
        cost_estimate=pl.CostEstimate(flops=0, bytes_accessed=4 * interp_weights.size, transcendentals=0),
        name="stage_operands",
    )(weights, carried)

    filled, x_one, x_two, y_one, y_two = pl.pallas_call(
        functools.partial(fill_kernel, dims + (n_yz, slots, depth)),
        out_shape=[jax.ShapeDtypeStruct((cell_rows, len_z), jnp.float32), face_x, face_x, face_y, face_y],
        in_specs=[VM, VM, VM] + [VM] * n_yz,
        out_specs=[VM] * 5,
        scratch_shapes=[
            pltpu.VMEM((2 * BLK, slots * rows, LANES), jnp.float32),
            pltpu.SMEM((plan_rows, LANES), jnp.float32),
            pltpu.SemaphoreType.DMA,
        ],
        input_output_aliases={2: 0},
        compiler_params=pltpu.CompilerParams(vmem_limit_bytes=16 * MIB),
        name="fill_blocks",
    )(plan, weights, grid, *moved)

    once_x, once_y = cycle(n_gx), cycle(n_yz)
    from_x_one = lax.ppermute(x_one, ("dom", "gx"), once_x)
    from_x_two = lax.ppermute(x_two, ("dom", "gx"), [(b, a) for a, b in once_x])
    from_y_one = lax.ppermute(y_one, ("dom", "yz"), once_y)
    from_y_two = lax.ppermute(y_two, ("dom", "yz"), [(b, a) for a, b in once_y])

    whole = jax.ShapeDtypeStruct((ncomp, len_x, len_y, len_z), jnp.float32)
    rim_x = jax.ShapeDtypeStruct((ncomp, len_y, len_z), jnp.float32)
    rim_y = jax.ShapeDtypeStruct((ncomp, len_x, len_z), jnp.float32)
    part, *rims = pl.pallas_call(
        functools.partial(inner_kernel, dims),
        out_shape=[whole, rim_x, rim_x, rim_y, rim_y],
        in_specs=[VM],
        out_specs=[HB] + [VM] * 4,
        scratch_shapes=[
            pltpu.VMEM((ncomp, len_x, len_y, len_z), jnp.float32),
            pltpu.SemaphoreType.DMA((len_x,)),
        ],
        compiler_params=pltpu.CompilerParams(vmem_limit_bytes=8 * MIB),
        cost_estimate=pl.CostEstimate(
            flops=300 * cell_rows * len_z, bytes_accessed=8 * cell_rows * len_z, transcendentals=0
        ),
        name="inner_faces",
    )(filled)

    updated = pl.pallas_call(
        functools.partial(edge_kernel, dims),
        out_shape=whole,
        in_specs=[HB] + [VM] * 13,
        out_specs=HB,
        scratch_shapes=[
            pltpu.VMEM((ncomp, len_y, len_z), jnp.float32),
            pltpu.VMEM((ncomp, len_y, len_z), jnp.float32),
            pltpu.VMEM((ncomp, len_x - 2, len_z), jnp.float32),
            pltpu.VMEM((ncomp, len_x - 2, len_z), jnp.float32),
            pltpu.SemaphoreType.DMA((4,)),
        ],
        input_output_aliases={0: 0},
        compiler_params=pltpu.CompilerParams(vmem_limit_bytes=8 * MIB),
        name="edge_faces",
    )(part, *rims, x_one, x_two, y_one, y_two, from_x_one, from_x_two, from_y_one, from_y_two, wrap)
    return updated.reshape(1, ncomp, len_x, len_y, len_z)


def solution(mesh):
    placed = (
        P("dom", None, "gx", "yz", None),
        P("gx", None, None),
        P("gx", "yz", None, None),
        P("gx", "yz", None),
        P("gx", "yz", None, None, None, None),
    )
    return jax.shard_map(
        local,
        mesh=mesh,
        in_specs=placed,
        out_specs=P("dom", None, "gx", "yz", None),
        check_vma=False,
    )
```

```python
import functools

import jax
import jax.numpy as jnp
from jax import lax
from jax.experimental import pallas as pl
from jax.experimental.pallas import tpu as pltpu
from jax.sharding import PartitionSpec as P

BLK = 8
SR = 2
CAP = 2
LANES = 128
MIB = 2**20
VMEM_BYTES = 64 * MIB

HEAT_RATIO = 5.0 / 3.0
CORONA_RATIO = 0.04
HELIO_RATIO = 0.03

VM = pl.BlockSpec(memory_space=pltpu.VMEM)
HB = pl.BlockSpec(memory_space=pltpu.HBM)


def partner(index, step, count):
    if count & (count - 1) == 0:
        return index ^ step
    return (index + step) % count


def cycle(count):
    pairs = [(count + i, count + i + 1) for i in range(count - 1)] + [(2 * count - 1, count - 1)]
    return pairs + [(i + 1, i) for i in range(count - 1)] + [(0, count)]


def wrap_pairs(count, lines):
    def index(domain, column, line):
        return (domain * count + column) * lines + line

    pairs = []
    for t in range(lines):
        pairs.append((index(0, 0, t), index(0, count - 1, t)))
        pairs += [(index(0, g, t), index(1, g, t)) for g in range(1, count - 1)]
    pairs += [(index(1, g, t), index(1, g, t + 1)) for g in (0, count - 1) for t in range(0, lines - 1, 2)]
    return pairs + [(b, a) for a, b in pairs]


def pack_kernel(dims, owner_hbm, source_hbm, target_hbm, grid_hbm, *rest):
    ncomp, len_x, len_y, len_z, n_yz, shells, slots, depth = dims
    outs, carried, wrap = rest[:n_yz], rest[n_yz], rest[n_yz + 1]
    grid_ref, owner_ref, source_ref, target_ref, table, plan, spread, send, sems = rest[n_yz + 2 :]
    me = lax.axis_index("yz")
    plane = len_x * len_y
    cell_rows = ncomp * plane
    n_bx, n_by, half = len_x // BLK, len_y // BLK, BLK // 2
    flat = grid_ref.reshape(cell_rows, len_z)
    onto = carried.at[pl.ds(0, ncomp)]
    slabs = [pl.ds(bx * BLK * len_y, BLK * len_y) for bx in range(n_bx)]
    grid_copies = [
        pltpu.make_async_copy(grid_hbm.at[:, slab, :], grid_ref.at[:, slab, :], sems.at[bx]) for bx, slab in enumerate(slabs)
    ]
    onward = [
        pltpu.make_async_copy(grid_ref.at[:, slab, :], onto.at[:, slab, :], sems.at[n_bx + bx])
        for bx, slab in enumerate(slabs)
    ]
    end = jnp.where(lax.axis_index("gx") == 0, 0, plane - len_y)
    first_sem = 2 * n_bx + 1
    wrap_copy = pltpu.make_async_copy(
        grid_ref.at[:, pl.ds(pl.multiple_of(end, BLK), len_y), :], wrap, sems.at[2 * n_bx]
    )
    copies = [
        pltpu.make_async_copy(owner_hbm, owner_ref, sems.at[first_sem]),
        pltpu.make_async_copy(source_hbm, source_ref, sems.at[first_sem + 1]),
        pltpu.make_async_copy(target_hbm, target_ref, sems.at[first_sem + 2]),
    ]

    @pl.when(lax.axis_index("dom") == 1)
    def _():
        for copy in copies:
            copy.start()
        for copy in grid_copies:
            copy.start()
        for copy in copies:
            copy.wait()
        position = jnp.int32(0)
        for t in range(n_yz):
            if n_yz & (n_yz - 1) == 0:
                step = t ^ me
            else:
                step = lax.rem(me - t + n_yz, n_yz)
            rank = jnp.int32(0)
            for b in range(shells):
                table[jnp.minimum(position, n_yz * CAP)] = step * CAP + jnp.minimum(rank, CAP - 1)
                mine = jnp.where(owner_ref[0, t, b] == me, 1, 0)
                position = position + mine
                rank = rank + mine
        for j in range(slots):
            for k in range(depth):
                entry = source_ref[0, 0, j, k]
                spot = jnp.where(entry >= 0, table[jnp.clip(entry, 0, n_yz * CAP)], -1)
                plan[j * depth + k : j * depth + k + 1, :] = jnp.full((1, LANES), spot.astype(jnp.float32))
            plan[slots * depth + j : slots * depth + j + 1, :] = jnp.full(
                (1, LANES), target_ref[0, 0, j].astype(jnp.float32)
            )
        told = pltpu.make_async_copy(plan, carried.at[ncomp, pl.ds(0, plan.shape[0])], sems.at[first_sem + 3])
        told.start()
        for arriving, leaving in zip(grid_copies, onward):
            arriving.wait()
            leaving.start()
        told.wait()
        for copy in onward:
            copy.wait()

    @pl.when(lax.axis_index("dom") == 0)
    def _():
        copies[0].start()
        for copy in grid_copies:
            copy.start()
        z_from = len_z - SR * BLK
        row_z = lax.broadcasted_iota(jnp.int32, (LANES, SR * LANES), 0) + (len_z - LANES)
        column = lax.broadcasted_iota(jnp.int32, (LANES, SR * LANES), 1)
        hit = row_z == z_from + column // LANES * BLK + column % BLK
        place = jnp.where(hit, column % LANES // BLK, -1)
        for m in range(2 * BLK):
            spread[m * LANES : (m + 1) * LANES, :] = jnp.where(place == m, 1.0, 0.0).astype(jnp.bfloat16)
        send[...] = jnp.zeros_like(send)
        copies[0].wait()
        spots = []
        for b in range(shells):
            owner = owner_ref[0, me, b]
            rank = jnp.int32(0)
            for other in range(b):
                rank = rank + jnp.where(owner_ref[0, me, other] == owner, 1, 0)
            if n_yz & (n_yz - 1) == 0:
                step = owner ^ me
            else:
                step = lax.rem(owner - me + n_yz, n_yz)
            spots.append(jnp.clip(step * CAP + rank, 0, n_yz * CAP - 1))
        rows = half * ncomp
        lines = []
        for bx in range(n_bx):
            grid_copies[bx].wait()
            onward[bx].start()
            line = []
            for ap in range(2):
                for cy in range(BLK):
                    pieces = []
                    for by in range(n_by):
                        for a2 in range(half):
                            first = (bx * BLK + a2 * 2 + ap) * len_y + by * BLK + cy
                            pieces.append(flat[pl.ds(first, ncomp, stride=plane), :])
                    line.append(jnp.concatenate(pieces, axis=0).astype(jnp.bfloat16))
            lines.append(jnp.concatenate(line, axis=1))
        total = jnp.dot(jnp.concatenate(lines, axis=0), spread[...], preferred_element_type=jnp.float32)
        total = total.astype(jnp.bfloat16)
        for b in range(shells):
            column_block, br = b // SR, b % SR
            send[spots[b]] = total[
                column_block * rows : (column_block + 1) * rows, br * LANES : (br + 1) * LANES
            ]
        wrap_copy.start()
        sends = [
            pltpu.make_async_copy(send.at[pl.ds(step * CAP, CAP)], outs[step], sems.at[first_sem + 4 + step])
            for step in range(n_yz)
        ]
        for copy in sends:
            copy.start()
        for copy in [wrap_copy] + onward + sends:
            copy.wait()


def early(size):
    return (lax.axis_index("dom") == 0) & (lax.axis_index("gx") < size)


def early_kernel(carried, wrap_in, grid_ref, wrap_out, sem):
    @pl.when(early(1))
    def _():
        copy = pltpu.make_async_copy(carried.at[pl.ds(0, grid_ref.shape[0])], grid_ref, sem)
        copy.start()
        copy.wait()


def stage_kernel(weight_hbm, carried, grid_in, weight_ref, grid_ref, plan_ref, sems):
    blocks, ncomp, plan_rows = weight_ref.shape[0], grid_ref.shape[0], plan_ref.shape[0]
    grid_copy = pltpu.make_async_copy(carried.at[pl.ds(0, ncomp)], grid_ref, sems.at[blocks])
    copies = [pltpu.make_async_copy(weight_hbm.at[i], weight_ref.at[i], sems.at[i]) for i in range(blocks)]
    copies.append(pltpu.make_async_copy(carried.at[ncomp, pl.ds(0, plan_rows)], plan_ref, sems.at[blocks + 1]))
    copies.append(grid_copy)

    @pl.when(lax.axis_index("dom") == 1)
    def _():
        for copy in copies:
            copy.start()
        for copy in copies:
            copy.wait()

    @pl.when((lax.axis_index("dom") == 0) & jnp.logical_not(early(1)))
    def _():
        grid_copy.start()
        grid_copy.wait()


def fill_kernel(dims, plan_vmem, weight_ref, grid_ref, *rest):
    ncomp, len_x, len_y, len_z, n_yz, slots, depth = dims
    got = rest[:n_yz]
    filled, x_one, x_two, y_one, y_two, result, plan, sem = rest[n_yz:]
    half = BLK // 2
    rows = half * ncomp
    plane = len_x * len_y

    helio = lax.axis_index("dom") == 1

    @pl.when(helio)
    def _():
        copy = pltpu.make_async_copy(plan_vmem, plan, sem)
        copy.start()
        held = [
            got[step][slot].astype(jnp.float32)
            for step in range(n_yz)
            for slot in range(CAP)
        ]
        lines = []
        for j in range(slots):
            sources = []
            for k in range(depth):
                entry = j * depth + k
                spot = jnp.broadcast_to(plan_vmem[entry : entry + 1, :], (rows, LANES))
                block = jnp.zeros((rows, LANES), jnp.float32)
                for place, candidate in enumerate(held):
                    block = jnp.where(spot == float(place), candidate, block)
                sources += [block[a2 * ncomp : (a2 + 1) * ncomp, :] for a2 in range(half)]
            cells = jnp.concatenate(sources, axis=1).astype(jnp.bfloat16)
            dense = weight_ref[j * depth : (j + 1) * depth].reshape(depth * weight_ref.shape[1], weight_ref.shape[2])
            total = jnp.dot(cells, dense, preferred_element_type=jnp.float32)
            lines += [total[:, a2 * LANES : (a2 + 1) * LANES] for a2 in range(half)]
        lines = jnp.concatenate(lines, axis=0)
        top = lines.astype(jnp.bfloat16)
        rest = lines - top.astype(jnp.float32)
        middle = rest.astype(jnp.bfloat16)
        bottom = (rest - middle.astype(jnp.float32)).astype(jnp.bfloat16)
        lines = jnp.concatenate([top, middle, bottom], axis=0)
        count = slots * rows
        pitch = count + BLK
        from_lane = lax.broadcasted_iota(jnp.int32, (LANES, LANES), 0)
        to_lane = lax.broadcasted_iota(jnp.int32, (LANES, LANES), 1)
        same = from_lane % BLK == to_lane % BLK
        for m in range(2 * BLK):
            spread = jnp.where(same & (from_lane // BLK == m), 1.0, 0.0).astype(jnp.bfloat16)
            parts = jnp.dot(lines, spread, preferred_element_type=jnp.float32)
            result[m * pitch : m * pitch + count, :] = parts[:count] + parts[count : 2 * count] + parts[2 * count :]
        copy.wait()
        lane = lax.broadcasted_iota(jnp.int32, (BLK, LANES), 1)
        per_y, per_z = len_y // BLK, len_z // BLK
        for j in range(slots):
            target = plan[slots * depth + j, 0].astype(jnp.int32)

            @pl.when(target >= 0)
            def _():
                block_x = target // (per_y * per_z)
                block_y = target // per_z % per_y
                z_from = target % per_z * BLK
                inside = (lane >= z_from) & (lane < z_from + BLK)
                first = block_x * BLK * len_y + block_y * BLK
                for a in range(BLK):
                    spots = [
                        pl.ds(pl.multiple_of(first + c * plane + a * len_y, BLK), BLK) for c in range(ncomp)
                    ]
                    row = a % 2 * BLK * pitch + j * rows + a // 2 * ncomp
                    old = [filled[spot, :] for spot in spots]
                    new = [result[pl.ds(row + c, BLK, stride=pitch), :] for c in range(ncomp)]
                    for spot, before, after in zip(spots, old, new):
                        filled[spot, :] = jnp.where(inside, after, before)

    def faces(x_low, x_high, y_low, y_high):
        for c in range(ncomp):
            x_low[c * len_y : (c + 1) * len_y, :] = filled[c * plane : c * plane + len_y, :]
            x_high[c * len_y : (c + 1) * len_y, :] = filled[(c + 1) * plane - len_y : (c + 1) * plane, :]
            y_low[c * len_x : (c + 1) * len_x, :] = filled[pl.ds(c * plane, len_x, stride=len_y), :]
            y_high[c * len_x : (c + 1) * len_x, :] = filled[
                pl.ds(c * plane + len_y - 1, len_x, stride=len_y), :
            ]

    @pl.when(helio)
    def _():
        faces(x_two, x_one, y_two, y_one)

    @pl.when(jnp.logical_not(helio))
    def _():
        faces(x_one, x_two, y_one, y_two)


def primitives(cells):
    density, energy = cells[0], cells[7]
    momentum, magnetic = cells[1:4], cells[4:7]
    inverse = 1.0 / density
    velocity = [m * inverse for m in momentum]
    field_sq = magnetic[0] * magnetic[0] + magnetic[1] * magnetic[1] + magnetic[2] * magnetic[2]
    kinetic = momentum[0] * velocity[0] + momentum[1] * velocity[1] + momentum[2] * velocity[2]
    pressure = (HEAT_RATIO - 1.0) * (energy - 0.5 * kinetic - 0.5 * field_sq)
    total_pressure = pressure + 0.5 * field_sq
    dot = velocity[0] * magnetic[0] + velocity[1] * magnetic[1] + velocity[2] * magnetic[2]
    fast = jnp.sqrt((HEAT_RATIO * pressure + field_sq) * inverse)
    return velocity, total_pressure, energy + total_pressure, dot, fast


def flux_of(cells, prims, direction):
    velocity, total_pressure, enthalpy, dot, fast = prims
    momentum, magnetic = cells[1:4], cells[4:7]
    speed, field = velocity[direction], magnetic[direction]
    flux = [momentum[direction]]
    for other in range(3):
        term = momentum[other] * speed - magnetic[other] * field
        flux.append(term + total_pressure if other == direction else term)
    for other in range(3):
        if other == direction:
            flux.append(None)
        else:
            flux.append(speed * magnetic[other] - field * velocity[other])
    flux.append(enthalpy * speed - field * dot)
    return flux, jnp.abs(speed) + fast


def face_sum(low, high):
    fastest = jnp.maximum(low[2], high[2])
    out = []
    for u_low, u_high, f_low, f_high in zip(low[0], high[0], low[1], high[1]):
        face = fastest * (u_high - u_low)
        out.append(face if f_low is None else face - (f_low + f_high))
    return out


def inner_kernel(dims, filled, out, rim_x_low, rim_x_high, rim_y_low, rim_y_high, part, sems):
    ncomp, len_x, len_y, len_z = dims
    plane = len_x * len_y
    half_ratio = jnp.where(lax.axis_index("dom") == 0, 0.5 * CORONA_RATIO, 0.5 * HELIO_RATIO).astype(jnp.float32)
    shape = (len_y, LANES)
    row = lax.broadcasted_iota(jnp.int32, shape, 0)
    lane = lax.broadcasted_iota(jnp.int32, shape, 1)

    def load(x):
        return [filled[pl.ds(pl.multiple_of(c * plane + x * len_y, BLK), len_y), :] for c in range(ncomp)]

    def shift_up(values, axis, size):
        return [None if v is None else pltpu.roll(v, size - 1, axis) for v in values]

    def step(x, carry, last):
        cells, prims, flux_x, speed_x, low_x = carry
        if last:
            high_x = [jnp.zeros(shape, jnp.float32)] * ncomp
            next_carry = None
        else:
            next_cells = load(x + 1)
            next_prims = primitives(next_cells)
            next_flux, next_speed = flux_of(next_cells, next_prims, 0)
            high_x = face_sum((cells, flux_x, speed_x), (next_cells, next_flux, next_speed))
            next_carry = (next_cells, next_prims, next_flux, next_speed, high_x)
        total = [high - low for high, low in zip(high_x, low_x)]
        flux, speed = flux_of(cells, prims, 1)
        beside = (shift_up(cells, 0, len_y), shift_up(flux, 0, len_y), pltpu.roll(speed, len_y - 1, 0))
        for c, face in enumerate(face_sum((cells, flux, speed), beside)):
            face = jnp.where(row == len_y - 1, 0.0, face)
            total[c] = total[c] + (face - pltpu.roll(face, 1, 0))
        flux, speed = flux_of(cells, prims, 2)
        beside = (shift_up(cells, 1, LANES), shift_up(flux, 1, LANES), pltpu.roll(speed, LANES - 1, 1))
        for c, face in enumerate(face_sum((cells, flux, speed), beside)):
            own = jnp.zeros(shape, jnp.float32) if flux[c] is None else -2.0 * flux[c]
            face = jnp.where(lane == LANES - 1, own, face)
            below = jnp.where(lane == 0, own, pltpu.roll(face, 1, 1))
            total[c] = total[c] + (face - below)
        for c in range(ncomp):
            part[c, x] = cells[c] + half_ratio * total[c]
        return next_carry

    def line_copy(x):
        return pltpu.make_async_copy(part.at[:, x], out.at[:, x], sems.at[x])

    cells = load(0)
    prims = primitives(cells)
    flux, speed = flux_of(cells, prims, 0)
    flux[4] = None
    zero = [jnp.zeros(shape, jnp.float32)] * ncomp
    carry = (cells, prims, flux, speed, zero)

    def pack(carry):
        cells, prims, flux, speed, low = carry
        return cells, prims, [f for f in flux if f is not None], speed, low

    def unpack(carry):
        cells, prims, flux, speed, low = carry
        return cells, prims, flux[:4] + [None] + flux[4:], speed, low

    def line(x, carry):
        carry = pack(step(x, unpack(carry), False))

        @pl.when(x > 0)
        def _():
            line_copy(x).start()

        return carry

    carry = lax.fori_loop(0, len_x - 1, line, pack(carry), unroll=3)
    step(len_x - 1, unpack(carry), True)
    for c in range(ncomp):
        rim_x_low[c] = part[c, 0]
        rim_x_high[c] = part[c, len_x - 1]
        rim_y_low[c] = part[c, :, 0, :]
        rim_y_high[c] = part[c, :, len_y - 1, :]
    for x in range(1, len_x - 1):
        line_copy(x).wait()


def edge_kernel(dims, part, rim_x_low, rim_x_high, rim_y_low, rim_y_high, *rest):
    ncomp, len_x, len_y, len_z = dims
    x_one, x_two, y_one, y_two, from_x_one, from_x_two, from_y_one, from_y_two, wrap = rest[:9]
    out, row_x_low, row_x_high, row_y_low, row_y_high, sems = rest[9:]
    helio = lax.axis_index("dom") == 1
    half_ratio = jnp.where(helio, 0.5 * HELIO_RATIO, 0.5 * CORONA_RATIO).astype(jnp.float32)

    def state(cells, direction):
        flux, speed = flux_of(cells, primitives(cells), direction)
        return cells, flux, speed

    def faces(own_ref, other_ref, end, end_ref, direction, upper, size):
        own = [own_ref[c * size : (c + 1) * size, :] for c in range(ncomp)]
        other = [other_ref[c * size : (c + 1) * size, :] for c in range(ncomp)]
        at_end = own if end_ref is None else [end_ref[c * size : (c + 1) * size, :] for c in range(ncomp)]
        other = [jnp.where(end, u, v) for u, v in zip(at_end, other)]
        own, other = state(own, direction), state(other, direction)
        if upper:
            return [half_ratio * f for f in face_sum(own, other)]
        return [-half_ratio * f for f in face_sum(other, own)]

    def both(x_low, x_high, y_low, y_high, from_x_low, from_x_high, from_y_low, from_y_high, x_end):
        column, line = lax.axis_index("gx"), lax.axis_index("yz")
        low_end, high_end = line == 0, line == lax.axis_size("yz") - 1
        y_lows = faces(y_low, from_y_low, low_end, None, 1, False, len_x)
        y_highs = faces(y_high, from_y_high, high_end, None, 1, True, len_x)
        for c in range(ncomp):
            row_y_low[c] = (rim_y_low[c] + y_lows[c])[1 : len_x - 1]
            row_y_high[c] = (rim_y_high[c] + y_highs[c])[1 : len_x - 1]
        inner_x = pl.ds(1, len_x - 2)
        copies = [
            pltpu.make_async_copy(row_y_low, out.at[:, inner_x, 0], sems.at[0]),
            pltpu.make_async_copy(row_y_high, out.at[:, inner_x, len_y - 1], sems.at[1]),
        ]
        copies[0].start()
        copies[1].start()
        low_end, high_end = column == 0, column == lax.axis_size("gx") - 1
        x_lows = faces(x_low, from_x_low, low_end, x_end, 0, False, len_y)
        x_highs = faces(x_high, from_x_high, high_end, x_end, 0, True, len_y)
        for row, rim, changes, x, sem in (
            (row_x_low, rim_x_low, x_lows, 0, 2),
            (row_x_high, rim_x_high, x_highs, len_x - 1, 3),
        ):
            for c in range(ncomp):
                row[c] = rim[c] + changes[c]
                row[c, 0:1] = row[c, 0:1] + y_lows[c][x : x + 1]
                row[c, len_y - 1 : len_y] = row[c, len_y - 1 : len_y] + y_highs[c][x : x + 1]
            copies.append(pltpu.make_async_copy(row, out.at[:, x], sems.at[sem]))
            copies[-1].start()
        for copy in copies:
            copy.wait()

    @pl.when(helio)
    def _():
        both(x_two, x_one, y_two, y_one, from_x_one, from_x_two, from_y_one, from_y_two, None)

    @pl.when(jnp.logical_not(helio))
    def _():
        both(x_one, x_two, y_one, y_two, from_x_two, from_x_one, from_y_two, from_y_one, wrap)


def local(field_state, shell_owner, block_sources, block_targets, interp_weights):
    _, ncomp, len_x, len_y, len_z = field_state.shape
    n_gx, n_yz = lax.axis_size("gx"), lax.axis_size("yz")
    shells = shell_owner.shape[2]
    slots, depth = block_sources.shape[2:]
    volume = BLK * BLK * BLK
    cell_rows = ncomp * len_x * len_y
    grid = field_state.reshape(ncomp, len_x * len_y, len_z)
    weights = interp_weights.reshape(slots * depth, volume, volume)
    rows = BLK // 2 * ncomp
    dims = (ncomp, len_x, len_y, len_z)

    plan_rows = -(-slots * (depth + 1) // BLK) * BLK
    face_x = jax.ShapeDtypeStruct((ncomp * len_y, len_z), jnp.float32)
    face_y = jax.ShapeDtypeStruct((ncomp * len_x, len_z), jnp.float32)
    plane = len_x * len_y
    carried_planes = max(ncomp + 1, 8 * MIB // (4 * LANES * plane))
    *packed, carried, wrap = pl.pallas_call(
        functools.partial(pack_kernel, dims + (n_yz, shells, slots, depth)),
        out_shape=[jax.ShapeDtypeStruct((CAP, rows, LANES), jnp.bfloat16)] * n_yz
        + [
            jax.ShapeDtypeStruct((carried_planes, plane, len_z), jnp.float32),
            jax.ShapeDtypeStruct((ncomp, len_y, len_z), jnp.float32),
        ],
        in_specs=[HB] * 4,
        out_specs=[HB] * (n_yz + 2),
        scratch_shapes=[
            pltpu.VMEM((ncomp, len_x * len_y, len_z), jnp.float32),
            pltpu.SMEM(shell_owner.shape, jnp.int32),
            pltpu.SMEM(block_sources.shape, jnp.int32),
            pltpu.SMEM(block_targets.shape, jnp.int32),
            pltpu.SMEM((n_yz * CAP + 1,), jnp.int32),
            pltpu.VMEM((plan_rows, LANES), jnp.float32),
            pltpu.VMEM((2 * BLK * LANES, SR * LANES), jnp.bfloat16),
            pltpu.VMEM((n_yz * CAP, rows, LANES), jnp.bfloat16),
            pltpu.SemaphoreType.DMA((2 * (len_x // BLK) + 5 + n_yz,)),
        ],
        compiler_params=pltpu.CompilerParams(vmem_limit_bytes=VMEM_BYTES - 8 * MIB),
        name="pack_shell",
    )(shell_owner, block_sources, block_targets, grid)

    moved = []
    for step in range(n_yz):
        pairs = [(t, n_yz + partner(t, step, n_yz)) for t in range(n_yz)]
        pairs = pairs + [(b, a) for a, b in pairs]
        moved.append(lax.ppermute(packed[step], ("dom", "yz"), pairs))

    staged = [
        jax.ShapeDtypeStruct(weights.shape, weights.dtype),
        jax.ShapeDtypeStruct((ncomp, plane, len_z), jnp.float32),
        jax.ShapeDtypeStruct((plan_rows, LANES), jnp.float32),
    ]
    staged_bytes = sum(x.size * x.dtype.itemsize for x in staged)
    room = pltpu.CompilerParams(vmem_limit_bytes=VMEM_BYTES - 13 * staged_bytes // 4)
    grid, wrap = pl.pallas_call(
        early_kernel,
        out_shape=[staged[1], jax.ShapeDtypeStruct(wrap.shape, wrap.dtype)],
        in_specs=[HB] * 2,
        out_specs=[VM, HB],
        scratch_shapes=[pltpu.SemaphoreType.DMA],
        input_output_aliases={1: 1},
        compiler_params=room,
        name="early_grid",
    )(carried, wrap)
    wrap = lax.ppermute(wrap, ("dom", "gx", "yz"), wrap_pairs(n_gx, n_yz))
    weights, grid, plan = pl.pallas_call(
        stage_kernel,
        out_shape=staged,
        in_specs=[HB, HB, VM],
        out_specs=[VM] * 3,
        scratch_shapes=[pltpu.SemaphoreType.DMA((slots * depth + 2,))],
        input_output_aliases={2: 1},
        compiler_params=room,
        cost_estimate=pl.CostEstimate(flops=0, bytes_accessed=4 * interp_weights.size, transcendentals=0),
        name="stage_operands",
    )(weights, carried, grid)

    filled, x_one, x_two, y_one, y_two = pl.pallas_call(
        functools.partial(fill_kernel, dims + (n_yz, slots, depth)),
        out_shape=[jax.ShapeDtypeStruct((cell_rows, len_z), jnp.float32), face_x, face_x, face_y, face_y],
        in_specs=[VM, VM, VM] + [VM] * n_yz,
        out_specs=[VM] * 5,
        scratch_shapes=[
            pltpu.VMEM((2 * BLK * (slots * rows + BLK), LANES), jnp.float32),
            pltpu.SMEM((plan_rows, LANES), jnp.float32),
            pltpu.SemaphoreType.DMA,
        ],
        input_output_aliases={2: 0},
        compiler_params=pltpu.CompilerParams(vmem_limit_bytes=16 * MIB),
        name="fill_blocks",
    )(plan, weights, grid.reshape(cell_rows, len_z), *moved)

    once_x, once_y = cycle(n_gx), cycle(n_yz)
    from_x_one = lax.ppermute(x_one, ("dom", "gx"), once_x)
    from_x_two = lax.ppermute(x_two, ("dom", "gx"), [(b, a) for a, b in once_x])
    from_y_one = lax.ppermute(y_one, ("dom", "yz"), once_y)
    from_y_two = lax.ppermute(y_two, ("dom", "yz"), [(b, a) for a, b in once_y])

    whole = jax.ShapeDtypeStruct((ncomp, len_x, len_y, len_z), jnp.float32)
    rim_x = jax.ShapeDtypeStruct((ncomp, len_y, len_z), jnp.float32)
    rim_y = jax.ShapeDtypeStruct((ncomp, len_x, len_z), jnp.float32)
    part, *rims = pl.pallas_call(
        functools.partial(inner_kernel, dims),
        out_shape=[whole, rim_x, rim_x, rim_y, rim_y],
        in_specs=[VM],
        out_specs=[HB] + [VM] * 4,
        scratch_shapes=[
            pltpu.VMEM((ncomp, len_x, len_y, len_z), jnp.float32),
            pltpu.SemaphoreType.DMA((len_x,)),
        ],
        compiler_params=pltpu.CompilerParams(vmem_limit_bytes=8 * MIB),
        cost_estimate=pl.CostEstimate(
            flops=300 * cell_rows * len_z, bytes_accessed=8 * cell_rows * len_z, transcendentals=0
        ),
        name="inner_faces",
    )(filled)

    updated = pl.pallas_call(
        functools.partial(edge_kernel, dims),
        out_shape=whole,
        in_specs=[HB] + [VM] * 13,
        out_specs=HB,
        scratch_shapes=[
            pltpu.VMEM((ncomp, len_y, len_z), jnp.float32),
            pltpu.VMEM((ncomp, len_y, len_z), jnp.float32),
            pltpu.VMEM((ncomp, len_x - 2, len_z), jnp.float32),
            pltpu.VMEM((ncomp, len_x - 2, len_z), jnp.float32),
            pltpu.SemaphoreType.DMA((4,)),
        ],
        input_output_aliases={0: 0},
        compiler_params=pltpu.CompilerParams(vmem_limit_bytes=8 * MIB),
        name="edge_faces",
    )(part, *rims, x_one, x_two, y_one, y_two, from_x_one, from_x_two, from_y_one, from_y_two, wrap.reshape(ncomp * len_y, len_z))
    return updated.reshape(1, ncomp, len_x, len_y, len_z)


def solution(mesh):
    placed = (
        P("dom", None, "gx", "yz", None),
        P("gx", None, None),
        P("gx", "yz", None, None),
        P("gx", "yz", None),
        P("gx", "yz", None, None, None, None),
    )
    return jax.shard_map(
        local,
        mesh=mesh,
        in_specs=placed,
        out_specs=P("dom", None, "gx", "yz", None),
        check_vma=False,
    )
```

```python
import functools

import jax
import jax.numpy as jnp
from jax import lax
from jax.experimental import pallas as pl
from jax.experimental.pallas import tpu as pltpu
from jax.sharding import PartitionSpec as P

BLK = 8
SR = 2
CAP = 2
LANES = 128
MIB = 2**20
VMEM_BYTES = 64 * MIB

HEAT_RATIO = 5.0 / 3.0
CORONA_RATIO = 0.04
HELIO_RATIO = 0.03

VM = pl.BlockSpec(memory_space=pltpu.VMEM)
HB = pl.BlockSpec(memory_space=pltpu.HBM)


def partner(index, step, count):
    if count & (count - 1) == 0:
        return index ^ step
    return (index + step) % count


def cycle(count):
    pairs = [(count + i, count + i + 1) for i in range(count - 1)] + [(2 * count - 1, count - 1)]
    return pairs + [(i + 1, i) for i in range(count - 1)] + [(0, count)]


def wrap_pairs(count, lines):
    def index(domain, column, line):
        return (domain * count + column) * lines + line

    pairs = []
    for t in range(lines):
        pairs.append((index(0, 0, t), index(0, count - 1, t)))
        pairs += [(index(0, g, t), index(1, g, t)) for g in range(1, count - 1)]
    pairs += [(index(1, g, t), index(1, g, t + 1)) for g in (0, count - 1) for t in range(0, lines - 1, 2)]
    return pairs + [(b, a) for a, b in pairs]


def pack_kernel(dims, owner_hbm, source_hbm, target_hbm, grid_hbm, *rest):
    ncomp, len_x, len_y, len_z, n_yz, shells, slots, depth = dims
    outs, carried, wrap = rest[:n_yz], rest[n_yz], rest[n_yz + 1]
    grid_ref, owner_ref, source_ref, target_ref, table, plan, spread, send, sems = rest[n_yz + 2 :]
    me = lax.axis_index("yz")
    plane = len_x * len_y
    n_bx, n_by, half = len_x // BLK, len_y // BLK, BLK // 2
    pitch = grid_ref.shape[1]
    flat = grid_ref.reshape(ncomp * pitch, len_z)
    onto = carried.at[pl.ds(0, ncomp)]
    slabs = [pl.ds(bx * BLK * len_y, BLK * len_y) for bx in range(n_bx)]
    grid_copies = [
        pltpu.make_async_copy(grid_hbm.at[:, slab, :], grid_ref.at[:, slab, :], sems.at[bx]) for bx, slab in enumerate(slabs)
    ]
    onward = [
        pltpu.make_async_copy(grid_ref.at[:, slab, :], onto.at[:, slab, :], sems.at[n_bx + bx])
        for bx, slab in enumerate(slabs)
    ]
    end = jnp.where(lax.axis_index("gx") == 0, 0, plane - len_y)
    first_sem = 2 * n_bx + 1
    wrap_copy = pltpu.make_async_copy(
        grid_ref.at[:, pl.ds(pl.multiple_of(end, BLK), len_y), :], wrap, sems.at[2 * n_bx]
    )
    copies = [
        pltpu.make_async_copy(owner_hbm, owner_ref, sems.at[first_sem]),
        pltpu.make_async_copy(source_hbm, source_ref, sems.at[first_sem + 1]),
        pltpu.make_async_copy(target_hbm, target_ref, sems.at[first_sem + 2]),
    ]

    @pl.when(lax.axis_index("dom") == 1)
    def _():
        for copy in copies:
            copy.start()
        for copy in grid_copies:
            copy.start()
        for copy in copies:
            copy.wait()
        position = jnp.int32(0)
        for t in range(n_yz):
            if n_yz & (n_yz - 1) == 0:
                step = t ^ me
            else:
                step = lax.rem(me - t + n_yz, n_yz)
            rank = jnp.int32(0)
            for b in range(shells):
                table[jnp.minimum(position, n_yz * CAP)] = step * CAP + jnp.minimum(rank, CAP - 1)
                mine = jnp.where(owner_ref[0, t, b] == me, 1, 0)
                position = position + mine
                rank = rank + mine
        for j in range(slots):
            for k in range(depth):
                entry = source_ref[0, 0, j, k]
                spot = jnp.where(entry >= 0, table[jnp.clip(entry, 0, n_yz * CAP)], -1)
                plan[j * depth + k : j * depth + k + 1, :] = jnp.full((1, LANES), spot.astype(jnp.float32))
            plan[slots * depth + j : slots * depth + j + 1, :] = jnp.full(
                (1, LANES), target_ref[0, 0, j].astype(jnp.float32)
            )
        told = pltpu.make_async_copy(plan, carried.at[ncomp, pl.ds(0, plan.shape[0])], sems.at[first_sem + 3])
        told.start()
        for arriving, leaving in zip(grid_copies, onward):
            arriving.wait()
            leaving.start()
        told.wait()
        for copy in onward:
            copy.wait()

    @pl.when(lax.axis_index("dom") == 0)
    def _():
        copies[0].start()
        for copy in grid_copies:
            copy.start()
        z_from = len_z - SR * BLK
        row_z = lax.broadcasted_iota(jnp.int32, (LANES, SR * LANES), 0) + (len_z - LANES)
        column = lax.broadcasted_iota(jnp.int32, (LANES, SR * LANES), 1)
        hit = row_z == z_from + column // LANES * BLK + column % BLK
        place = jnp.where(hit, column % LANES // BLK, -1)
        for m in range(2 * BLK):
            spread[m * LANES : (m + 1) * LANES, :] = jnp.where(place == m, 1.0, 0.0).astype(jnp.bfloat16)
        send[...] = jnp.zeros_like(send)
        copies[0].wait()
        spots = []
        for b in range(shells):
            owner = owner_ref[0, me, b]
            rank = jnp.int32(0)
            for other in range(b):
                rank = rank + jnp.where(owner_ref[0, me, other] == owner, 1, 0)
            if n_yz & (n_yz - 1) == 0:
                step = owner ^ me
            else:
                step = lax.rem(owner - me + n_yz, n_yz)
            spots.append(jnp.clip(step * CAP + rank, 0, n_yz * CAP - 1))
        rows = half * ncomp
        lines = []
        for bx in range(n_bx):
            grid_copies[bx].wait()
            onward[bx].start()
            line = []
            for ap in range(2):
                for cy in range(BLK):
                    pieces = []
                    for by in range(n_by):
                        for a2 in range(half):
                            first = (bx * BLK + a2 * 2 + ap) * len_y + by * BLK + cy
                            pieces.append(flat[pl.ds(first, ncomp, stride=pitch), :])
                    line.append(jnp.concatenate(pieces, axis=0).astype(jnp.bfloat16))
            lines.append(jnp.concatenate(line, axis=1))
        total = jnp.dot(jnp.concatenate(lines, axis=0), spread[...], preferred_element_type=jnp.float32)
        total = total.astype(jnp.bfloat16)
        for b in range(shells):
            column_block, br = b // SR, b % SR
            send[spots[b]] = total[
                column_block * rows : (column_block + 1) * rows, br * LANES : (br + 1) * LANES
            ]
        wrap_copy.start()
        sends = [
            pltpu.make_async_copy(send.at[pl.ds(step * CAP, CAP)], outs[step], sems.at[first_sem + 4 + step])
            for step in range(n_yz)
        ]
        for copy in sends:
            copy.start()
        for copy in [wrap_copy] + onward + sends:
            copy.wait()


def early(size):
    return (lax.axis_index("dom") == 0) & (lax.axis_index("gx") < size)


def early_kernel(carried, wrap_in, grid_ref, wrap_out, sem):
    @pl.when(early(1))
    def _():
        copy = pltpu.make_async_copy(carried.at[pl.ds(0, grid_ref.shape[0])], grid_ref, sem)
        copy.start()
        copy.wait()


def stage_kernel(weight_hbm, carried, grid_in, weight_ref, grid_ref, plan_ref, sems):
    blocks, ncomp, plan_rows = weight_ref.shape[0], grid_ref.shape[0], plan_ref.shape[0]
    grid_copy = pltpu.make_async_copy(carried.at[pl.ds(0, ncomp)], grid_ref, sems.at[blocks])
    copies = [pltpu.make_async_copy(weight_hbm.at[i], weight_ref.at[i], sems.at[i]) for i in range(blocks)]
    copies.append(pltpu.make_async_copy(carried.at[ncomp, pl.ds(0, plan_rows)], plan_ref, sems.at[blocks + 1]))
    copies.append(grid_copy)

    @pl.when(lax.axis_index("dom") == 1)
    def _():
        for copy in copies:
            copy.start()
        for copy in copies:
            copy.wait()

    @pl.when((lax.axis_index("dom") == 0) & jnp.logical_not(early(1)))
    def _():
        grid_copy.start()
        grid_copy.wait()


def fill_kernel(dims, plan_vmem, weight_ref, grid_ref, *rest):
    ncomp, len_x, len_y, len_z, n_yz, slots, depth = dims
    got = rest[:n_yz]
    filled, y_one, y_two, x_one, x_two, result, plan, sem = rest[n_yz:]
    half = BLK // 2
    rows = half * ncomp
    plane = len_x * len_y

    helio = lax.axis_index("dom") == 1

    @pl.when(helio)
    def _():
        copy = pltpu.make_async_copy(plan_vmem, plan, sem)
        copy.start()
        held = [
            got[step][slot].astype(jnp.float32)
            for step in range(n_yz)
            for slot in range(CAP)
        ]
        lines = []
        for j in range(slots):
            sources = []
            for k in range(depth):
                entry = j * depth + k
                spot = jnp.broadcast_to(plan_vmem[entry : entry + 1, :], (rows, LANES))
                block = jnp.zeros((rows, LANES), jnp.float32)
                for place, candidate in enumerate(held):
                    block = jnp.where(spot == float(place), candidate, block)
                sources += [block[a2 * ncomp : (a2 + 1) * ncomp, :] for a2 in range(half)]
            cells = jnp.concatenate(sources, axis=1).astype(jnp.bfloat16)
            dense = weight_ref[j * depth : (j + 1) * depth].reshape(depth * weight_ref.shape[1], weight_ref.shape[2])
            total = jnp.dot(cells, dense, preferred_element_type=jnp.float32)
            lines += [total[:, a2 * LANES : (a2 + 1) * LANES] for a2 in range(half)]
        lines = jnp.concatenate(lines, axis=0)
        top = lines.astype(jnp.bfloat16)
        rest = lines - top.astype(jnp.float32)
        middle = rest.astype(jnp.bfloat16)
        bottom = (rest - middle.astype(jnp.float32)).astype(jnp.bfloat16)
        lines = jnp.concatenate([top, middle, bottom], axis=0)
        count = slots * rows
        pitch = count + BLK
        from_lane = lax.broadcasted_iota(jnp.int32, (LANES, LANES), 0)
        to_lane = lax.broadcasted_iota(jnp.int32, (LANES, LANES), 1)
        same = from_lane % BLK == to_lane % BLK
        for m in range(2 * BLK):
            spread = jnp.where(same & (from_lane // BLK == m), 1.0, 0.0).astype(jnp.bfloat16)
            parts = jnp.dot(lines, spread, preferred_element_type=jnp.float32)
            result[m * pitch : m * pitch + count, :] = parts[:count] + parts[count : 2 * count] + parts[2 * count :]
        copy.wait()
        lane = lax.broadcasted_iota(jnp.int32, (BLK, LANES), 1)
        per_y, per_z = len_y // BLK, len_z // BLK
        for j in range(slots):
            target = plan[slots * depth + j, 0].astype(jnp.int32)

            @pl.when(target >= 0)
            def _():
                block_x = target // (per_y * per_z)
                block_y = target // per_z % per_y
                z_from = target % per_z * BLK
                inside = (lane >= z_from) & (lane < z_from + BLK)
                first = block_x * BLK * len_y + block_y * BLK
                for a in range(BLK):
                    spots = [
                        pl.ds(pl.multiple_of(first + c * plane + a * len_y, BLK), BLK) for c in range(ncomp)
                    ]
                    row = a % 2 * BLK * pitch + j * rows + a // 2 * ncomp
                    old = [filled[spot, :] for spot in spots]
                    new = [result[pl.ds(row + c, BLK, stride=pitch), :] for c in range(ncomp)]
                    for spot, before, after in zip(spots, old, new):
                        filled[spot, :] = jnp.where(inside, after, before)

    def faces(x_low, x_high, y_low, y_high):
        for c in range(ncomp):
            x_low[c * len_y : (c + 1) * len_y, :] = filled[c * plane : c * plane + len_y, :]
            x_high[c * len_y : (c + 1) * len_y, :] = filled[(c + 1) * plane - len_y : (c + 1) * plane, :]
            y_low[c * len_x : (c + 1) * len_x, :] = filled[pl.ds(c * plane, len_x, stride=len_y), :]
            y_high[c * len_x : (c + 1) * len_x, :] = filled[
                pl.ds(c * plane + len_y - 1, len_x, stride=len_y), :
            ]

    @pl.when(helio)
    def _():
        faces(x_two, x_one, y_two, y_one)

    @pl.when(jnp.logical_not(helio))
    def _():
        faces(x_one, x_two, y_one, y_two)


def primitives(cells):
    density, energy = cells[0], cells[7]
    momentum, magnetic = cells[1:4], cells[4:7]
    inverse = 1.0 / density
    velocity = [m * inverse for m in momentum]
    field_sq = magnetic[0] * magnetic[0] + magnetic[1] * magnetic[1] + magnetic[2] * magnetic[2]
    kinetic = momentum[0] * velocity[0] + momentum[1] * velocity[1] + momentum[2] * velocity[2]
    pressure = (HEAT_RATIO - 1.0) * (energy - 0.5 * kinetic - 0.5 * field_sq)
    total_pressure = pressure + 0.5 * field_sq
    dot = velocity[0] * magnetic[0] + velocity[1] * magnetic[1] + velocity[2] * magnetic[2]
    fast = jnp.sqrt((HEAT_RATIO * pressure + field_sq) * inverse)
    return velocity, total_pressure, energy + total_pressure, dot, fast


def flux_of(cells, prims, direction):
    velocity, total_pressure, enthalpy, dot, fast = prims
    momentum, magnetic = cells[1:4], cells[4:7]
    speed, field = velocity[direction], magnetic[direction]
    flux = [momentum[direction]]
    for other in range(3):
        term = momentum[other] * speed - magnetic[other] * field
        flux.append(term + total_pressure if other == direction else term)
    for other in range(3):
        if other == direction:
            flux.append(None)
        else:
            flux.append(speed * magnetic[other] - field * velocity[other])
    flux.append(enthalpy * speed - field * dot)
    return flux, jnp.abs(speed) + fast


def face_sum(low, high):
    fastest = jnp.maximum(low[2], high[2])
    out = []
    for u_low, u_high, f_low, f_high in zip(low[0], high[0], low[1], high[1]):
        face = fastest * (u_high - u_low)
        out.append(face if f_low is None else face - (f_low + f_high))
    return out


def inner_kernel(dims, filled, out, rim_x_low, rim_x_high, rim_y_low, rim_y_high, part, sems):
    ncomp, len_x, len_y, len_z = dims
    plane = len_x * len_y
    half_ratio = jnp.where(lax.axis_index("dom") == 0, 0.5 * CORONA_RATIO, 0.5 * HELIO_RATIO).astype(jnp.float32)
    shape = (len_y, LANES)
    row = lax.broadcasted_iota(jnp.int32, shape, 0)
    lane = lax.broadcasted_iota(jnp.int32, shape, 1)

    def load(x):
        return [filled[pl.ds(pl.multiple_of(c * plane + x * len_y, BLK), len_y), :] for c in range(ncomp)]

    def shift_up(values, axis, size):
        return [None if v is None else pltpu.roll(v, size - 1, axis) for v in values]

    def step(x, carry, last):
        cells, prims, flux_x, speed_x, low_x = carry
        if last:
            high_x = [jnp.zeros(shape, jnp.float32)] * ncomp
            next_carry = None
        else:
            next_cells = load(x + 1)
            next_prims = primitives(next_cells)
            next_flux, next_speed = flux_of(next_cells, next_prims, 0)
            high_x = face_sum((cells, flux_x, speed_x), (next_cells, next_flux, next_speed))
            next_carry = (next_cells, next_prims, next_flux, next_speed, high_x)
        total = [high - low for high, low in zip(high_x, low_x)]
        flux, speed = flux_of(cells, prims, 1)
        beside = (shift_up(cells, 0, len_y), shift_up(flux, 0, len_y), pltpu.roll(speed, len_y - 1, 0))
        for c, face in enumerate(face_sum((cells, flux, speed), beside)):
            face = jnp.where(row == len_y - 1, 0.0, face)
            total[c] = total[c] + (face - pltpu.roll(face, 1, 0))
        flux, speed = flux_of(cells, prims, 2)
        beside = (shift_up(cells, 1, LANES), shift_up(flux, 1, LANES), pltpu.roll(speed, LANES - 1, 1))
        for c, face in enumerate(face_sum((cells, flux, speed), beside)):
            own = jnp.zeros(shape, jnp.float32) if flux[c] is None else -2.0 * flux[c]
            face = jnp.where(lane == LANES - 1, own, face)
            below = jnp.where(lane == 0, own, pltpu.roll(face, 1, 1))
            total[c] = total[c] + (face - below)
        for c in range(ncomp):
            part[c, x] = cells[c] + half_ratio * total[c]
        return next_carry

    def line_copy(x):
        return pltpu.make_async_copy(part.at[:, x], out.at[:, x], sems.at[x])

    cells = load(0)
    prims = primitives(cells)
    flux, speed = flux_of(cells, prims, 0)
    flux[4] = None
    zero = [jnp.zeros(shape, jnp.float32)] * ncomp
    carry = (cells, prims, flux, speed, zero)

    def pack(carry):
        cells, prims, flux, speed, low = carry
        return cells, prims, [f for f in flux if f is not None], speed, low

    def unpack(carry):
        cells, prims, flux, speed, low = carry
        return cells, prims, flux[:4] + [None] + flux[4:], speed, low

    def line(x, carry):
        carry = pack(step(x, unpack(carry), False))

        @pl.when(x > 0)
        def _():
            line_copy(x).start()

        return carry

    carry = lax.fori_loop(0, len_x - 1, line, pack(carry), unroll=3)
    step(len_x - 1, unpack(carry), True)
    for c in range(ncomp):
        rim_x_low[c] = part[c, 0]
        rim_x_high[c] = part[c, len_x - 1]
        rim_y_low[c] = part[c, :, 0, :]
        rim_y_high[c] = part[c, :, len_y - 1, :]
    for x in range(1, len_x - 1):
        line_copy(x).wait()


def edge_kernel(dims, part, rim_x_low, rim_x_high, rim_y_low, rim_y_high, *rest):
    ncomp, len_x, len_y, len_z = dims
    y_one, y_two, x_one, x_two, from_y_one, from_y_two, from_x_one, from_x_two, wrap = rest[:9]
    out, row_x_low, row_x_high, row_y_low, row_y_high, sems = rest[9:]
    helio = lax.axis_index("dom") == 1
    half_ratio = jnp.where(helio, 0.5 * HELIO_RATIO, 0.5 * CORONA_RATIO).astype(jnp.float32)

    def state(cells, direction):
        flux, speed = flux_of(cells, primitives(cells), direction)
        return cells, flux, speed

    def faces(own_ref, other_ref, end, end_ref, direction, upper, size):
        own = [own_ref[c * size : (c + 1) * size, :] for c in range(ncomp)]
        other = [other_ref[c * size : (c + 1) * size, :] for c in range(ncomp)]
        at_end = own if end_ref is None else [end_ref[c * size : (c + 1) * size, :] for c in range(ncomp)]
        other = [jnp.where(end, u, v) for u, v in zip(at_end, other)]
        own, other = state(own, direction), state(other, direction)
        if upper:
            return [half_ratio * f for f in face_sum(own, other)]
        return [-half_ratio * f for f in face_sum(other, own)]

    def both(x_low, x_high, y_low, y_high, from_x_low, from_x_high, from_y_low, from_y_high, x_end):
        column, line = lax.axis_index("gx"), lax.axis_index("yz")
        low_end, high_end = line == 0, line == lax.axis_size("yz") - 1
        y_lows = faces(y_low, from_y_low, low_end, None, 1, False, len_x)
        y_highs = faces(y_high, from_y_high, high_end, None, 1, True, len_x)
        for c in range(ncomp):
            row_y_low[c] = (rim_y_low[c] + y_lows[c])[1 : len_x - 1]
            row_y_high[c] = (rim_y_high[c] + y_highs[c])[1 : len_x - 1]
        inner_x = pl.ds(1, len_x - 2)
        copies = [
            pltpu.make_async_copy(row_y_low, out.at[:, inner_x, 0], sems.at[0]),
            pltpu.make_async_copy(row_y_high, out.at[:, inner_x, len_y - 1], sems.at[1]),
        ]
        copies[0].start()
        copies[1].start()
        low_end, high_end = column == 0, column == lax.axis_size("gx") - 1
        x_lows = faces(x_low, from_x_low, low_end, x_end, 0, False, len_y)
        x_highs = faces(x_high, from_x_high, high_end, x_end, 0, True, len_y)
        for row, rim, changes, x, sem in (
            (row_x_low, rim_x_low, x_lows, 0, 2),
            (row_x_high, rim_x_high, x_highs, len_x - 1, 3),
        ):
            for c in range(ncomp):
                row[c] = rim[c] + changes[c]
                row[c, 0:1] = row[c, 0:1] + y_lows[c][x : x + 1]
                row[c, len_y - 1 : len_y] = row[c, len_y - 1 : len_y] + y_highs[c][x : x + 1]
            copies.append(pltpu.make_async_copy(row, out.at[:, x], sems.at[sem]))
            copies[-1].start()
        for copy in copies:
            copy.wait()

    @pl.when(helio)
    def _():
        both(x_two, x_one, y_two, y_one, from_x_one, from_x_two, from_y_one, from_y_two, None)

    @pl.when(jnp.logical_not(helio))
    def _():
        both(x_one, x_two, y_one, y_two, from_x_two, from_x_one, from_y_two, from_y_one, wrap)


def local(field_state, shell_owner, block_sources, block_targets, interp_weights):
    _, ncomp, len_x, len_y, len_z = field_state.shape
    n_gx, n_yz = lax.axis_size("gx"), lax.axis_size("yz")
    shells = shell_owner.shape[2]
    slots, depth = block_sources.shape[2:]
    volume = BLK * BLK * BLK
    cell_rows = ncomp * len_x * len_y
    grid = field_state.reshape(ncomp, len_x * len_y, len_z)
    weights = interp_weights.reshape(slots * depth, volume, volume)
    rows = BLK // 2 * ncomp
    dims = (ncomp, len_x, len_y, len_z)

    plan_rows = -(-slots * (depth + 1) // BLK) * BLK
    face_x = jax.ShapeDtypeStruct((ncomp * len_y, len_z), jnp.float32)
    face_y = jax.ShapeDtypeStruct((ncomp * len_x, len_z), jnp.float32)
    plane = len_x * len_y
    carried_planes = max(ncomp + 1, 8 * MIB // (4 * LANES * plane))
    *packed, carried, wrap = pl.pallas_call(
        functools.partial(pack_kernel, dims + (n_yz, shells, slots, depth)),
        out_shape=[jax.ShapeDtypeStruct((CAP, rows, LANES), jnp.bfloat16)] * n_yz
        + [
            jax.ShapeDtypeStruct((carried_planes, plane, len_z), jnp.float32),
            jax.ShapeDtypeStruct((ncomp, len_y, len_z), jnp.float32),
        ],
        in_specs=[HB] * 4,
        out_specs=[HB] * (n_yz + 2),
        scratch_shapes=[
            pltpu.VMEM((ncomp, plane + BLK, len_z), jnp.float32),
            pltpu.SMEM(shell_owner.shape, jnp.int32),
            pltpu.SMEM(block_sources.shape, jnp.int32),
            pltpu.SMEM(block_targets.shape, jnp.int32),
            pltpu.SMEM((n_yz * CAP + 1,), jnp.int32),
            pltpu.VMEM((plan_rows, LANES), jnp.float32),
            pltpu.VMEM((2 * BLK * LANES, SR * LANES), jnp.bfloat16),
            pltpu.VMEM((n_yz * CAP, rows, LANES), jnp.bfloat16),
            pltpu.SemaphoreType.DMA((2 * (len_x // BLK) + 5 + n_yz,)),
        ],
        compiler_params=pltpu.CompilerParams(vmem_limit_bytes=VMEM_BYTES - 8 * MIB),
        name="pack_shell",
    )(shell_owner, block_sources, block_targets, grid)

    moved = []
    for step in range(n_yz):
        pairs = [(t, n_yz + partner(t, step, n_yz)) for t in range(n_yz)]
        pairs = pairs + [(b, a) for a, b in pairs]
        moved.append(lax.ppermute(packed[step], ("dom", "yz"), pairs))

    staged = [
        jax.ShapeDtypeStruct(weights.shape, weights.dtype),
        jax.ShapeDtypeStruct((ncomp, plane, len_z), jnp.float32),
        jax.ShapeDtypeStruct((plan_rows, LANES), jnp.float32),
    ]
    staged_bytes = sum(x.size * x.dtype.itemsize for x in staged)
    room = pltpu.CompilerParams(vmem_limit_bytes=VMEM_BYTES - 13 * staged_bytes // 4)
    grid, wrap = pl.pallas_call(
        early_kernel,
        out_shape=[staged[1], jax.ShapeDtypeStruct(wrap.shape, wrap.dtype)],
        in_specs=[HB] * 2,
        out_specs=[VM, HB],
        scratch_shapes=[pltpu.SemaphoreType.DMA],
        input_output_aliases={1: 1},
        compiler_params=room,
        name="early_grid",
    )(carried, wrap)
    wrap = lax.ppermute(wrap, ("dom", "gx", "yz"), wrap_pairs(n_gx, n_yz))
    weights, grid, plan = pl.pallas_call(
        stage_kernel,
        out_shape=staged,
        in_specs=[HB, HB, VM],
        out_specs=[VM] * 3,
        scratch_shapes=[pltpu.SemaphoreType.DMA((slots * depth + 2,))],
        input_output_aliases={2: 1},
        compiler_params=room,
        cost_estimate=pl.CostEstimate(flops=0, bytes_accessed=4 * interp_weights.size, transcendentals=0),
        name="stage_operands",
    )(weights, carried, grid)

    filled, y_one, y_two, x_one, x_two = pl.pallas_call(
        functools.partial(fill_kernel, dims + (n_yz, slots, depth)),
        out_shape=[jax.ShapeDtypeStruct((cell_rows, len_z), jnp.float32), face_y, face_y, face_x, face_x],
        in_specs=[VM, VM, VM] + [VM] * n_yz,
        out_specs=[VM] * 5,
        scratch_shapes=[
            pltpu.VMEM((2 * BLK * (slots * rows + BLK), LANES), jnp.float32),
            pltpu.SMEM((plan_rows, LANES), jnp.float32),
            pltpu.SemaphoreType.DMA,
        ],
        input_output_aliases={2: 0},
        compiler_params=pltpu.CompilerParams(vmem_limit_bytes=16 * MIB),
        name="fill_blocks",
    )(plan, weights, grid.reshape(cell_rows, len_z), *moved)

    once_x, once_y = cycle(n_gx), cycle(n_yz)
    from_y_one = lax.ppermute(y_one, ("dom", "yz"), once_y)
    from_y_two = lax.ppermute(y_two, ("dom", "yz"), [(b, a) for a, b in once_y])
    from_x_one = lax.ppermute(x_one, ("dom", "gx"), once_x)
    from_x_two = lax.ppermute(x_two, ("dom", "gx"), [(b, a) for a, b in once_x])

    whole = jax.ShapeDtypeStruct((ncomp, len_x, len_y, len_z), jnp.float32)
    rim_x = jax.ShapeDtypeStruct((ncomp, len_y, len_z), jnp.float32)
    rim_y = jax.ShapeDtypeStruct((ncomp, len_x, len_z), jnp.float32)
    part, *rims = pl.pallas_call(
        functools.partial(inner_kernel, dims),
        out_shape=[whole, rim_x, rim_x, rim_y, rim_y],
        in_specs=[VM],
        out_specs=[HB] + [VM] * 4,
        scratch_shapes=[
            pltpu.VMEM((ncomp, len_x, len_y, len_z), jnp.float32),
            pltpu.SemaphoreType.DMA((len_x,)),
        ],
        compiler_params=pltpu.CompilerParams(vmem_limit_bytes=8 * MIB),
        cost_estimate=pl.CostEstimate(
            flops=300 * cell_rows * len_z, bytes_accessed=8 * cell_rows * len_z, transcendentals=0
        ),
        name="inner_faces",
    )(filled)

    updated = pl.pallas_call(
        functools.partial(edge_kernel, dims),
        out_shape=whole,
        in_specs=[HB] + [VM] * 13,
        out_specs=HB,
        scratch_shapes=[
            pltpu.VMEM((ncomp, len_y, len_z), jnp.float32),
            pltpu.VMEM((ncomp, len_y, len_z), jnp.float32),
            pltpu.VMEM((ncomp, len_x - 2, len_z), jnp.float32),
            pltpu.VMEM((ncomp, len_x - 2, len_z), jnp.float32),
            pltpu.SemaphoreType.DMA((4,)),
        ],
        input_output_aliases={0: 0},
        compiler_params=pltpu.CompilerParams(vmem_limit_bytes=8 * MIB),
        name="edge_faces",
    )(part, *rims, y_one, y_two, x_one, x_two, from_y_one, from_y_two, from_x_one, from_x_two, wrap.reshape(ncomp * len_y, len_z))
    return updated.reshape(1, ncomp, len_x, len_y, len_z)


def solution(mesh):
    placed = (
        P("dom", None, "gx", "yz", None),
        P("gx", None, None),
        P("gx", "yz", None, None),
        P("gx", "yz", None),
        P("gx", "yz", None, None, None, None),
    )
    return jax.shard_map(
        local,
        mesh=mesh,
        in_specs=placed,
        out_specs=P("dom", None, "gx", "yz", None),
        check_vma=False,
    )
```

```python
import functools

import jax
import jax.numpy as jnp
from jax import lax
from jax.experimental import pallas as pl
from jax.experimental.pallas import tpu as pltpu
from jax.sharding import PartitionSpec as P

BLK = 8
SR = 2
CAP = 2
LANES = 128
MIB = 2**20
VMEM_BYTES = 64 * MIB

HEAT_RATIO = 5.0 / 3.0
CORONA_RATIO = 0.04
HELIO_RATIO = 0.03

VM = pl.BlockSpec(memory_space=pltpu.VMEM)
HB = pl.BlockSpec(memory_space=pltpu.HBM)


def partner(index, step, count):
    if count & (count - 1) == 0:
        return index ^ step
    return (index + step) % count


def cycle(count):
    pairs = [(count + i, count + i + 1) for i in range(count - 1)] + [(2 * count - 1, count - 1)]
    return pairs + [(i + 1, i) for i in range(count - 1)] + [(0, count)]


def wrap_pairs(count, lines):
    def index(domain, column, line):
        return (domain * count + column) * lines + line

    pairs = []
    for t in range(lines):
        pairs.append((index(0, 0, t), index(0, count - 1, t)))
        pairs += [(index(0, g, t), index(1, g, t)) for g in range(1, count - 1)]
    pairs += [(index(1, g, t), index(1, g, t + 1)) for g in (0, count - 1) for t in range(0, lines - 1, 2)]
    return pairs + [(b, a) for a, b in pairs]


def pack_kernel(dims, owner_hbm, source_hbm, target_hbm, grid_hbm, *rest):
    ncomp, len_x, len_y, len_z, n_yz, shells, slots, depth = dims
    outs, carried, wrap = rest[:n_yz], rest[n_yz], rest[n_yz + 1]
    grid_ref, owner_ref, source_ref, target_ref, table, plan, spread, send, sems = rest[n_yz + 2 :]
    me = lax.axis_index("yz")
    plane = len_x * len_y
    n_bx, n_by, half = len_x // BLK, len_y // BLK, BLK // 2
    pitch = grid_ref.shape[1]
    flat = grid_ref.reshape(ncomp * pitch, len_z)
    onto = carried.at[pl.ds(0, ncomp)]
    slabs = [pl.ds(bx * BLK * len_y, BLK * len_y) for bx in range(n_bx)]
    grid_copies = [
        pltpu.make_async_copy(grid_hbm.at[:, slab, :], grid_ref.at[:, slab, :], sems.at[bx]) for bx, slab in enumerate(slabs)
    ]
    onward = [
        pltpu.make_async_copy(grid_ref.at[:, slab, :], onto.at[:, slab, :], sems.at[n_bx + bx])
        for bx, slab in enumerate(slabs)
    ]
    end = jnp.where(lax.axis_index("gx") == 0, 0, plane - len_y)
    first_sem = 2 * n_bx + 1
    wrap_copy = pltpu.make_async_copy(
        grid_ref.at[:, pl.ds(pl.multiple_of(end, BLK), len_y), :], wrap, sems.at[2 * n_bx]
    )
    copies = [
        pltpu.make_async_copy(owner_hbm, owner_ref, sems.at[first_sem]),
        pltpu.make_async_copy(source_hbm, source_ref, sems.at[first_sem + 1]),
        pltpu.make_async_copy(target_hbm, target_ref, sems.at[first_sem + 2]),
    ]

    @pl.when(lax.axis_index("dom") == 1)
    def _():
        for copy in copies:
            copy.start()
        for copy in grid_copies:
            copy.start()
        for copy in copies:
            copy.wait()
        position = jnp.int32(0)
        for t in range(n_yz):
            if n_yz & (n_yz - 1) == 0:
                step = t ^ me
            else:
                step = lax.rem(me - t + n_yz, n_yz)
            rank = jnp.int32(0)
            for b in range(shells):
                table[jnp.minimum(position, n_yz * CAP)] = step * CAP + jnp.minimum(rank, CAP - 1)
                mine = jnp.where(owner_ref[0, t, b] == me, 1, 0)
                position = position + mine
                rank = rank + mine
        for j in range(slots):
            for k in range(depth):
                entry = source_ref[0, 0, j, k]
                spot = jnp.where(entry >= 0, table[jnp.clip(entry, 0, n_yz * CAP)], -1)
                plan[j * depth + k : j * depth + k + 1, :] = jnp.full((1, LANES), spot.astype(jnp.float32))
            plan[slots * depth + j : slots * depth + j + 1, :] = jnp.full(
                (1, LANES), target_ref[0, 0, j].astype(jnp.float32)
            )
        told = pltpu.make_async_copy(plan, carried.at[ncomp, pl.ds(0, plan.shape[0])], sems.at[first_sem + 3])
        told.start()
        for arriving, leaving in zip(grid_copies, onward):
            arriving.wait()
            leaving.start()
        told.wait()
        for copy in onward:
            copy.wait()

    @pl.when(lax.axis_index("dom") == 0)
    def _():
        copies[0].start()
        for copy in grid_copies:
            copy.start()
        z_from = len_z - SR * BLK
        row_z = lax.broadcasted_iota(jnp.int32, (LANES, SR * LANES), 0) + (len_z - LANES)
        column = lax.broadcasted_iota(jnp.int32, (LANES, SR * LANES), 1)
        hit = row_z == z_from + column // LANES * BLK + column % BLK
        place = jnp.where(hit, column % LANES // BLK, -1)
        for m in range(2 * BLK):
            spread[m * LANES : (m + 1) * LANES, :] = jnp.where(place == m, 1.0, 0.0).astype(jnp.bfloat16)
        send[...] = jnp.zeros_like(send)
        copies[0].wait()
        spots = []
        for b in range(shells):
            owner = owner_ref[0, me, b]
            rank = jnp.int32(0)
            for other in range(b):
                rank = rank + jnp.where(owner_ref[0, me, other] == owner, 1, 0)
            if n_yz & (n_yz - 1) == 0:
                step = owner ^ me
            else:
                step = lax.rem(owner - me + n_yz, n_yz)
            spots.append(jnp.clip(step * CAP + rank, 0, n_yz * CAP - 1))
        rows = half * ncomp
        lines = []
        for bx in range(n_bx):
            grid_copies[bx].wait()
            onward[bx].start()
            line = []
            for ap in range(2):
                for cy in range(BLK):
                    pieces = []
                    for by in range(n_by):
                        for a2 in range(half):
                            first = (bx * BLK + a2 * 2 + ap) * len_y + by * BLK + cy
                            pieces.append(flat[pl.ds(first, ncomp, stride=pitch), :])
                    line.append(jnp.concatenate(pieces, axis=0).astype(jnp.bfloat16))
            lines.append(jnp.concatenate(line, axis=1))
        total = jnp.dot(jnp.concatenate(lines, axis=0), spread[...], preferred_element_type=jnp.float32)
        total = total.astype(jnp.bfloat16)
        for b in range(shells):
            column_block, br = b // SR, b % SR
            send[spots[b]] = total[
                column_block * rows : (column_block + 1) * rows, br * LANES : (br + 1) * LANES
            ]
        wrap_copy.start()
        sends = [
            pltpu.make_async_copy(send.at[pl.ds(step * CAP, CAP)], outs[step], sems.at[first_sem + 4 + step])
            for step in range(n_yz)
        ]
        for copy in sends:
            copy.start()
        for copy in [wrap_copy] + onward + sends:
            copy.wait()


def early(size):
    return (lax.axis_index("dom") == 0) & (lax.axis_index("gx") < size)


def early_kernel(carried, wrap_in, grid_ref, wrap_out, sem):
    @pl.when(early(1))
    def _():
        copy = pltpu.make_async_copy(carried.at[pl.ds(0, grid_ref.shape[0])], grid_ref, sem)
        copy.start()
        copy.wait()


def stage_kernel(weight_hbm, carried, grid_in, weight_ref, grid_ref, plan_ref, sems):
    blocks, ncomp, plan_rows = weight_ref.shape[0], grid_ref.shape[0], plan_ref.shape[0]
    grid_copy = pltpu.make_async_copy(carried.at[pl.ds(0, ncomp)], grid_ref, sems.at[blocks])
    copies = [pltpu.make_async_copy(weight_hbm.at[i], weight_ref.at[i], sems.at[i]) for i in range(blocks)]
    copies.append(pltpu.make_async_copy(carried.at[ncomp, pl.ds(0, plan_rows)], plan_ref, sems.at[blocks + 1]))
    copies.append(grid_copy)

    @pl.when(lax.axis_index("dom") == 1)
    def _():
        for copy in copies:
            copy.start()
        for copy in copies:
            copy.wait()

    @pl.when(early(1))
    def _():
        grid_ref[...] = grid_in[...]

    @pl.when((lax.axis_index("dom") == 0) & jnp.logical_not(early(1)))
    def _():
        grid_copy.start()
        grid_copy.wait()


def fill_kernel(dims, plan_vmem, weight_ref, grid_ref, *rest):
    ncomp, len_x, len_y, len_z, n_yz, slots, depth = dims
    got = rest[:n_yz]
    filled, y_one, y_two, x_one, x_two, result, plan, sem = rest[n_yz:]
    half = BLK // 2
    rows = half * ncomp
    plane = len_x * len_y

    helio = lax.axis_index("dom") == 1
    filled[...] = grid_ref[...]

    @pl.when(helio)
    def _():
        copy = pltpu.make_async_copy(plan_vmem, plan, sem)
        copy.start()
        held = [
            got[step][slot].astype(jnp.float32)
            for step in range(n_yz)
            for slot in range(CAP)
        ]
        lines = []
        for j in range(slots):
            sources = []
            for k in range(depth):
                entry = j * depth + k
                spot = jnp.broadcast_to(plan_vmem[entry : entry + 1, :], (rows, LANES))
                block = jnp.zeros((rows, LANES), jnp.float32)
                for place, candidate in enumerate(held):
                    block = jnp.where(spot == float(place), candidate, block)
                sources += [block[a2 * ncomp : (a2 + 1) * ncomp, :] for a2 in range(half)]
            cells = jnp.concatenate(sources, axis=1).astype(jnp.bfloat16)
            dense = weight_ref[j * depth : (j + 1) * depth].reshape(depth * weight_ref.shape[1], weight_ref.shape[2])
            total = jnp.dot(cells, dense, preferred_element_type=jnp.float32)
            lines += [total[:, a2 * LANES : (a2 + 1) * LANES] for a2 in range(half)]
        lines = jnp.concatenate(lines, axis=0)
        top = lines.astype(jnp.bfloat16)
        rest = lines - top.astype(jnp.float32)
        middle = rest.astype(jnp.bfloat16)
        bottom = (rest - middle.astype(jnp.float32)).astype(jnp.bfloat16)
        lines = jnp.concatenate([top, middle, bottom], axis=0)
        count = slots * rows
        pitch = count + BLK
        from_lane = lax.broadcasted_iota(jnp.int32, (LANES, LANES), 0)
        to_lane = lax.broadcasted_iota(jnp.int32, (LANES, LANES), 1)
        same = from_lane % BLK == to_lane % BLK
        for m in range(2 * BLK):
            spread = jnp.where(same & (from_lane // BLK == m), 1.0, 0.0).astype(jnp.bfloat16)
            parts = jnp.dot(lines, spread, preferred_element_type=jnp.float32)
            result[m * pitch : m * pitch + count, :] = parts[:count] + parts[count : 2 * count] + parts[2 * count :]
        copy.wait()
        lane = lax.broadcasted_iota(jnp.int32, (BLK, LANES), 1)
        per_y, per_z = len_y // BLK, len_z // BLK
        for j in range(slots):
            target = plan[slots * depth + j, 0].astype(jnp.int32)

            @pl.when(target >= 0)
            def _():
                block_x = target // (per_y * per_z)
                block_y = target // per_z % per_y
                z_from = target % per_z * BLK
                inside = (lane >= z_from) & (lane < z_from + BLK)
                first = block_x * BLK * len_y + block_y * BLK
                for a in range(BLK):
                    spots = [
                        pl.ds(pl.multiple_of(first + c * plane + a * len_y, BLK), BLK) for c in range(ncomp)
                    ]
                    row = a % 2 * BLK * pitch + j * rows + a // 2 * ncomp
                    old = [filled[spot, :] for spot in spots]
                    new = [result[pl.ds(row + c, BLK, stride=pitch), :] for c in range(ncomp)]
                    for spot, before, after in zip(spots, old, new):
                        filled[spot, :] = jnp.where(inside, after, before)

    def faces(x_low, x_high, y_low, y_high):
        for c in range(ncomp):
            x_low[c * len_y : (c + 1) * len_y, :] = filled[c * plane : c * plane + len_y, :]
            x_high[c * len_y : (c + 1) * len_y, :] = filled[(c + 1) * plane - len_y : (c + 1) * plane, :]
            y_low[c * len_x : (c + 1) * len_x, :] = filled[pl.ds(c * plane, len_x, stride=len_y), :]
            y_high[c * len_x : (c + 1) * len_x, :] = filled[
                pl.ds(c * plane + len_y - 1, len_x, stride=len_y), :
            ]

    @pl.when(helio)
    def _():
        faces(x_two, x_one, y_two, y_one)

    @pl.when(jnp.logical_not(helio))
    def _():
        faces(x_one, x_two, y_one, y_two)


def primitives(cells):
    density, energy = cells[0], cells[7]
    momentum, magnetic = cells[1:4], cells[4:7]
    inverse = 1.0 / density
    velocity = [m * inverse for m in momentum]
    field_sq = magnetic[0] * magnetic[0] + magnetic[1] * magnetic[1] + magnetic[2] * magnetic[2]
    kinetic = momentum[0] * velocity[0] + momentum[1] * velocity[1] + momentum[2] * velocity[2]
    pressure = (HEAT_RATIO - 1.0) * (energy - 0.5 * kinetic - 0.5 * field_sq)
    total_pressure = pressure + 0.5 * field_sq
    dot = velocity[0] * magnetic[0] + velocity[1] * magnetic[1] + velocity[2] * magnetic[2]
    fast = jnp.sqrt((HEAT_RATIO * pressure + field_sq) * inverse)
    return velocity, total_pressure, energy + total_pressure, dot, fast


def flux_of(cells, prims, direction):
    velocity, total_pressure, enthalpy, dot, fast = prims
    momentum, magnetic = cells[1:4], cells[4:7]
    speed, field = velocity[direction], magnetic[direction]
    flux = [momentum[direction]]
    for other in range(3):
        term = momentum[other] * speed - magnetic[other] * field
        flux.append(term + total_pressure if other == direction else term)
    for other in range(3):
        if other == direction:
            flux.append(None)
        else:
            flux.append(speed * magnetic[other] - field * velocity[other])
    flux.append(enthalpy * speed - field * dot)
    return flux, jnp.abs(speed) + fast


def face_sum(low, high):
    fastest = jnp.maximum(low[2], high[2])
    out = []
    for u_low, u_high, f_low, f_high in zip(low[0], high[0], low[1], high[1]):
        face = fastest * (u_high - u_low)
        out.append(face if f_low is None else face - (f_low + f_high))
    return out


def inner_kernel(dims, filled, out, rim_x_low, rim_x_high, rim_y_low, rim_y_high, part, sems):
    ncomp, len_x, len_y, len_z = dims
    plane = len_x * len_y
    half_ratio = jnp.where(lax.axis_index("dom") == 0, 0.5 * CORONA_RATIO, 0.5 * HELIO_RATIO).astype(jnp.float32)
    shape = (len_y, LANES)
    row = lax.broadcasted_iota(jnp.int32, shape, 0)
    lane = lax.broadcasted_iota(jnp.int32, shape, 1)

    def load(x):
        return [filled[pl.ds(pl.multiple_of(c * plane + x * len_y, BLK), len_y), :] for c in range(ncomp)]

    def shift_up(values, axis, size):
        return [None if v is None else pltpu.roll(v, size - 1, axis) for v in values]

    def step(x, carry, last):
        cells, prims, flux_x, speed_x, low_x = carry
        if last:
            high_x = [jnp.zeros(shape, jnp.float32)] * ncomp
            next_carry = None
        else:
            next_cells = load(x + 1)
            next_prims = primitives(next_cells)
            next_flux, next_speed = flux_of(next_cells, next_prims, 0)
            high_x = face_sum((cells, flux_x, speed_x), (next_cells, next_flux, next_speed))
            next_carry = (next_cells, next_prims, next_flux, next_speed, high_x)
        total = [high - low for high, low in zip(high_x, low_x)]
        flux, speed = flux_of(cells, prims, 1)
        beside = (shift_up(cells, 0, len_y), shift_up(flux, 0, len_y), pltpu.roll(speed, len_y - 1, 0))
        for c, face in enumerate(face_sum((cells, flux, speed), beside)):
            face = jnp.where(row == len_y - 1, 0.0, face)
            total[c] = total[c] + (face - pltpu.roll(face, 1, 0))
        flux, speed = flux_of(cells, prims, 2)
        beside = (shift_up(cells, 1, LANES), shift_up(flux, 1, LANES), pltpu.roll(speed, LANES - 1, 1))
        for c, face in enumerate(face_sum((cells, flux, speed), beside)):
            own = jnp.zeros(shape, jnp.float32) if flux[c] is None else -2.0 * flux[c]
            face = jnp.where(lane == LANES - 1, own, face)
            below = jnp.where(lane == 0, own, pltpu.roll(face, 1, 1))
            total[c] = total[c] + (face - below)
        for c in range(ncomp):
            part[c, x] = cells[c] + half_ratio * total[c]
        return next_carry

    def line_copy(x):
        return pltpu.make_async_copy(part.at[:, x], out.at[:, x], sems.at[x])

    cells = load(0)
    prims = primitives(cells)
    flux, speed = flux_of(cells, prims, 0)
    flux[4] = None
    zero = [jnp.zeros(shape, jnp.float32)] * ncomp
    carry = (cells, prims, flux, speed, zero)

    def pack(carry):
        cells, prims, flux, speed, low = carry
        return cells, prims, [f for f in flux if f is not None], speed, low

    def unpack(carry):
        cells, prims, flux, speed, low = carry
        return cells, prims, flux[:4] + [None] + flux[4:], speed, low

    def line(x, carry):
        carry = pack(step(x, unpack(carry), False))

        @pl.when(x > 0)
        def _():
            line_copy(x).start()

        return carry

    carry = lax.fori_loop(0, len_x - 1, line, pack(carry), unroll=3)
    step(len_x - 1, unpack(carry), True)
    for c in range(ncomp):
        rim_x_low[c] = part[c, 0]
        rim_x_high[c] = part[c, len_x - 1]
        rim_y_low[c] = part[c, :, 0, :]
        rim_y_high[c] = part[c, :, len_y - 1, :]
    for x in range(1, len_x - 1):
        line_copy(x).wait()


def edge_kernel(dims, part, rim_x_low, rim_x_high, rim_y_low, rim_y_high, *rest):
    ncomp, len_x, len_y, len_z = dims
    y_one, y_two, x_one, x_two, from_y_one, from_y_two, from_x_one, from_x_two, wrap = rest[:9]
    out, row_x_low, row_x_high, row_y_low, row_y_high, sems = rest[9:]
    helio = lax.axis_index("dom") == 1
    half_ratio = jnp.where(helio, 0.5 * HELIO_RATIO, 0.5 * CORONA_RATIO).astype(jnp.float32)

    def state(cells, direction):
        flux, speed = flux_of(cells, primitives(cells), direction)
        return cells, flux, speed

    def faces(own_ref, other_ref, end, end_ref, direction, upper, size):
        own = [own_ref[c * size : (c + 1) * size, :] for c in range(ncomp)]
        other = [other_ref[c * size : (c + 1) * size, :] for c in range(ncomp)]
        at_end = own if end_ref is None else [end_ref[c * size : (c + 1) * size, :] for c in range(ncomp)]
        other = [jnp.where(end, u, v) for u, v in zip(at_end, other)]
        own, other = state(own, direction), state(other, direction)
        if upper:
            return [half_ratio * f for f in face_sum(own, other)]
        return [-half_ratio * f for f in face_sum(other, own)]

    def both(x_low, x_high, y_low, y_high, from_x_low, from_x_high, from_y_low, from_y_high, x_end):
        column, line = lax.axis_index("gx"), lax.axis_index("yz")
        low_end, high_end = line == 0, line == lax.axis_size("yz") - 1
        y_lows = faces(y_low, from_y_low, low_end, None, 1, False, len_x)
        y_highs = faces(y_high, from_y_high, high_end, None, 1, True, len_x)
        for c in range(ncomp):
            row_y_low[c] = (rim_y_low[c] + y_lows[c])[1 : len_x - 1]
            row_y_high[c] = (rim_y_high[c] + y_highs[c])[1 : len_x - 1]
        inner_x = pl.ds(1, len_x - 2)
        copies = [
            pltpu.make_async_copy(row_y_low, out.at[:, inner_x, 0], sems.at[0]),
            pltpu.make_async_copy(row_y_high, out.at[:, inner_x, len_y - 1], sems.at[1]),
        ]
        copies[0].start()
        copies[1].start()
        low_end, high_end = column == 0, column == lax.axis_size("gx") - 1
        x_lows = faces(x_low, from_x_low, low_end, x_end, 0, False, len_y)
        x_highs = faces(x_high, from_x_high, high_end, x_end, 0, True, len_y)
        for row, rim, changes, x, sem in (
            (row_x_low, rim_x_low, x_lows, 0, 2),
            (row_x_high, rim_x_high, x_highs, len_x - 1, 3),
        ):
            for c in range(ncomp):
                row[c] = rim[c] + changes[c]
                row[c, 0:1] = row[c, 0:1] + y_lows[c][x : x + 1]
                row[c, len_y - 1 : len_y] = row[c, len_y - 1 : len_y] + y_highs[c][x : x + 1]
            copies.append(pltpu.make_async_copy(row, out.at[:, x], sems.at[sem]))
            copies[-1].start()
        for copy in copies:
            copy.wait()

    @pl.when(helio)
    def _():
        both(x_two, x_one, y_two, y_one, from_x_one, from_x_two, from_y_one, from_y_two, None)

    @pl.when(jnp.logical_not(helio))
    def _():
        both(x_one, x_two, y_one, y_two, from_x_two, from_x_one, from_y_two, from_y_one, wrap)


def local(field_state, shell_owner, block_sources, block_targets, interp_weights):
    _, ncomp, len_x, len_y, len_z = field_state.shape
    n_gx, n_yz = lax.axis_size("gx"), lax.axis_size("yz")
    shells = shell_owner.shape[2]
    slots, depth = block_sources.shape[2:]
    volume = BLK * BLK * BLK
    cell_rows = ncomp * len_x * len_y
    grid = field_state.reshape(ncomp, len_x * len_y, len_z)
    weights = interp_weights.reshape(slots * depth, volume, volume)
    rows = BLK // 2 * ncomp
    dims = (ncomp, len_x, len_y, len_z)

    plan_rows = -(-slots * (depth + 1) // BLK) * BLK
    face_x = jax.ShapeDtypeStruct((ncomp * len_y, len_z), jnp.float32)
    face_y = jax.ShapeDtypeStruct((ncomp * len_x, len_z), jnp.float32)
    plane = len_x * len_y
    carried_planes = max(ncomp + 1, 8 * MIB // (4 * LANES * plane))
    *packed, carried, wrap = pl.pallas_call(
        functools.partial(pack_kernel, dims + (n_yz, shells, slots, depth)),
        out_shape=[jax.ShapeDtypeStruct((CAP, rows, LANES), jnp.bfloat16)] * n_yz
        + [
            jax.ShapeDtypeStruct((carried_planes, plane, len_z), jnp.float32),
            jax.ShapeDtypeStruct((ncomp, len_y, len_z), jnp.float32),
        ],
        in_specs=[HB] * 4,
        out_specs=[HB] * (n_yz + 2),
        scratch_shapes=[
            pltpu.VMEM((ncomp, plane + BLK, len_z), jnp.float32),
            pltpu.SMEM(shell_owner.shape, jnp.int32),
            pltpu.SMEM(block_sources.shape, jnp.int32),
            pltpu.SMEM(block_targets.shape, jnp.int32),
            pltpu.SMEM((n_yz * CAP + 1,), jnp.int32),
            pltpu.VMEM((plan_rows, LANES), jnp.float32),
            pltpu.VMEM((2 * BLK * LANES, SR * LANES), jnp.bfloat16),
            pltpu.VMEM((n_yz * CAP, rows, LANES), jnp.bfloat16),
            pltpu.SemaphoreType.DMA((2 * (len_x // BLK) + 5 + n_yz,)),
        ],
        compiler_params=pltpu.CompilerParams(vmem_limit_bytes=VMEM_BYTES - 8 * MIB),
        name="pack_shell",
    )(shell_owner, block_sources, block_targets, grid)

    moved = []
    for step in range(n_yz):
        pairs = [(t, n_yz + partner(t, step, n_yz)) for t in range(n_yz)]
        pairs = pairs + [(b, a) for a, b in pairs]
        moved.append(lax.ppermute(packed[step], ("dom", "yz"), pairs))

    staged = [
        jax.ShapeDtypeStruct(weights.shape, weights.dtype),
        jax.ShapeDtypeStruct((ncomp, plane, len_z), jnp.float32),
        jax.ShapeDtypeStruct((plan_rows, LANES), jnp.float32),
    ]
    staged_bytes = sum(x.size * x.dtype.itemsize for x in staged)
    room = pltpu.CompilerParams(vmem_limit_bytes=VMEM_BYTES - 13 * staged_bytes // 4)
    grid, wrap = pl.pallas_call(
        early_kernel,
        out_shape=[staged[1], jax.ShapeDtypeStruct(wrap.shape, wrap.dtype)],
        in_specs=[HB] * 2,
        out_specs=[VM, HB],
        scratch_shapes=[pltpu.SemaphoreType.DMA],
        input_output_aliases={1: 1},
        compiler_params=room,
        name="early_grid",
    )(carried, wrap)
    wrap = lax.ppermute(wrap, ("dom", "gx", "yz"), wrap_pairs(n_gx, n_yz))
    weights, grid, plan = pl.pallas_call(
        stage_kernel,
        out_shape=staged,
        in_specs=[HB, HB, VM],
        out_specs=[VM] * 3,
        scratch_shapes=[pltpu.SemaphoreType.DMA((slots * depth + 2,))],
        input_output_aliases={2: 1},
        compiler_params=room,
        cost_estimate=pl.CostEstimate(flops=0, bytes_accessed=4 * interp_weights.size, transcendentals=0),
        name="stage_operands",
    )(weights, carried, grid)

    filled, y_one, y_two, x_one, x_two = pl.pallas_call(
        functools.partial(fill_kernel, dims + (n_yz, slots, depth)),
        out_shape=[jax.ShapeDtypeStruct((cell_rows, len_z), jnp.float32), face_y, face_y, face_x, face_x],
        in_specs=[VM, VM, VM] + [VM] * n_yz,
        out_specs=[VM] * 5,
        scratch_shapes=[
            pltpu.VMEM((2 * BLK * (slots * rows + BLK), LANES), jnp.float32),
            pltpu.SMEM((plan_rows, LANES), jnp.float32),
            pltpu.SemaphoreType.DMA,
        ],
        input_output_aliases={2: 0},
        compiler_params=pltpu.CompilerParams(vmem_limit_bytes=16 * MIB),
        name="fill_blocks",
    )(plan, weights, grid.reshape(cell_rows, len_z), *moved)

    once_x, once_y = cycle(n_gx), cycle(n_yz)
    from_y_one = lax.ppermute(y_one, ("dom", "yz"), once_y)
    from_y_two = lax.ppermute(y_two, ("dom", "yz"), [(b, a) for a, b in once_y])
    from_x_one = lax.ppermute(x_one, ("dom", "gx"), once_x)
    from_x_two = lax.ppermute(x_two, ("dom", "gx"), [(b, a) for a, b in once_x])

    whole = jax.ShapeDtypeStruct((ncomp, len_x, len_y, len_z), jnp.float32)
    rim_x = jax.ShapeDtypeStruct((ncomp, len_y, len_z), jnp.float32)
    rim_y = jax.ShapeDtypeStruct((ncomp, len_x, len_z), jnp.float32)
    part, *rims = pl.pallas_call(
        functools.partial(inner_kernel, dims),
        out_shape=[whole, rim_x, rim_x, rim_y, rim_y],
        in_specs=[VM],
        out_specs=[HB] + [VM] * 4,
        scratch_shapes=[
            pltpu.VMEM((ncomp, len_x, len_y, len_z), jnp.float32),
            pltpu.SemaphoreType.DMA((len_x,)),
        ],
        compiler_params=pltpu.CompilerParams(vmem_limit_bytes=8 * MIB),
        cost_estimate=pl.CostEstimate(
            flops=300 * cell_rows * len_z, bytes_accessed=8 * cell_rows * len_z, transcendentals=0
        ),
        name="inner_faces",
    )(filled)

    updated = pl.pallas_call(
        functools.partial(edge_kernel, dims),
        out_shape=whole,
        in_specs=[HB] + [VM] * 13,
        out_specs=HB,
        scratch_shapes=[
            pltpu.VMEM((ncomp, len_y, len_z), jnp.float32),
            pltpu.VMEM((ncomp, len_y, len_z), jnp.float32),
            pltpu.VMEM((ncomp, len_x - 2, len_z), jnp.float32),
            pltpu.VMEM((ncomp, len_x - 2, len_z), jnp.float32),
            pltpu.SemaphoreType.DMA((4,)),
        ],
        input_output_aliases={0: 0},
        compiler_params=pltpu.CompilerParams(vmem_limit_bytes=8 * MIB),
        name="edge_faces",
    )(part, *rims, y_one, y_two, x_one, x_two, from_y_one, from_y_two, from_x_one, from_x_two, wrap.reshape(ncomp * len_y, len_z))
    return updated.reshape(1, ncomp, len_x, len_y, len_z)


def solution(mesh):
    placed = (
        P("dom", None, "gx", "yz", None),
        P("gx", None, None),
        P("gx", "yz", None, None),
        P("gx", "yz", None),
        P("gx", "yz", None, None, None, None),
    )
    return jax.shard_map(
        local,
        mesh=mesh,
        in_specs=placed,
        out_specs=P("dom", None, "gx", "yz", None),
        check_vma=False,
    )
```

```python
import functools

import jax
import jax.numpy as jnp
from jax import lax
from jax.experimental import pallas as pl
from jax.experimental.pallas import tpu as pltpu
from jax.sharding import PartitionSpec as P

BLK = 8
SR = 2
CAP = 2
LANES = 128
MIB = 2**20
VMEM_BYTES = 64 * MIB

HEAT_RATIO = 5.0 / 3.0
CORONA_RATIO = 0.04
HELIO_RATIO = 0.03

VM = pl.BlockSpec(memory_space=pltpu.VMEM)
HB = pl.BlockSpec(memory_space=pltpu.HBM)


def partner(index, step, count):
    if count & (count - 1) == 0:
        return index ^ step
    return (index + step) % count


def cycle(count):
    pairs = [(count + i, count + i + 1) for i in range(count - 1)] + [(2 * count - 1, count - 1)]
    return pairs + [(i + 1, i) for i in range(count - 1)] + [(0, count)]


def wrap_pairs(count, lines):
    def index(domain, column, line):
        return (domain * count + column) * lines + line

    pairs = []
    for t in range(lines):
        pairs.append((index(0, 0, t), index(0, count - 1, t)))
        pairs += [(index(0, g, t), index(1, g, t)) for g in range(1, count - 1)]
    pairs += [(index(1, g, t), index(1, g, t + 1)) for g in (0, count - 1) for t in range(0, lines - 1, 2)]
    return pairs + [(b, a) for a, b in pairs]


def pack_kernel(dims, owner_hbm, source_hbm, target_hbm, grid_hbm, *rest):
    ncomp, len_x, len_y, len_z, n_yz, shells, slots, depth = dims
    outs, carried, wrap = rest[:n_yz], rest[n_yz], rest[n_yz + 1]
    grid_ref, owner_ref, source_ref, target_ref, table, plan, spread, send, sems = rest[n_yz + 2 :]
    me = lax.axis_index("yz")
    plane = len_x * len_y
    n_bx, n_by, half = len_x // BLK, len_y // BLK, BLK // 2
    pitch = grid_ref.shape[1]
    flat = grid_ref.reshape(ncomp * pitch, len_z)
    onto = carried.at[pl.ds(0, ncomp)]
    slabs = [pl.ds(bx * BLK * len_y, BLK * len_y) for bx in range(n_bx)]
    grid_copies = [
        pltpu.make_async_copy(grid_hbm.at[:, slab, :], grid_ref.at[:, slab, :], sems.at[bx]) for bx, slab in enumerate(slabs)
    ]
    onward = [
        pltpu.make_async_copy(grid_ref.at[:, slab, :], onto.at[:, slab, :], sems.at[n_bx + bx])
        for bx, slab in enumerate(slabs)
    ]
    end = jnp.where(lax.axis_index("gx") == 0, 0, plane - len_y)
    first_sem = 2 * n_bx + 1
    wrap_copy = pltpu.make_async_copy(
        grid_ref.at[:, pl.ds(pl.multiple_of(end, BLK), len_y), :], wrap, sems.at[2 * n_bx]
    )
    copies = [
        pltpu.make_async_copy(owner_hbm, owner_ref, sems.at[first_sem]),
        pltpu.make_async_copy(source_hbm, source_ref, sems.at[first_sem + 1]),
        pltpu.make_async_copy(target_hbm, target_ref, sems.at[first_sem + 2]),
    ]

    @pl.when(lax.axis_index("dom") == 1)
    def _():
        for copy in copies:
            copy.start()
        for copy in grid_copies:
            copy.start()
        for copy in copies:
            copy.wait()
        position = jnp.int32(0)
        for t in range(n_yz):
            if n_yz & (n_yz - 1) == 0:
                step = t ^ me
            else:
                step = lax.rem(me - t + n_yz, n_yz)
            rank = jnp.int32(0)
            for b in range(shells):
                table[jnp.minimum(position, n_yz * CAP)] = step * CAP + jnp.minimum(rank, CAP - 1)
                mine = jnp.where(owner_ref[0, t, b] == me, 1, 0)
                position = position + mine
                rank = rank + mine
        for j in range(slots):
            for k in range(depth):
                entry = source_ref[0, 0, j, k]
                spot = jnp.where(entry >= 0, table[jnp.clip(entry, 0, n_yz * CAP)], -1)
                plan[j * depth + k : j * depth + k + 1, :] = jnp.full((1, LANES), spot.astype(jnp.float32))
            plan[slots * depth + j : slots * depth + j + 1, :] = jnp.full(
                (1, LANES), target_ref[0, 0, j].astype(jnp.float32)
            )
        told = pltpu.make_async_copy(plan, carried.at[ncomp, pl.ds(0, plan.shape[0])], sems.at[first_sem + 3])
        told.start()
        for arriving, leaving in zip(grid_copies, onward):
            arriving.wait()
            leaving.start()
        told.wait()
        for copy in onward:
            copy.wait()

    @pl.when(lax.axis_index("dom") == 0)
    def _():
        copies[0].start()
        for copy in grid_copies:
            copy.start()
        z_from = len_z - SR * BLK
        row_z = lax.broadcasted_iota(jnp.int32, (LANES, SR * LANES), 0) + (len_z - LANES)
        column = lax.broadcasted_iota(jnp.int32, (LANES, SR * LANES), 1)
        hit = row_z == z_from + column // LANES * BLK + column % BLK
        place = jnp.where(hit, column % LANES // BLK, -1)
        for m in range(2 * BLK):
            spread[m * LANES : (m + 1) * LANES, :] = jnp.where(place == m, 1.0, 0.0).astype(jnp.bfloat16)
        send[...] = jnp.zeros_like(send)
        copies[0].wait()
        spots = []
        for b in range(shells):
            owner = owner_ref[0, me, b]
            rank = jnp.int32(0)
            for other in range(b):
                rank = rank + jnp.where(owner_ref[0, me, other] == owner, 1, 0)
            if n_yz & (n_yz - 1) == 0:
                step = owner ^ me
            else:
                step = lax.rem(owner - me + n_yz, n_yz)
            spots.append(jnp.clip(step * CAP + rank, 0, n_yz * CAP - 1))
        rows = half * ncomp
        lines = []
        for bx in range(n_bx):
            grid_copies[bx].wait()
            onward[bx].start()
            line = []
            for ap in range(2):
                for cy in range(BLK):
                    pieces = []
                    for by in range(n_by):
                        for a2 in range(half):
                            first = (bx * BLK + a2 * 2 + ap) * len_y + by * BLK + cy
                            pieces.append(flat[pl.ds(first, ncomp, stride=pitch), :])
                    line.append(jnp.concatenate(pieces, axis=0).astype(jnp.bfloat16))
            lines.append(jnp.concatenate(line, axis=1))
        total = jnp.dot(jnp.concatenate(lines, axis=0), spread[...], preferred_element_type=jnp.float32)
        total = total.astype(jnp.bfloat16)
        for b in range(shells):
            column_block, br = b // SR, b % SR
            send[spots[b]] = total[
                column_block * rows : (column_block + 1) * rows, br * LANES : (br + 1) * LANES
            ]
        wrap_copy.start()
        sends = [
            pltpu.make_async_copy(send.at[pl.ds(step * CAP, CAP)], outs[step], sems.at[first_sem + 4 + step])
            for step in range(n_yz)
        ]
        for copy in sends:
            copy.start()
        for copy in [wrap_copy] + onward + sends:
            copy.wait()


def early(size):
    return (lax.axis_index("dom") == 0) & (lax.axis_index("gx") < size)


def early_kernel(carried, wrap_in, grid_ref, wrap_out, sem):
    @pl.when(early(1))
    def _():
        copy = pltpu.make_async_copy(carried.at[pl.ds(0, grid_ref.shape[0])], grid_ref, sem)
        copy.start()
        copy.wait()


def stage_kernel(carried, grid_ref, plan_ref, sems):
    ncomp, plan_rows = grid_ref.shape[0], plan_ref.shape[0]
    grid_copy = pltpu.make_async_copy(carried.at[pl.ds(0, ncomp)], grid_ref, sems.at[0])
    copies = [pltpu.make_async_copy(carried.at[ncomp, pl.ds(0, plan_rows)], plan_ref, sems.at[1]), grid_copy]

    @pl.when(lax.axis_index("dom") == 1)
    def _():
        for copy in copies:
            copy.start()
        for copy in copies:
            copy.wait()

    @pl.when((lax.axis_index("dom") == 0) & jnp.logical_not(early(1)))
    def _():
        grid_copy.start()
        grid_copy.wait()


def fill_kernel(dims, plan_vmem, weight_ref, grid_ref, early_ref, *rest):
    ncomp, len_x, len_y, len_z, n_yz, slots, depth = dims
    got = rest[:n_yz]
    filled, y_one, y_two, x_one, x_two, result, plan, sem = rest[n_yz:]
    half = BLK // 2
    rows = half * ncomp
    plane = len_x * len_y

    helio = lax.axis_index("dom") == 1
    ahead = early(1)

    @pl.when(ahead)
    def _():
        filled[...] = early_ref[...]

    @pl.when(jnp.logical_not(ahead))
    def _():
        filled[...] = grid_ref[...]

    @pl.when(helio)
    def _():
        copy = pltpu.make_async_copy(plan_vmem, plan, sem)
        copy.start()
        held = [
            got[step][slot].astype(jnp.float32)
            for step in range(n_yz)
            for slot in range(CAP)
        ]
        lines = []
        for j in range(slots):
            sources = []
            for k in range(depth):
                entry = j * depth + k
                spot = jnp.broadcast_to(plan_vmem[entry : entry + 1, :], (rows, LANES))
                block = jnp.zeros((rows, LANES), jnp.float32)
                for place, candidate in enumerate(held):
                    block = jnp.where(spot == float(place), candidate, block)
                sources += [block[a2 * ncomp : (a2 + 1) * ncomp, :] for a2 in range(half)]
            cells = jnp.concatenate(sources, axis=1).astype(jnp.bfloat16)
            dense = weight_ref[j * depth : (j + 1) * depth].reshape(depth * weight_ref.shape[1], weight_ref.shape[2])
            total = jnp.dot(cells, dense, preferred_element_type=jnp.float32)
            lines += [total[:, a2 * LANES : (a2 + 1) * LANES] for a2 in range(half)]
        lines = jnp.concatenate(lines, axis=0)
        top = lines.astype(jnp.bfloat16)
        rest = lines - top.astype(jnp.float32)
        middle = rest.astype(jnp.bfloat16)
        bottom = (rest - middle.astype(jnp.float32)).astype(jnp.bfloat16)
        lines = jnp.concatenate([top, middle, bottom], axis=0)
        count = slots * rows
        pitch = count + BLK
        from_lane = lax.broadcasted_iota(jnp.int32, (LANES, LANES), 0)
        to_lane = lax.broadcasted_iota(jnp.int32, (LANES, LANES), 1)
        same = from_lane % BLK == to_lane % BLK
        for m in range(2 * BLK):
            spread = jnp.where(same & (from_lane // BLK == m), 1.0, 0.0).astype(jnp.bfloat16)
            parts = jnp.dot(lines, spread, preferred_element_type=jnp.float32)
            result[m * pitch : m * pitch + count, :] = parts[:count] + parts[count : 2 * count] + parts[2 * count :]
        copy.wait()
        lane = lax.broadcasted_iota(jnp.int32, (BLK, LANES), 1)
        per_y, per_z = len_y // BLK, len_z // BLK
        for j in range(slots):
            target = plan[slots * depth + j, 0].astype(jnp.int32)

            @pl.when(target >= 0)
            def _():
                block_x = target // (per_y * per_z)
                block_y = target // per_z % per_y
                z_from = target % per_z * BLK
                inside = (lane >= z_from) & (lane < z_from + BLK)
                first = block_x * BLK * len_y + block_y * BLK
                for a in range(BLK):
                    spots = [
                        pl.ds(pl.multiple_of(first + c * plane + a * len_y, BLK), BLK) for c in range(ncomp)
                    ]
                    row = a % 2 * BLK * pitch + j * rows + a // 2 * ncomp
                    old = [filled[spot, :] for spot in spots]
                    new = [result[pl.ds(row + c, BLK, stride=pitch), :] for c in range(ncomp)]
                    for spot, before, after in zip(spots, old, new):
                        filled[spot, :] = jnp.where(inside, after, before)

    def faces(x_low, x_high, y_low, y_high):
        for c in range(ncomp):
            x_low[c * len_y : (c + 1) * len_y, :] = filled[c * plane : c * plane + len_y, :]
            x_high[c * len_y : (c + 1) * len_y, :] = filled[(c + 1) * plane - len_y : (c + 1) * plane, :]
            y_low[c * len_x : (c + 1) * len_x, :] = filled[pl.ds(c * plane, len_x, stride=len_y), :]
            y_high[c * len_x : (c + 1) * len_x, :] = filled[
                pl.ds(c * plane + len_y - 1, len_x, stride=len_y), :
            ]

    @pl.when(helio)
    def _():
        faces(x_two, x_one, y_two, y_one)

    @pl.when(jnp.logical_not(helio))
    def _():
        faces(x_one, x_two, y_one, y_two)


def primitives(cells):
    density, energy = cells[0], cells[7]
    momentum, magnetic = cells[1:4], cells[4:7]
    inverse = 1.0 / density
    velocity = [m * inverse for m in momentum]
    field_sq = magnetic[0] * magnetic[0] + magnetic[1] * magnetic[1] + magnetic[2] * magnetic[2]
    kinetic = momentum[0] * velocity[0] + momentum[1] * velocity[1] + momentum[2] * velocity[2]
    pressure = (HEAT_RATIO - 1.0) * (energy - 0.5 * kinetic - 0.5 * field_sq)
    total_pressure = pressure + 0.5 * field_sq
    dot = velocity[0] * magnetic[0] + velocity[1] * magnetic[1] + velocity[2] * magnetic[2]
    fast = jnp.sqrt((HEAT_RATIO * pressure + field_sq) * inverse)
    return velocity, total_pressure, energy + total_pressure, dot, fast


def flux_of(cells, prims, direction):
    velocity, total_pressure, enthalpy, dot, fast = prims
    momentum, magnetic = cells[1:4], cells[4:7]
    speed, field = velocity[direction], magnetic[direction]
    flux = [momentum[direction]]
    for other in range(3):
        term = momentum[other] * speed - magnetic[other] * field
        flux.append(term + total_pressure if other == direction else term)
    for other in range(3):
        if other == direction:
            flux.append(None)
        else:
            flux.append(speed * magnetic[other] - field * velocity[other])
    flux.append(enthalpy * speed - field * dot)
    return flux, jnp.abs(speed) + fast


def face_sum(low, high):
    fastest = jnp.maximum(low[2], high[2])
    out = []
    for u_low, u_high, f_low, f_high in zip(low[0], high[0], low[1], high[1]):
        face = fastest * (u_high - u_low)
        out.append(face if f_low is None else face - (f_low + f_high))
    return out


def inner_kernel(dims, filled, out, rim_x_low, rim_x_high, rim_y_low, rim_y_high, part, sems):
    ncomp, len_x, len_y, len_z = dims
    plane = len_x * len_y
    half_ratio = jnp.where(lax.axis_index("dom") == 0, 0.5 * CORONA_RATIO, 0.5 * HELIO_RATIO).astype(jnp.float32)
    shape = (len_y, LANES)
    row = lax.broadcasted_iota(jnp.int32, shape, 0)
    lane = lax.broadcasted_iota(jnp.int32, shape, 1)

    def load(x):
        return [filled[pl.ds(pl.multiple_of(c * plane + x * len_y, BLK), len_y), :] for c in range(ncomp)]

    def shift_up(values, axis, size):
        return [None if v is None else pltpu.roll(v, size - 1, axis) for v in values]

    def step(x, carry, last):
        cells, prims, flux_x, speed_x, low_x = carry
        if last:
            high_x = [jnp.zeros(shape, jnp.float32)] * ncomp
            next_carry = None
        else:
            next_cells = load(x + 1)
            next_prims = primitives(next_cells)
            next_flux, next_speed = flux_of(next_cells, next_prims, 0)
            high_x = face_sum((cells, flux_x, speed_x), (next_cells, next_flux, next_speed))
            next_carry = (next_cells, next_prims, next_flux, next_speed, high_x)
        total = [high - low for high, low in zip(high_x, low_x)]
        flux, speed = flux_of(cells, prims, 1)
        beside = (shift_up(cells, 0, len_y), shift_up(flux, 0, len_y), pltpu.roll(speed, len_y - 1, 0))
        for c, face in enumerate(face_sum((cells, flux, speed), beside)):
            face = jnp.where(row == len_y - 1, 0.0, face)
            total[c] = total[c] + (face - pltpu.roll(face, 1, 0))
        flux, speed = flux_of(cells, prims, 2)
        beside = (shift_up(cells, 1, LANES), shift_up(flux, 1, LANES), pltpu.roll(speed, LANES - 1, 1))
        for c, face in enumerate(face_sum((cells, flux, speed), beside)):
            own = jnp.zeros(shape, jnp.float32) if flux[c] is None else -2.0 * flux[c]
            face = jnp.where(lane == LANES - 1, own, face)
            below = jnp.where(lane == 0, own, pltpu.roll(face, 1, 1))
            total[c] = total[c] + (face - below)
        for c in range(ncomp):
            part[c, x] = cells[c] + half_ratio * total[c]
        return next_carry

    def line_copy(x):
        return pltpu.make_async_copy(part.at[:, x], out.at[:, x], sems.at[x])

    cells = load(0)
    prims = primitives(cells)
    flux, speed = flux_of(cells, prims, 0)
    flux[4] = None
    zero = [jnp.zeros(shape, jnp.float32)] * ncomp
    carry = (cells, prims, flux, speed, zero)

    def pack(carry):
        cells, prims, flux, speed, low = carry
        return cells, prims, [f for f in flux if f is not None], speed, low

    def unpack(carry):
        cells, prims, flux, speed, low = carry
        return cells, prims, flux[:4] + [None] + flux[4:], speed, low

    def line(x, carry):
        carry = pack(step(x, unpack(carry), False))

        @pl.when(x > 0)
        def _():
            line_copy(x).start()

        return carry

    carry = lax.fori_loop(0, len_x - 1, line, pack(carry), unroll=3)
    step(len_x - 1, unpack(carry), True)
    for c in range(ncomp):
        rim_x_low[c] = part[c, 0]
        rim_x_high[c] = part[c, len_x - 1]
        rim_y_low[c] = part[c, :, 0, :]
        rim_y_high[c] = part[c, :, len_y - 1, :]
    for x in range(1, len_x - 1):
        line_copy(x).wait()


def edge_kernel(dims, part, rim_x_low, rim_x_high, rim_y_low, rim_y_high, *rest):
    ncomp, len_x, len_y, len_z = dims
    y_one, y_two, x_one, x_two, from_y_one, from_y_two, from_x_one, from_x_two, wrap = rest[:9]
    out, row_x_low, row_x_high, row_y_low, row_y_high, sems = rest[9:]
    helio = lax.axis_index("dom") == 1
    half_ratio = jnp.where(helio, 0.5 * HELIO_RATIO, 0.5 * CORONA_RATIO).astype(jnp.float32)

    def state(cells, direction):
        flux, speed = flux_of(cells, primitives(cells), direction)
        return cells, flux, speed

    def faces(own_ref, other_ref, end, end_ref, direction, upper, size):
        own = [own_ref[c * size : (c + 1) * size, :] for c in range(ncomp)]
        other = [other_ref[c * size : (c + 1) * size, :] for c in range(ncomp)]
        at_end = own if end_ref is None else [end_ref[c * size : (c + 1) * size, :] for c in range(ncomp)]
        other = [jnp.where(end, u, v) for u, v in zip(at_end, other)]
        own, other = state(own, direction), state(other, direction)
        if upper:
            return [half_ratio * f for f in face_sum(own, other)]
        return [-half_ratio * f for f in face_sum(other, own)]

    def both(x_low, x_high, y_low, y_high, from_x_low, from_x_high, from_y_low, from_y_high, x_end):
        column, line = lax.axis_index("gx"), lax.axis_index("yz")
        low_end, high_end = line == 0, line == lax.axis_size("yz") - 1
        y_lows = faces(y_low, from_y_low, low_end, None, 1, False, len_x)
        y_highs = faces(y_high, from_y_high, high_end, None, 1, True, len_x)
        for c in range(ncomp):
            row_y_low[c] = (rim_y_low[c] + y_lows[c])[1 : len_x - 1]
            row_y_high[c] = (rim_y_high[c] + y_highs[c])[1 : len_x - 1]
        inner_x = pl.ds(1, len_x - 2)
        copies = [
            pltpu.make_async_copy(row_y_low, out.at[:, inner_x, 0], sems.at[0]),
            pltpu.make_async_copy(row_y_high, out.at[:, inner_x, len_y - 1], sems.at[1]),
        ]
        copies[0].start()
        copies[1].start()
        low_end, high_end = column == 0, column == lax.axis_size("gx") - 1
        x_lows = faces(x_low, from_x_low, low_end, x_end, 0, False, len_y)
        x_highs = faces(x_high, from_x_high, high_end, x_end, 0, True, len_y)
        for row, rim, changes, x, sem in (
            (row_x_low, rim_x_low, x_lows, 0, 2),
            (row_x_high, rim_x_high, x_highs, len_x - 1, 3),
        ):
            for c in range(ncomp):
                row[c] = rim[c] + changes[c]
                row[c, 0:1] = row[c, 0:1] + y_lows[c][x : x + 1]
                row[c, len_y - 1 : len_y] = row[c, len_y - 1 : len_y] + y_highs[c][x : x + 1]
            copies.append(pltpu.make_async_copy(row, out.at[:, x], sems.at[sem]))
            copies[-1].start()
        for copy in copies:
            copy.wait()

    @pl.when(helio)
    def _():
        both(x_two, x_one, y_two, y_one, from_x_one, from_x_two, from_y_one, from_y_two, None)

    @pl.when(jnp.logical_not(helio))
    def _():
        both(x_one, x_two, y_one, y_two, from_x_two, from_x_one, from_y_two, from_y_one, wrap)


def local(field_state, shell_owner, block_sources, block_targets, interp_weights):
    _, ncomp, len_x, len_y, len_z = field_state.shape
    n_gx, n_yz = lax.axis_size("gx"), lax.axis_size("yz")
    shells = shell_owner.shape[2]
    slots, depth = block_sources.shape[2:]
    volume = BLK * BLK * BLK
    cell_rows = ncomp * len_x * len_y
    grid = field_state.reshape(ncomp, len_x * len_y, len_z)
    weights = interp_weights.reshape(slots * depth, volume, volume)
    rows = BLK // 2 * ncomp
    dims = (ncomp, len_x, len_y, len_z)

    plan_rows = -(-slots * (depth + 1) // BLK) * BLK
    face_x = jax.ShapeDtypeStruct((ncomp * len_y, len_z), jnp.float32)
    face_y = jax.ShapeDtypeStruct((ncomp * len_x, len_z), jnp.float32)
    plane = len_x * len_y
    carried_planes = max(ncomp + 1, 16 * MIB // (4 * LANES * plane))
    *packed, carried, wrap = pl.pallas_call(
        functools.partial(pack_kernel, dims + (n_yz, shells, slots, depth)),
        out_shape=[jax.ShapeDtypeStruct((CAP, rows, LANES), jnp.bfloat16)] * n_yz
        + [
            jax.ShapeDtypeStruct((carried_planes, plane, len_z), jnp.float32),
            jax.ShapeDtypeStruct((ncomp, len_y, len_z), jnp.float32),
        ],
        in_specs=[HB] * 4,
        out_specs=[HB] * (n_yz + 2),
        scratch_shapes=[
            pltpu.VMEM((ncomp, plane + BLK, len_z), jnp.float32),
            pltpu.SMEM(shell_owner.shape, jnp.int32),
            pltpu.SMEM(block_sources.shape, jnp.int32),
            pltpu.SMEM(block_targets.shape, jnp.int32),
            pltpu.SMEM((n_yz * CAP + 1,), jnp.int32),
            pltpu.VMEM((plan_rows, LANES), jnp.float32),
            pltpu.VMEM((2 * BLK * LANES, SR * LANES), jnp.bfloat16),
            pltpu.VMEM((n_yz * CAP, rows, LANES), jnp.bfloat16),
            pltpu.SemaphoreType.DMA((2 * (len_x // BLK) + 5 + n_yz,)),
        ],
        compiler_params=pltpu.CompilerParams(vmem_limit_bytes=VMEM_BYTES - 8 * MIB),
        name="pack_shell",
    )(shell_owner, block_sources, block_targets, grid)

    moved = []
    for step in range(n_yz):
        pairs = [(t, n_yz + partner(t, step, n_yz)) for t in range(n_yz)]
        pairs = pairs + [(b, a) for a, b in pairs]
        moved.append(lax.ppermute(packed[step], ("dom", "yz"), pairs))

    staged = [
        jax.ShapeDtypeStruct(weights.shape, weights.dtype),
        jax.ShapeDtypeStruct((ncomp, plane, len_z), jnp.float32),
        jax.ShapeDtypeStruct((plan_rows, LANES), jnp.float32),
    ]
    staged_bytes = sum(x.size * x.dtype.itemsize for x in staged)
    room = pltpu.CompilerParams(vmem_limit_bytes=VMEM_BYTES - 17 * staged_bytes // 4)
    early_grid, wrap = pl.pallas_call(
        early_kernel,
        out_shape=[staged[1], jax.ShapeDtypeStruct(wrap.shape, wrap.dtype)],
        in_specs=[HB] * 2,
        out_specs=[VM, HB],
        scratch_shapes=[pltpu.SemaphoreType.DMA],
        input_output_aliases={1: 1},
        compiler_params=room,
        name="early_grid",
    )(carried, wrap)
    wrap = lax.ppermute(wrap, ("dom", "gx", "yz"), wrap_pairs(n_gx, n_yz))
    grid, plan = pl.pallas_call(
        stage_kernel,
        out_shape=staged[1:],
        in_specs=[HB] * 1,
        out_specs=[VM] * 2,
        scratch_shapes=[pltpu.SemaphoreType.DMA((2,))],
        compiler_params=room,
        cost_estimate=pl.CostEstimate(flops=0, bytes_accessed=4 * interp_weights.size, transcendentals=0),
        name="stage_operands",
    )(carried)

    filled, y_one, y_two, x_one, x_two = pl.pallas_call(
        functools.partial(fill_kernel, dims + (n_yz, slots, depth)),
        out_shape=[jax.ShapeDtypeStruct((cell_rows, len_z), jnp.float32), face_y, face_y, face_x, face_x],
        in_specs=[VM] * (4 + n_yz),
        out_specs=[VM] * 5,
        scratch_shapes=[
            pltpu.VMEM((2 * BLK * (slots * rows + BLK), LANES), jnp.float32),
            pltpu.SMEM((plan_rows, LANES), jnp.float32),
            pltpu.SemaphoreType.DMA,
        ],
        input_output_aliases={2: 0},
        compiler_params=pltpu.CompilerParams(vmem_limit_bytes=16 * MIB),
        name="fill_blocks",
    )(plan, weights, grid.reshape(cell_rows, len_z), early_grid.reshape(cell_rows, len_z), *moved)

    once_x, once_y = cycle(n_gx), cycle(n_yz)
    from_y_one = lax.ppermute(y_one, ("dom", "yz"), once_y)
    from_y_two = lax.ppermute(y_two, ("dom", "yz"), [(b, a) for a, b in once_y])
    from_x_one = lax.ppermute(x_one, ("dom", "gx"), once_x)
    from_x_two = lax.ppermute(x_two, ("dom", "gx"), [(b, a) for a, b in once_x])

    whole = jax.ShapeDtypeStruct((ncomp, len_x, len_y, len_z), jnp.float32)
    rim_x = jax.ShapeDtypeStruct((ncomp, len_y, len_z), jnp.float32)
    rim_y = jax.ShapeDtypeStruct((ncomp, len_x, len_z), jnp.float32)
    part, *rims = pl.pallas_call(
        functools.partial(inner_kernel, dims),
        out_shape=[whole, rim_x, rim_x, rim_y, rim_y],
        in_specs=[VM],
        out_specs=[HB] + [VM] * 4,
        scratch_shapes=[
            pltpu.VMEM((ncomp, len_x, len_y, len_z), jnp.float32),
            pltpu.SemaphoreType.DMA((len_x,)),
        ],
        compiler_params=pltpu.CompilerParams(vmem_limit_bytes=8 * MIB),
        cost_estimate=pl.CostEstimate(
            flops=300 * cell_rows * len_z, bytes_accessed=8 * cell_rows * len_z, transcendentals=0
        ),
        name="inner_faces",
    )(filled)

    updated = pl.pallas_call(
        functools.partial(edge_kernel, dims),
        out_shape=whole,
        in_specs=[HB] + [VM] * 13,
        out_specs=HB,
        scratch_shapes=[
            pltpu.VMEM((ncomp, len_y, len_z), jnp.float32),
            pltpu.VMEM((ncomp, len_y, len_z), jnp.float32),
            pltpu.VMEM((ncomp, len_x - 2, len_z), jnp.float32),
            pltpu.VMEM((ncomp, len_x - 2, len_z), jnp.float32),
            pltpu.SemaphoreType.DMA((4,)),
        ],
        input_output_aliases={0: 0},
        compiler_params=pltpu.CompilerParams(vmem_limit_bytes=8 * MIB),
        name="edge_faces",
    )(part, *rims, y_one, y_two, x_one, x_two, from_y_one, from_y_two, from_x_one, from_x_two, wrap.reshape(ncomp * len_y, len_z))
    return updated.reshape(1, ncomp, len_x, len_y, len_z)


def solution(mesh):
    placed = (
        P("dom", None, "gx", "yz", None),
        P("gx", None, None),
        P("gx", "yz", None, None),
        P("gx", "yz", None),
        P("gx", "yz", None, None, None, None),
    )
    return jax.shard_map(
        local,
        mesh=mesh,
        in_specs=placed,
        out_specs=P("dom", None, "gx", "yz", None),
        check_vma=False,
    )
```

```python
import functools

import jax
import jax.numpy as jnp
from jax import lax
from jax.experimental import pallas as pl
from jax.experimental.pallas import tpu as pltpu
from jax.sharding import PartitionSpec as P

BLK = 8
SR = 2
CAP = 2
LANES = 128
MIB = 2**20
VMEM_BYTES = 64 * MIB

HEAT_RATIO = 5.0 / 3.0
CORONA_RATIO = 0.04
HELIO_RATIO = 0.03

VM = pl.BlockSpec(memory_space=pltpu.VMEM)
HB = pl.BlockSpec(memory_space=pltpu.HBM)


def partner(index, step, count):
    if count & (count - 1) == 0:
        return index ^ step
    return (index + step) % count


def cycle(count):
    pairs = [(count + i, count + i + 1) for i in range(count - 1)] + [(2 * count - 1, count - 1)]
    return pairs + [(i + 1, i) for i in range(count - 1)] + [(0, count)]


def wrap_pairs(count, lines):
    def index(domain, column, line):
        return (domain * count + column) * lines + line

    pairs = []
    for t in range(lines):
        pairs.append((index(0, 0, t), index(0, count - 1, t)))
        pairs += [(index(0, g, t), index(1, g, t)) for g in range(1, count - 1)]
    pairs += [(index(1, g, t), index(1, g, t + 1)) for g in (0, count - 1) for t in range(0, lines - 1, 2)]
    return pairs + [(b, a) for a, b in pairs]


def pack_kernel(dims, owner_hbm, source_hbm, target_hbm, grid_hbm, *rest):
    ncomp, len_x, len_y, len_z, n_yz, shells, slots, depth = dims
    outs, carried, wrap = rest[:n_yz], rest[n_yz], rest[n_yz + 1]
    grid_ref, owner_ref, source_ref, target_ref, table, plan, spread, send, sems = rest[n_yz + 2 :]
    me = lax.axis_index("yz")
    plane = len_x * len_y
    n_bx, n_by, half = len_x // BLK, len_y // BLK, BLK // 2
    pitch = grid_ref.shape[1]
    flat = grid_ref.reshape(ncomp * pitch, len_z)
    onto = carried.at[pl.ds(0, ncomp)]
    slabs = [pl.ds(bx * BLK * len_y, BLK * len_y) for bx in range(n_bx)]
    grid_copies = [
        pltpu.make_async_copy(grid_hbm.at[:, slab, :], grid_ref.at[:, slab, :], sems.at[bx]) for bx, slab in enumerate(slabs)
    ]
    onward = [
        pltpu.make_async_copy(grid_ref.at[:, slab, :], onto.at[:, slab, :], sems.at[n_bx + bx])
        for bx, slab in enumerate(slabs)
    ]
    end = jnp.where(lax.axis_index("gx") == 0, 0, plane - len_y)
    first_sem = 2 * n_bx + 1
    wrap_copy = pltpu.make_async_copy(
        grid_ref.at[:, pl.ds(pl.multiple_of(end, BLK), len_y), :], wrap, sems.at[2 * n_bx]
    )
    copies = [
        pltpu.make_async_copy(owner_hbm, owner_ref, sems.at[first_sem]),
        pltpu.make_async_copy(source_hbm, source_ref, sems.at[first_sem + 1]),
        pltpu.make_async_copy(target_hbm, target_ref, sems.at[first_sem + 2]),
    ]

    @pl.when(lax.axis_index("dom") == 1)
    def _():
        for copy in copies:
            copy.start()
        for copy in grid_copies:
            copy.start()
        for copy in copies:
            copy.wait()
        position = jnp.int32(0)
        for t in range(n_yz):
            if n_yz & (n_yz - 1) == 0:
                step = t ^ me
            else:
                step = lax.rem(me - t + n_yz, n_yz)
            rank = jnp.int32(0)
            for b in range(shells):
                table[jnp.minimum(position, n_yz * CAP)] = step * CAP + jnp.minimum(rank, CAP - 1)
                mine = jnp.where(owner_ref[0, t, b] == me, 1, 0)
                position = position + mine
                rank = rank + mine
        for j in range(slots):
            for k in range(depth):
                entry = source_ref[0, 0, j, k]
                spot = jnp.where(entry >= 0, table[jnp.clip(entry, 0, n_yz * CAP)], -1)
                plan[j * depth + k : j * depth + k + 1, :] = jnp.full((1, LANES), spot.astype(jnp.float32))
            plan[slots * depth + j : slots * depth + j + 1, :] = jnp.full(
                (1, LANES), target_ref[0, 0, j].astype(jnp.float32)
            )
        told = pltpu.make_async_copy(plan, carried.at[ncomp, pl.ds(0, plan.shape[0])], sems.at[first_sem + 3])
        told.start()
        for arriving, leaving in zip(grid_copies, onward):
            arriving.wait()
            leaving.start()
        told.wait()
        for copy in onward:
            copy.wait()

    @pl.when(lax.axis_index("dom") == 0)
    def _():
        copies[0].start()
        for copy in grid_copies:
            copy.start()
        z_from = len_z - SR * BLK
        row_z = lax.broadcasted_iota(jnp.int32, (LANES, SR * LANES), 0) + (len_z - LANES)
        column = lax.broadcasted_iota(jnp.int32, (LANES, SR * LANES), 1)
        hit = row_z == z_from + column // LANES * BLK + column % BLK
        place = jnp.where(hit, column % LANES // BLK, -1)
        for m in range(2 * BLK):
            spread[m * LANES : (m + 1) * LANES, :] = jnp.where(place == m, 1.0, 0.0).astype(jnp.bfloat16)
        send[...] = jnp.zeros_like(send)
        copies[0].wait()
        spots = []
        for b in range(shells):
            owner = owner_ref[0, me, b]
            rank = jnp.int32(0)
            for other in range(b):
                rank = rank + jnp.where(owner_ref[0, me, other] == owner, 1, 0)
            if n_yz & (n_yz - 1) == 0:
                step = owner ^ me
            else:
                step = lax.rem(owner - me + n_yz, n_yz)
            spots.append(jnp.clip(step * CAP + rank, 0, n_yz * CAP - 1))
        rows = half * ncomp
        lines = []
        for bx in range(n_bx):
            grid_copies[bx].wait()
            onward[bx].start()
            line = []
            for ap in range(2):
                for cy in range(BLK):
                    pieces = []
                    for by in range(n_by):
                        for a2 in range(half):
                            first = (bx * BLK + a2 * 2 + ap) * len_y + by * BLK + cy
                            pieces.append(flat[pl.ds(first, ncomp, stride=pitch), :])
                    line.append(jnp.concatenate(pieces, axis=0).astype(jnp.bfloat16))
            lines.append(jnp.concatenate(line, axis=1))
        total = jnp.dot(jnp.concatenate(lines, axis=0), spread[...], preferred_element_type=jnp.float32)
        total = total.astype(jnp.bfloat16)
        for b in range(shells):
            column_block, br = b // SR, b % SR
            send[spots[b]] = total[
                column_block * rows : (column_block + 1) * rows, br * LANES : (br + 1) * LANES
            ]
        wrap_copy.start()
        sends = [
            pltpu.make_async_copy(send.at[pl.ds(step * CAP, CAP)], outs[step], sems.at[first_sem + 4 + step])
            for step in range(n_yz)
        ]
        for copy in sends:
            copy.start()
        for copy in [wrap_copy] + onward + sends:
            copy.wait()


def early(size):
    return (lax.axis_index("dom") == 0) & (lax.axis_index("gx") < size)


def early_kernel(carried, wrap_in, grid_ref, wrap_out, sem):
    @pl.when(early(1))
    def _():
        copy = pltpu.make_async_copy(carried.at[pl.ds(0, grid_ref.shape[0])], grid_ref, sem)
        copy.start()
        copy.wait()


def stage_kernel(carried, grid_ref, plan_ref, sems):
    ncomp, plan_rows = grid_ref.shape[0], plan_ref.shape[0]
    grid_copy = pltpu.make_async_copy(carried.at[pl.ds(0, ncomp)], grid_ref, sems.at[0])
    copies = [pltpu.make_async_copy(carried.at[ncomp, pl.ds(0, plan_rows)], plan_ref, sems.at[1]), grid_copy]

    @pl.when(lax.axis_index("dom") == 1)
    def _():
        for copy in copies:
            copy.start()
        for copy in copies:
            copy.wait()

    @pl.when((lax.axis_index("dom") == 0) & jnp.logical_not(early(1)))
    def _():
        grid_copy.start()
        grid_copy.wait()


def fill_kernel(dims, plan_vmem, weight_ref, grid_ref, early_ref, *rest):
    ncomp, len_x, len_y, len_z, n_yz, slots, depth = dims
    got = rest[:n_yz][::-1]
    filled, y_one, y_two, x_one, x_two, result, plan, sem = rest[n_yz:]
    half = BLK // 2
    rows = half * ncomp
    plane = len_x * len_y

    helio = lax.axis_index("dom") == 1
    ahead = early(1)

    @pl.when(ahead)
    def _():
        filled[...] = early_ref[...]

    @pl.when(jnp.logical_not(ahead))
    def _():
        filled[...] = grid_ref[...]

    @pl.when(helio)
    def _():
        copy = pltpu.make_async_copy(plan_vmem, plan, sem)
        copy.start()
        held = [
            got[step][slot].astype(jnp.float32)
            for step in range(n_yz)
            for slot in range(CAP)
        ]
        lines = []
        for j in range(slots):
            sources = []
            for k in range(depth):
                entry = j * depth + k
                spot = jnp.broadcast_to(plan_vmem[entry : entry + 1, :], (rows, LANES))
                block = jnp.zeros((rows, LANES), jnp.float32)
                for place, candidate in enumerate(held):
                    block = jnp.where(spot == float(place), candidate, block)
                sources += [block[a2 * ncomp : (a2 + 1) * ncomp, :] for a2 in range(half)]
            cells = jnp.concatenate(sources, axis=1).astype(jnp.bfloat16)
            dense = weight_ref[j * depth : (j + 1) * depth].reshape(depth * weight_ref.shape[1], weight_ref.shape[2])
            total = jnp.dot(cells, dense, preferred_element_type=jnp.float32)
            lines += [total[:, a2 * LANES : (a2 + 1) * LANES] for a2 in range(half)]
        lines = jnp.concatenate(lines, axis=0)
        top = lines.astype(jnp.bfloat16)
        rest = lines - top.astype(jnp.float32)
        middle = rest.astype(jnp.bfloat16)
        bottom = (rest - middle.astype(jnp.float32)).astype(jnp.bfloat16)
        lines = jnp.concatenate([top, middle, bottom], axis=0)
        count = slots * rows
        pitch = count + BLK
        from_lane = lax.broadcasted_iota(jnp.int32, (LANES, LANES), 0)
        to_lane = lax.broadcasted_iota(jnp.int32, (LANES, LANES), 1)
        same = from_lane % BLK == to_lane % BLK
        for m in range(2 * BLK):
            spread = jnp.where(same & (from_lane // BLK == m), 1.0, 0.0).astype(jnp.bfloat16)
            parts = jnp.dot(lines, spread, preferred_element_type=jnp.float32)
            result[m * pitch : m * pitch + count, :] = parts[:count] + parts[count : 2 * count] + parts[2 * count :]
        copy.wait()
        lane = lax.broadcasted_iota(jnp.int32, (BLK, LANES), 1)
        per_y, per_z = len_y // BLK, len_z // BLK
        for j in range(slots):
            target = plan[slots * depth + j, 0].astype(jnp.int32)

            @pl.when(target >= 0)
            def _():
                block_x = target // (per_y * per_z)
                block_y = target // per_z % per_y
                z_from = target % per_z * BLK
                inside = (lane >= z_from) & (lane < z_from + BLK)
                first = block_x * BLK * len_y + block_y * BLK
                for a in range(BLK):
                    spots = [
                        pl.ds(pl.multiple_of(first + c * plane + a * len_y, BLK), BLK) for c in range(ncomp)
                    ]
                    row = a % 2 * BLK * pitch + j * rows + a // 2 * ncomp
                    old = [filled[spot, :] for spot in spots]
                    new = [result[pl.ds(row + c, BLK, stride=pitch), :] for c in range(ncomp)]
                    for spot, before, after in zip(spots, old, new):
                        filled[spot, :] = jnp.where(inside, after, before)

    def faces(x_low, x_high, y_low, y_high):
        for c in range(ncomp):
            x_low[c * len_y : (c + 1) * len_y, :] = filled[c * plane : c * plane + len_y, :]
            x_high[c * len_y : (c + 1) * len_y, :] = filled[(c + 1) * plane - len_y : (c + 1) * plane, :]
            y_low[c * len_x : (c + 1) * len_x, :] = filled[pl.ds(c * plane, len_x, stride=len_y), :]
            y_high[c * len_x : (c + 1) * len_x, :] = filled[
                pl.ds(c * plane + len_y - 1, len_x, stride=len_y), :
            ]

    @pl.when(helio)
    def _():
        faces(x_two, x_one, y_two, y_one)

    @pl.when(jnp.logical_not(helio))
    def _():
        faces(x_one, x_two, y_one, y_two)


def primitives(cells):
    density, energy = cells[0], cells[7]
    momentum, magnetic = cells[1:4], cells[4:7]
    inverse = 1.0 / density
    velocity = [m * inverse for m in momentum]
    field_sq = magnetic[0] * magnetic[0] + magnetic[1] * magnetic[1] + magnetic[2] * magnetic[2]
    kinetic = momentum[0] * velocity[0] + momentum[1] * velocity[1] + momentum[2] * velocity[2]
    pressure = (HEAT_RATIO - 1.0) * (energy - 0.5 * kinetic - 0.5 * field_sq)
    total_pressure = pressure + 0.5 * field_sq
    dot = velocity[0] * magnetic[0] + velocity[1] * magnetic[1] + velocity[2] * magnetic[2]
    fast = jnp.sqrt((HEAT_RATIO * pressure + field_sq) * inverse)
    return velocity, total_pressure, energy + total_pressure, dot, fast


def flux_of(cells, prims, direction):
    velocity, total_pressure, enthalpy, dot, fast = prims
    momentum, magnetic = cells[1:4], cells[4:7]
    speed, field = velocity[direction], magnetic[direction]
    flux = [momentum[direction]]
    for other in range(3):
        term = momentum[other] * speed - magnetic[other] * field
        flux.append(term + total_pressure if other == direction else term)
    for other in range(3):
        if other == direction:
            flux.append(None)
        else:
            flux.append(speed * magnetic[other] - field * velocity[other])
    flux.append(enthalpy * speed - field * dot)
    return flux, jnp.abs(speed) + fast


def face_sum(low, high):
    fastest = jnp.maximum(low[2], high[2])
    out = []
    for u_low, u_high, f_low, f_high in zip(low[0], high[0], low[1], high[1]):
        face = fastest * (u_high - u_low)
        out.append(face if f_low is None else face - (f_low + f_high))
    return out


def inner_kernel(dims, filled, out, rim_x_low, rim_x_high, rim_y_low, rim_y_high, part, sems):
    ncomp, len_x, len_y, len_z = dims
    plane = len_x * len_y
    half_ratio = jnp.where(lax.axis_index("dom") == 0, 0.5 * CORONA_RATIO, 0.5 * HELIO_RATIO).astype(jnp.float32)
    shape = (len_y, LANES)
    row = lax.broadcasted_iota(jnp.int32, shape, 0)
    lane = lax.broadcasted_iota(jnp.int32, shape, 1)

    def load(x):
        return [filled[pl.ds(pl.multiple_of(c * plane + x * len_y, BLK), len_y), :] for c in range(ncomp)]

    def shift_up(values, axis, size):
        return [None if v is None else pltpu.roll(v, size - 1, axis) for v in values]

    def step(x, carry, last):
        cells, prims, flux_x, speed_x, low_x = carry
        if last:
            high_x = [jnp.zeros(shape, jnp.float32)] * ncomp
            next_carry = None
        else:
            next_cells = load(x + 1)
            next_prims = primitives(next_cells)
            next_flux, next_speed = flux_of(next_cells, next_prims, 0)
            high_x = face_sum((cells, flux_x, speed_x), (next_cells, next_flux, next_speed))
            next_carry = (next_cells, next_prims, next_flux, next_speed, high_x)
        total = [high - low for high, low in zip(high_x, low_x)]
        flux, speed = flux_of(cells, prims, 1)
        beside = (shift_up(cells, 0, len_y), shift_up(flux, 0, len_y), pltpu.roll(speed, len_y - 1, 0))
        for c, face in enumerate(face_sum((cells, flux, speed), beside)):
            face = jnp.where(row == len_y - 1, 0.0, face)
            total[c] = total[c] + (face - pltpu.roll(face, 1, 0))
        flux, speed = flux_of(cells, prims, 2)
        beside = (shift_up(cells, 1, LANES), shift_up(flux, 1, LANES), pltpu.roll(speed, LANES - 1, 1))
        for c, face in enumerate(face_sum((cells, flux, speed), beside)):
            own = jnp.zeros(shape, jnp.float32) if flux[c] is None else -2.0 * flux[c]
            face = jnp.where(lane == LANES - 1, own, face)
            below = jnp.where(lane == 0, own, pltpu.roll(face, 1, 1))
            total[c] = total[c] + (face - below)
        for c in range(ncomp):
            part[c, x] = cells[c] + half_ratio * total[c]
        return next_carry

    def line_copy(x):
        return pltpu.make_async_copy(part.at[:, x], out.at[:, x], sems.at[x])

    cells = load(0)
    prims = primitives(cells)
    flux, speed = flux_of(cells, prims, 0)
    flux[4] = None
    zero = [jnp.zeros(shape, jnp.float32)] * ncomp
    carry = (cells, prims, flux, speed, zero)

    def pack(carry):
        cells, prims, flux, speed, low = carry
        return cells, prims, [f for f in flux if f is not None], speed, low

    def unpack(carry):
        cells, prims, flux, speed, low = carry
        return cells, prims, flux[:4] + [None] + flux[4:], speed, low

    def line(x, carry):
        carry = pack(step(x, unpack(carry), False))

        @pl.when(x > 0)
        def _():
            line_copy(x).start()

        return carry

    carry = lax.fori_loop(0, len_x - 1, line, pack(carry), unroll=3)
    step(len_x - 1, unpack(carry), True)
    for c in range(ncomp):
        rim_x_low[c] = part[c, 0]
        rim_x_high[c] = part[c, len_x - 1]
        rim_y_low[c] = part[c, :, 0, :]
        rim_y_high[c] = part[c, :, len_y - 1, :]
    for x in range(1, len_x - 1):
        line_copy(x).wait()


def edge_kernel(dims, part, rim_x_low, rim_x_high, rim_y_low, rim_y_high, *rest):
    ncomp, len_x, len_y, len_z = dims
    y_one, y_two, x_one, x_two, from_y_one, from_y_two, from_x_one, from_x_two, wrap = rest[:9]
    out, row_x_low, row_x_high, row_y_low, row_y_high, sems = rest[9:]
    helio = lax.axis_index("dom") == 1
    half_ratio = jnp.where(helio, 0.5 * HELIO_RATIO, 0.5 * CORONA_RATIO).astype(jnp.float32)

    def state(cells, direction):
        flux, speed = flux_of(cells, primitives(cells), direction)
        return cells, flux, speed

    def faces(own_ref, other_ref, end, end_ref, direction, upper, size):
        own = [own_ref[c * size : (c + 1) * size, :] for c in range(ncomp)]
        other = [other_ref[c * size : (c + 1) * size, :] for c in range(ncomp)]
        at_end = own if end_ref is None else [end_ref[c * size : (c + 1) * size, :] for c in range(ncomp)]
        other = [jnp.where(end, u, v) for u, v in zip(at_end, other)]
        own, other = state(own, direction), state(other, direction)
        if upper:
            return [half_ratio * f for f in face_sum(own, other)]
        return [-half_ratio * f for f in face_sum(other, own)]

    def both(x_low, x_high, y_low, y_high, from_x_low, from_x_high, from_y_low, from_y_high, x_end):
        column, line = lax.axis_index("gx"), lax.axis_index("yz")
        low_end, high_end = line == 0, line == lax.axis_size("yz") - 1
        y_lows = faces(y_low, from_y_low, low_end, None, 1, False, len_x)
        y_highs = faces(y_high, from_y_high, high_end, None, 1, True, len_x)
        for c in range(ncomp):
            row_y_low[c] = (rim_y_low[c] + y_lows[c])[1 : len_x - 1]
            row_y_high[c] = (rim_y_high[c] + y_highs[c])[1 : len_x - 1]
        inner_x = pl.ds(1, len_x - 2)
        copies = [
            pltpu.make_async_copy(row_y_low, out.at[:, inner_x, 0], sems.at[0]),
            pltpu.make_async_copy(row_y_high, out.at[:, inner_x, len_y - 1], sems.at[1]),
        ]
        copies[0].start()
        copies[1].start()
        low_end, high_end = column == 0, column == lax.axis_size("gx") - 1
        x_lows = faces(x_low, from_x_low, low_end, x_end, 0, False, len_y)
        x_highs = faces(x_high, from_x_high, high_end, x_end, 0, True, len_y)
        for row, rim, changes, x, sem in (
            (row_x_low, rim_x_low, x_lows, 0, 2),
            (row_x_high, rim_x_high, x_highs, len_x - 1, 3),
        ):
            for c in range(ncomp):
                row[c] = rim[c] + changes[c]
                row[c, 0:1] = row[c, 0:1] + y_lows[c][x : x + 1]
                row[c, len_y - 1 : len_y] = row[c, len_y - 1 : len_y] + y_highs[c][x : x + 1]
            copies.append(pltpu.make_async_copy(row, out.at[:, x], sems.at[sem]))
            copies[-1].start()
        for copy in copies:
            copy.wait()

    @pl.when(helio)
    def _():
        both(x_two, x_one, y_two, y_one, from_x_one, from_x_two, from_y_one, from_y_two, None)

    @pl.when(jnp.logical_not(helio))
    def _():
        both(x_one, x_two, y_one, y_two, from_x_two, from_x_one, from_y_two, from_y_one, wrap)


def local(field_state, shell_owner, block_sources, block_targets, interp_weights):
    _, ncomp, len_x, len_y, len_z = field_state.shape
    n_gx, n_yz = lax.axis_size("gx"), lax.axis_size("yz")
    shells = shell_owner.shape[2]
    slots, depth = block_sources.shape[2:]
    volume = BLK * BLK * BLK
    cell_rows = ncomp * len_x * len_y
    grid = field_state.reshape(ncomp, len_x * len_y, len_z)
    weights = interp_weights.reshape(slots * depth, volume, volume)
    rows = BLK // 2 * ncomp
    dims = (ncomp, len_x, len_y, len_z)

    plan_rows = -(-slots * (depth + 1) // BLK) * BLK
    face_x = jax.ShapeDtypeStruct((ncomp * len_y, len_z), jnp.float32)
    face_y = jax.ShapeDtypeStruct((ncomp * len_x, len_z), jnp.float32)
    plane = len_x * len_y
    carried_planes = max(ncomp + 1, 16 * MIB // (4 * LANES * plane))
    *packed, carried, wrap = pl.pallas_call(
        functools.partial(pack_kernel, dims + (n_yz, shells, slots, depth)),
        out_shape=[jax.ShapeDtypeStruct((CAP, rows, LANES), jnp.bfloat16)] * n_yz
        + [
            jax.ShapeDtypeStruct((carried_planes, plane, len_z), jnp.float32),
            jax.ShapeDtypeStruct((ncomp, len_y, len_z), jnp.float32),
        ],
        in_specs=[HB] * 4,
        out_specs=[HB] * (n_yz + 2),
        scratch_shapes=[
            pltpu.VMEM((ncomp, plane + BLK, len_z), jnp.float32),
            pltpu.SMEM(shell_owner.shape, jnp.int32),
            pltpu.SMEM(block_sources.shape, jnp.int32),
            pltpu.SMEM(block_targets.shape, jnp.int32),
            pltpu.SMEM((n_yz * CAP + 1,), jnp.int32),
            pltpu.VMEM((plan_rows, LANES), jnp.float32),
            pltpu.VMEM((2 * BLK * LANES, SR * LANES), jnp.bfloat16),
            pltpu.VMEM((n_yz * CAP, rows, LANES), jnp.bfloat16),
            pltpu.SemaphoreType.DMA((2 * (len_x // BLK) + 5 + n_yz,)),
        ],
        compiler_params=pltpu.CompilerParams(vmem_limit_bytes=VMEM_BYTES - 8 * MIB),
        name="pack_shell",
    )(shell_owner, block_sources, block_targets, grid)

    moved = []
    for step in range(n_yz):
        pairs = [(t, n_yz + partner(t, step, n_yz)) for t in range(n_yz)]
        pairs = pairs + [(b, a) for a, b in pairs]
        moved.append(lax.ppermute(packed[step], ("dom", "yz"), pairs))

    staged = [
        jax.ShapeDtypeStruct(weights.shape, weights.dtype),
        jax.ShapeDtypeStruct((ncomp, plane, len_z), jnp.float32),
        jax.ShapeDtypeStruct((plan_rows, LANES), jnp.float32),
    ]
    staged_bytes = sum(x.size * x.dtype.itemsize for x in staged)
    room = pltpu.CompilerParams(vmem_limit_bytes=VMEM_BYTES - 17 * staged_bytes // 4)
    early_grid, wrap = pl.pallas_call(
        early_kernel,
        out_shape=[staged[1], jax.ShapeDtypeStruct(wrap.shape, wrap.dtype)],
        in_specs=[HB] * 2,
        out_specs=[VM, HB],
        scratch_shapes=[pltpu.SemaphoreType.DMA],
        input_output_aliases={1: 1},
        compiler_params=room,
        name="early_grid",
    )(carried, wrap)
    wrap = lax.ppermute(wrap, ("dom", "gx", "yz"), wrap_pairs(n_gx, n_yz))
    grid, plan = pl.pallas_call(
        stage_kernel,
        out_shape=staged[1:],
        in_specs=[HB] * 1,
        out_specs=[VM] * 2,
        scratch_shapes=[pltpu.SemaphoreType.DMA((2,))],
        compiler_params=room,
        cost_estimate=pl.CostEstimate(flops=0, bytes_accessed=4 * interp_weights.size, transcendentals=0),
        name="stage_operands",
    )(carried)

    filled, y_one, y_two, x_one, x_two = pl.pallas_call(
        functools.partial(fill_kernel, dims + (n_yz, slots, depth)),
        out_shape=[jax.ShapeDtypeStruct((cell_rows, len_z), jnp.float32), face_y, face_y, face_x, face_x],
        in_specs=[VM] * (4 + n_yz),
        out_specs=[VM] * 5,
        scratch_shapes=[
            pltpu.VMEM((2 * BLK * (slots * rows + BLK), LANES), jnp.float32),
            pltpu.SMEM((plan_rows, LANES), jnp.float32),
            pltpu.SemaphoreType.DMA,
        ],
        input_output_aliases={2: 0},
        compiler_params=pltpu.CompilerParams(vmem_limit_bytes=16 * MIB),
        name="fill_blocks",
    )(plan, weights, grid.reshape(cell_rows, len_z), early_grid.reshape(cell_rows, len_z), *moved[::-1])

    once_x, once_y = cycle(n_gx), cycle(n_yz)
    from_y_one = lax.ppermute(y_one, ("dom", "yz"), once_y)
    from_y_two = lax.ppermute(y_two, ("dom", "yz"), [(b, a) for a, b in once_y])
    from_x_one = lax.ppermute(x_one, ("dom", "gx"), once_x)
    from_x_two = lax.ppermute(x_two, ("dom", "gx"), [(b, a) for a, b in once_x])

    whole = jax.ShapeDtypeStruct((ncomp, len_x, len_y, len_z), jnp.float32)
    rim_x = jax.ShapeDtypeStruct((ncomp, len_y, len_z), jnp.float32)
    rim_y = jax.ShapeDtypeStruct((ncomp, len_x, len_z), jnp.float32)
    part, *rims = pl.pallas_call(
        functools.partial(inner_kernel, dims),
        out_shape=[whole, rim_x, rim_x, rim_y, rim_y],
        in_specs=[VM],
        out_specs=[HB] + [VM] * 4,
        scratch_shapes=[
            pltpu.VMEM((ncomp, len_x, len_y, len_z), jnp.float32),
            pltpu.SemaphoreType.DMA((len_x,)),
        ],
        compiler_params=pltpu.CompilerParams(vmem_limit_bytes=8 * MIB),
        cost_estimate=pl.CostEstimate(
            flops=300 * cell_rows * len_z, bytes_accessed=8 * cell_rows * len_z, transcendentals=0
        ),
        name="inner_faces",
    )(filled)

    updated = pl.pallas_call(
        functools.partial(edge_kernel, dims),
        out_shape=whole,
        in_specs=[HB] + [VM] * 13,
        out_specs=HB,
        scratch_shapes=[
            pltpu.VMEM((ncomp, len_y, len_z), jnp.float32),
            pltpu.VMEM((ncomp, len_y, len_z), jnp.float32),
            pltpu.VMEM((ncomp, len_x - 2, len_z), jnp.float32),
            pltpu.VMEM((ncomp, len_x - 2, len_z), jnp.float32),
            pltpu.SemaphoreType.DMA((4,)),
        ],
        input_output_aliases={0: 0},
        compiler_params=pltpu.CompilerParams(vmem_limit_bytes=8 * MIB),
        name="edge_faces",
    )(part, *rims, y_one, y_two, x_one, x_two, from_y_one, from_y_two, from_x_one, from_x_two, wrap.reshape(ncomp * len_y, len_z))
    return updated.reshape(1, ncomp, len_x, len_y, len_z)


def solution(mesh):
    placed = (
        P("dom", None, "gx", "yz", None),
        P("gx", None, None),
        P("gx", "yz", None, None),
        P("gx", "yz", None),
        P("gx", "yz", None, None, None, None),
    )
    return jax.shard_map(
        local,
        mesh=mesh,
        in_specs=placed,
        out_specs=P("dom", None, "gx", "yz", None),
        check_vma=False,
    )
```

```python
import functools

import jax
import jax.numpy as jnp
from jax import lax
from jax.experimental import pallas as pl
from jax.experimental.pallas import tpu as pltpu
from jax.sharding import PartitionSpec as P

BLK = 8
SR = 2
CAP = 2
LANES = 128
MIB = 2**20
VMEM_BYTES = 64 * MIB

HEAT_RATIO = 5.0 / 3.0
CORONA_RATIO = 0.04
HELIO_RATIO = 0.03

VM = pl.BlockSpec(memory_space=pltpu.VMEM)
HB = pl.BlockSpec(memory_space=pltpu.HBM)


def partner(index, step, count):
    if count & (count - 1) == 0:
        return index ^ step
    return (index + step) % count


def cycle(count):
    pairs = [(count + i, count + i + 1) for i in range(count - 1)] + [(2 * count - 1, count - 1)]
    return pairs + [(i + 1, i) for i in range(count - 1)] + [(0, count)]


def wrap_pairs(count, lines):
    def index(domain, column, line):
        return (domain * count + column) * lines + line

    pairs = []
    for t in range(lines):
        pairs.append((index(0, 0, t), index(0, count - 1, t)))
        pairs += [(index(0, g, t), index(1, g, t)) for g in range(1, count - 1)]
    pairs += [(index(1, g, t), index(1, g, t + 1)) for g in (0, count - 1) for t in range(0, lines - 1, 2)]
    return pairs + [(b, a) for a, b in pairs]


def pack_kernel(dims, owner_hbm, source_hbm, target_hbm, grid_hbm, *rest):
    ncomp, len_x, len_y, len_z, n_yz, shells, slots, depth = dims
    outs, carried, wrap = rest[:n_yz], rest[n_yz], rest[n_yz + 1]
    grid_ref, owner_ref, source_ref, target_ref, table, plan, spread, send, sems = rest[n_yz + 2 :]
    me = lax.axis_index("yz")
    plane = len_x * len_y
    n_bx, n_by, half = len_x // BLK, len_y // BLK, BLK // 2
    pitch = grid_ref.shape[1]
    flat = grid_ref.reshape(ncomp * pitch, len_z)
    onto = carried.at[pl.ds(0, ncomp)]
    slabs = [pl.ds(bx * BLK * len_y, BLK * len_y) for bx in range(n_bx)]
    grid_copies = [
        pltpu.make_async_copy(grid_hbm.at[:, slab, :], grid_ref.at[:, slab, :], sems.at[bx]) for bx, slab in enumerate(slabs)
    ]
    onward = [
        pltpu.make_async_copy(grid_ref.at[:, slab, :], onto.at[:, slab, :], sems.at[n_bx + bx])
        for bx, slab in enumerate(slabs)
    ]
    end = jnp.where(lax.axis_index("gx") == 0, 0, plane - len_y)
    first_sem = 2 * n_bx + 1
    wrap_copy = pltpu.make_async_copy(
        grid_ref.at[:, pl.ds(pl.multiple_of(end, BLK), len_y), :], wrap, sems.at[2 * n_bx]
    )
    copies = [
        pltpu.make_async_copy(owner_hbm, owner_ref, sems.at[first_sem]),
        pltpu.make_async_copy(source_hbm, source_ref, sems.at[first_sem + 1]),
        pltpu.make_async_copy(target_hbm, target_ref, sems.at[first_sem + 2]),
    ]

    @pl.when(lax.axis_index("dom") == 1)
    def _():
        for copy in copies:
            copy.start()
        for copy in grid_copies:
            copy.start()
        for copy in copies:
            copy.wait()
        position = jnp.int32(0)
        for t in range(n_yz):
            if n_yz & (n_yz - 1) == 0:
                step = t ^ me
            else:
                step = lax.rem(me - t + n_yz, n_yz)
            rank = jnp.int32(0)
            for b in range(shells):
                table[jnp.minimum(position, n_yz * CAP)] = step * CAP + jnp.minimum(rank, CAP - 1)
                mine = jnp.where(owner_ref[0, t, b] == me, 1, 0)
                position = position + mine
                rank = rank + mine
        for j in range(slots):
            for k in range(depth):
                entry = source_ref[0, 0, j, k]
                spot = jnp.where(entry >= 0, table[jnp.clip(entry, 0, n_yz * CAP)], -1)
                plan[j * depth + k : j * depth + k + 1, :] = jnp.full((1, LANES), spot.astype(jnp.float32))
            plan[slots * depth + j : slots * depth + j + 1, :] = jnp.full(
                (1, LANES), target_ref[0, 0, j].astype(jnp.float32)
            )
        told = pltpu.make_async_copy(plan, carried.at[ncomp, pl.ds(0, plan.shape[0])], sems.at[first_sem + 3])
        told.start()
        for arriving, leaving in zip(grid_copies, onward):
            arriving.wait()
            leaving.start()
        told.wait()
        for copy in onward:
            copy.wait()

    @pl.when(lax.axis_index("dom") == 0)
    def _():
        copies[0].start()
        for copy in grid_copies:
            copy.start()
        z_from = len_z - SR * BLK
        row_z = lax.broadcasted_iota(jnp.int32, (LANES, SR * LANES), 0) + (len_z - LANES)
        column = lax.broadcasted_iota(jnp.int32, (LANES, SR * LANES), 1)
        hit = row_z == z_from + column // LANES * BLK + column % BLK
        place = jnp.where(hit, column % LANES // BLK, -1)
        for m in range(2 * BLK):
            spread[m * LANES : (m + 1) * LANES, :] = jnp.where(place == m, 1.0, 0.0).astype(jnp.bfloat16)
        send[...] = jnp.zeros_like(send)
        copies[0].wait()
        spots = []
        for b in range(shells):
            owner = owner_ref[0, me, b]
            rank = jnp.int32(0)
            for other in range(b):
                rank = rank + jnp.where(owner_ref[0, me, other] == owner, 1, 0)
            if n_yz & (n_yz - 1) == 0:
                step = owner ^ me
            else:
                step = lax.rem(owner - me + n_yz, n_yz)
            spots.append(jnp.clip(step * CAP + rank, 0, n_yz * CAP - 1))
        rows = half * ncomp
        lines = []
        for bx in range(n_bx):
            grid_copies[bx].wait()
            onward[bx].start()
            line = []
            for ap in range(2):
                for cy in range(BLK):
                    pieces = []
                    for by in range(n_by):
                        for a2 in range(half):
                            first = (bx * BLK + a2 * 2 + ap) * len_y + by * BLK + cy
                            pieces.append(flat[pl.ds(first, ncomp, stride=pitch), :])
                    line.append(jnp.concatenate(pieces, axis=0).astype(jnp.bfloat16))
            lines.append(jnp.concatenate(line, axis=1))
        wrap_copy.start()
        total = jnp.dot(jnp.concatenate(lines, axis=0), spread[...], preferred_element_type=jnp.float32)
        total = total.astype(jnp.bfloat16)
        for b in range(shells):
            column_block, br = b // SR, b % SR
            send[spots[b]] = total[
                column_block * rows : (column_block + 1) * rows, br * LANES : (br + 1) * LANES
            ]
        sends = [
            pltpu.make_async_copy(send.at[pl.ds(step * CAP, CAP)], outs[step], sems.at[first_sem + 4 + step])
            for step in range(n_yz)
        ]
        for copy in sends:
            copy.start()
        for copy in [wrap_copy] + onward + sends:
            copy.wait()


def early(size):
    return (lax.axis_index("dom") == 0) & (lax.axis_index("gx") < size)


def early_kernel(carried, wrap_in, grid_ref, wrap_out, sem):
    @pl.when(early(1))
    def _():
        copy = pltpu.make_async_copy(carried.at[pl.ds(0, grid_ref.shape[0])], grid_ref, sem)
        copy.start()
        copy.wait()


def stage_kernel(carried, grid_ref, plan_ref, sems):
    ncomp, plan_rows = grid_ref.shape[0], plan_ref.shape[0]
    grid_copy = pltpu.make_async_copy(carried.at[pl.ds(0, ncomp)], grid_ref, sems.at[0])
    copies = [pltpu.make_async_copy(carried.at[ncomp, pl.ds(0, plan_rows)], plan_ref, sems.at[1]), grid_copy]

    @pl.when(lax.axis_index("dom") == 1)
    def _():
        for copy in copies:
            copy.start()
        for copy in copies:
            copy.wait()

    @pl.when((lax.axis_index("dom") == 0) & jnp.logical_not(early(1)))
    def _():
        grid_copy.start()
        grid_copy.wait()


def fill_kernel(dims, plan_vmem, weight_ref, grid_ref, early_ref, *rest):
    ncomp, len_x, len_y, len_z, n_yz, slots, depth = dims
    got = rest[:n_yz]
    filled, y_one, y_two, x_one, x_two, result, plan, sem = rest[n_yz:]
    half = BLK // 2
    rows = half * ncomp
    plane = len_x * len_y

    helio = lax.axis_index("dom") == 1
    ahead = early(1)

    @pl.when(ahead)
    def _():
        filled[...] = early_ref[...]

    @pl.when(jnp.logical_not(ahead | helio))
    def _():
        filled[...] = grid_ref[...]

    @pl.when(helio)
    def _():
        copy = pltpu.make_async_copy(plan_vmem, plan, sem)
        copy.start()
        held = [
            got[step][slot].astype(jnp.float32)
            for step in range(n_yz)
            for slot in range(CAP)
        ]
        lines = []
        for j in range(slots):
            sources = []
            for k in range(depth):
                entry = j * depth + k
                spot = jnp.broadcast_to(plan_vmem[entry : entry + 1, :], (rows, LANES))
                block = jnp.zeros((rows, LANES), jnp.float32)
                for place, candidate in enumerate(held):
                    block = jnp.where(spot == float(place), candidate, block)
                sources += [block[a2 * ncomp : (a2 + 1) * ncomp, :] for a2 in range(half)]
            cells = jnp.concatenate(sources, axis=1).astype(jnp.bfloat16)
            dense = weight_ref[j * depth : (j + 1) * depth].reshape(depth * weight_ref.shape[1], weight_ref.shape[2])
            total = jnp.dot(cells, dense, preferred_element_type=jnp.float32)
            lines += [total[:, a2 * LANES : (a2 + 1) * LANES] for a2 in range(half)]
        lines = jnp.concatenate(lines, axis=0)
        top = lines.astype(jnp.bfloat16)
        rest = lines - top.astype(jnp.float32)
        middle = rest.astype(jnp.bfloat16)
        bottom = (rest - middle.astype(jnp.float32)).astype(jnp.bfloat16)
        lines = jnp.concatenate([top, middle, bottom], axis=0)
        count = slots * rows
        pitch = count + BLK
        from_lane = lax.broadcasted_iota(jnp.int32, (LANES, LANES), 0)
        to_lane = lax.broadcasted_iota(jnp.int32, (LANES, LANES), 1)
        same = from_lane % BLK == to_lane % BLK
        for m in range(2 * BLK):
            spread = jnp.where(same & (from_lane // BLK == m), 1.0, 0.0).astype(jnp.bfloat16)
            parts = jnp.dot(lines, spread, preferred_element_type=jnp.float32)
            result[m * pitch : m * pitch + count, :] = parts[:count] + parts[count : 2 * count] + parts[2 * count :]
        filled[...] = grid_ref[...]
        copy.wait()
        lane = lax.broadcasted_iota(jnp.int32, (BLK, LANES), 1)
        per_y, per_z = len_y // BLK, len_z // BLK
        for j in range(slots):
            target = plan[slots * depth + j, 0].astype(jnp.int32)

            @pl.when(target >= 0)
            def _():
                block_x = target // (per_y * per_z)
                block_y = target // per_z % per_y
                z_from = target % per_z * BLK
                inside = (lane >= z_from) & (lane < z_from + BLK)
                first = block_x * BLK * len_y + block_y * BLK
                for a in range(BLK):
                    spots = [
                        pl.ds(pl.multiple_of(first + c * plane + a * len_y, BLK), BLK) for c in range(ncomp)
                    ]
                    row = a % 2 * BLK * pitch + j * rows + a // 2 * ncomp
                    old = [filled[spot, :] for spot in spots]
                    new = [result[pl.ds(row + c, BLK, stride=pitch), :] for c in range(ncomp)]
                    for spot, before, after in zip(spots, old, new):
                        filled[spot, :] = jnp.where(inside, after, before)

    def faces(x_low, x_high, y_low, y_high):
        for c in range(ncomp):
            x_low[c * len_y : (c + 1) * len_y, :] = filled[c * plane : c * plane + len_y, :]
            x_high[c * len_y : (c + 1) * len_y, :] = filled[(c + 1) * plane - len_y : (c + 1) * plane, :]
            y_low[c * len_x : (c + 1) * len_x, :] = filled[pl.ds(c * plane, len_x, stride=len_y), :]
            y_high[c * len_x : (c + 1) * len_x, :] = filled[
                pl.ds(c * plane + len_y - 1, len_x, stride=len_y), :
            ]

    @pl.when(helio)
    def _():
        faces(x_two, x_one, y_two, y_one)

    @pl.when(jnp.logical_not(helio))
    def _():
        faces(x_one, x_two, y_one, y_two)


def primitives(cells):
    density, energy = cells[0], cells[7]
    momentum, magnetic = cells[1:4], cells[4:7]
    inverse = 1.0 / density
    velocity = [m * inverse for m in momentum]
    field_sq = magnetic[0] * magnetic[0] + magnetic[1] * magnetic[1] + magnetic[2] * magnetic[2]
    kinetic = momentum[0] * velocity[0] + momentum[1] * velocity[1] + momentum[2] * velocity[2]
    pressure = (HEAT_RATIO - 1.0) * (energy - 0.5 * kinetic - 0.5 * field_sq)
    total_pressure = pressure + 0.5 * field_sq
    dot = velocity[0] * magnetic[0] + velocity[1] * magnetic[1] + velocity[2] * magnetic[2]
    fast = jnp.sqrt((HEAT_RATIO * pressure + field_sq) * inverse)
    return velocity, total_pressure, energy + total_pressure, dot, fast


def flux_of(cells, prims, direction):
    velocity, total_pressure, enthalpy, dot, fast = prims
    momentum, magnetic = cells[1:4], cells[4:7]
    speed, field = velocity[direction], magnetic[direction]
    flux = [momentum[direction]]
    for other in range(3):
        term = momentum[other] * speed - magnetic[other] * field
        flux.append(term + total_pressure if other == direction else term)
    for other in range(3):
        if other == direction:
            flux.append(None)
        else:
            flux.append(speed * magnetic[other] - field * velocity[other])
    flux.append(enthalpy * speed - field * dot)
    return flux, jnp.abs(speed) + fast


def face_sum(low, high):
    fastest = jnp.maximum(low[2], high[2])
    out = []
    for u_low, u_high, f_low, f_high in zip(low[0], high[0], low[1], high[1]):
        face = fastest * (u_high - u_low)
        out.append(face if f_low is None else face - (f_low + f_high))
    return out


def inner_kernel(dims, filled, out, rim_x_low, rim_x_high, rim_y_low, rim_y_high, part, sems):
    ncomp, len_x, len_y, len_z = dims
    plane = len_x * len_y
    half_ratio = jnp.where(lax.axis_index("dom") == 0, 0.5 * CORONA_RATIO, 0.5 * HELIO_RATIO).astype(jnp.float32)
    shape = (len_y, LANES)
    row = lax.broadcasted_iota(jnp.int32, shape, 0)
    lane = lax.broadcasted_iota(jnp.int32, shape, 1)

    def load(x):
        return [filled[pl.ds(pl.multiple_of(c * plane + x * len_y, BLK), len_y), :] for c in range(ncomp)]

    def shift_up(values, axis, size):
        return [None if v is None else pltpu.roll(v, size - 1, axis) for v in values]

    def step(x, carry, last):
        cells, prims, flux_x, speed_x, low_x = carry
        if last:
            high_x = [jnp.zeros(shape, jnp.float32)] * ncomp
            next_carry = None
        else:
            next_cells = load(x + 1)
            next_prims = primitives(next_cells)
            next_flux, next_speed = flux_of(next_cells, next_prims, 0)
            high_x = face_sum((cells, flux_x, speed_x), (next_cells, next_flux, next_speed))
            next_carry = (next_cells, next_prims, next_flux, next_speed, high_x)
        total = [high - low for high, low in zip(high_x, low_x)]
        flux, speed = flux_of(cells, prims, 1)
        beside = (shift_up(cells, 0, len_y), shift_up(flux, 0, len_y), pltpu.roll(speed, len_y - 1, 0))
        for c, face in enumerate(face_sum((cells, flux, speed), beside)):
            face = jnp.where(row == len_y - 1, 0.0, face)
            total[c] = total[c] + (face - pltpu.roll(face, 1, 0))
        flux, speed = flux_of(cells, prims, 2)
        beside = (shift_up(cells, 1, LANES), shift_up(flux, 1, LANES), pltpu.roll(speed, LANES - 1, 1))
        for c, face in enumerate(face_sum((cells, flux, speed), beside)):
            own = jnp.zeros(shape, jnp.float32) if flux[c] is None else -2.0 * flux[c]
            face = jnp.where(lane == LANES - 1, own, face)
            below = jnp.where(lane == 0, own, pltpu.roll(face, 1, 1))
            total[c] = total[c] + (face - below)
        for c in range(ncomp):
            part[c, x] = cells[c] + half_ratio * total[c]
        return next_carry

    def line_copy(x):
        return pltpu.make_async_copy(part.at[:, x], out.at[:, x], sems.at[x])

    cells = load(0)
    prims = primitives(cells)
    flux, speed = flux_of(cells, prims, 0)
    flux[4] = None
    zero = [jnp.zeros(shape, jnp.float32)] * ncomp
    carry = (cells, prims, flux, speed, zero)

    def pack(carry):
        cells, prims, flux, speed, low = carry
        return cells, prims, [f for f in flux if f is not None], speed, low

    def unpack(carry):
        cells, prims, flux, speed, low = carry
        return cells, prims, flux[:4] + [None] + flux[4:], speed, low

    def line(x, carry):
        carry = pack(step(x, unpack(carry), False))

        @pl.when(x > 0)
        def _():
            line_copy(x).start()

        return carry

    carry = lax.fori_loop(0, len_x - 1, line, pack(carry), unroll=3)
    step(len_x - 1, unpack(carry), True)
    for c in range(ncomp):
        rim_x_low[c] = part[c, 0]
        rim_x_high[c] = part[c, len_x - 1]
        rim_y_low[c] = part[c, :, 0, :]
        rim_y_high[c] = part[c, :, len_y - 1, :]
    for x in range(1, len_x - 1):
        line_copy(x).wait()


def edge_kernel(dims, part, rim_x_low, rim_x_high, rim_y_low, rim_y_high, *rest):
    ncomp, len_x, len_y, len_z = dims
    y_one, y_two, x_one, x_two, from_y_one, from_y_two, from_x_one, from_x_two, wrap = rest[:9]
    out, row_x_low, row_x_high, row_y_low, row_y_high, sems = rest[9:]
    helio = lax.axis_index("dom") == 1
    half_ratio = jnp.where(helio, 0.5 * HELIO_RATIO, 0.5 * CORONA_RATIO).astype(jnp.float32)

    def state(cells, direction):
        flux, speed = flux_of(cells, primitives(cells), direction)
        return cells, flux, speed

    def faces(own_ref, other_ref, end, end_ref, direction, upper, size):
        own = [own_ref[c * size : (c + 1) * size, :] for c in range(ncomp)]
        other = [other_ref[c * size : (c + 1) * size, :] for c in range(ncomp)]
        at_end = own if end_ref is None else [end_ref[c * size : (c + 1) * size, :] for c in range(ncomp)]
        other = [jnp.where(end, u, v) for u, v in zip(at_end, other)]
        own, other = state(own, direction), state(other, direction)
        if upper:
            return [half_ratio * f for f in face_sum(own, other)]
        return [-half_ratio * f for f in face_sum(other, own)]

    def both(x_low, x_high, y_low, y_high, from_x_low, from_x_high, from_y_low, from_y_high, x_end):
        column, line = lax.axis_index("gx"), lax.axis_index("yz")
        low_end, high_end = line == 0, line == lax.axis_size("yz") - 1
        y_lows = faces(y_low, from_y_low, low_end, None, 1, False, len_x)
        y_highs = faces(y_high, from_y_high, high_end, None, 1, True, len_x)
        for c in range(ncomp):
            row_y_low[c] = (rim_y_low[c] + y_lows[c])[1 : len_x - 1]
            row_y_high[c] = (rim_y_high[c] + y_highs[c])[1 : len_x - 1]
        inner_x = pl.ds(1, len_x - 2)
        copies = [
            pltpu.make_async_copy(row_y_low, out.at[:, inner_x, 0], sems.at[0]),
            pltpu.make_async_copy(row_y_high, out.at[:, inner_x, len_y - 1], sems.at[1]),
        ]
        copies[0].start()
        copies[1].start()
        low_end, high_end = column == 0, column == lax.axis_size("gx") - 1
        x_lows = faces(x_low, from_x_low, low_end, x_end, 0, False, len_y)
        x_highs = faces(x_high, from_x_high, high_end, x_end, 0, True, len_y)
        for row, rim, changes, x, sem in (
            (row_x_low, rim_x_low, x_lows, 0, 2),
            (row_x_high, rim_x_high, x_highs, len_x - 1, 3),
        ):
            for c in range(ncomp):
                row[c] = rim[c] + changes[c]
                row[c, 0:1] = row[c, 0:1] + y_lows[c][x : x + 1]
                row[c, len_y - 1 : len_y] = row[c, len_y - 1 : len_y] + y_highs[c][x : x + 1]
            copies.append(pltpu.make_async_copy(row, out.at[:, x], sems.at[sem]))
            copies[-1].start()
        for copy in copies:
            copy.wait()

    @pl.when(helio)
    def _():
        both(x_two, x_one, y_two, y_one, from_x_one, from_x_two, from_y_one, from_y_two, None)

    @pl.when(jnp.logical_not(helio))
    def _():
        both(x_one, x_two, y_one, y_two, from_x_two, from_x_one, from_y_two, from_y_one, wrap)


def local(field_state, shell_owner, block_sources, block_targets, interp_weights):
    _, ncomp, len_x, len_y, len_z = field_state.shape
    n_gx, n_yz = lax.axis_size("gx"), lax.axis_size("yz")
    shells = shell_owner.shape[2]
    slots, depth = block_sources.shape[2:]
    volume = BLK * BLK * BLK
    cell_rows = ncomp * len_x * len_y
    grid = field_state.reshape(ncomp, len_x * len_y, len_z)
    weights = interp_weights.reshape(slots * depth, volume, volume)
    rows = BLK // 2 * ncomp
    dims = (ncomp, len_x, len_y, len_z)

    plan_rows = -(-slots * (depth + 1) // BLK) * BLK
    face_x = jax.ShapeDtypeStruct((ncomp * len_y, len_z), jnp.float32)
    face_y = jax.ShapeDtypeStruct((ncomp * len_x, len_z), jnp.float32)
    plane = len_x * len_y
    carried_planes = max(ncomp + 1, 16 * MIB // (4 * LANES * plane))
    *packed, carried, wrap = pl.pallas_call(
        functools.partial(pack_kernel, dims + (n_yz, shells, slots, depth)),
        out_shape=[jax.ShapeDtypeStruct((CAP, rows, LANES), jnp.bfloat16)] * n_yz
        + [
            jax.ShapeDtypeStruct((carried_planes, plane, len_z), jnp.float32),
            jax.ShapeDtypeStruct((ncomp, len_y, len_z), jnp.float32),
        ],
        in_specs=[HB] * 4,
        out_specs=[HB] * (n_yz + 2),
        scratch_shapes=[
            pltpu.VMEM((ncomp, plane + BLK, len_z), jnp.float32),
            pltpu.SMEM(shell_owner.shape, jnp.int32),
            pltpu.SMEM(block_sources.shape, jnp.int32),
            pltpu.SMEM(block_targets.shape, jnp.int32),
            pltpu.SMEM((n_yz * CAP + 1,), jnp.int32),
            pltpu.VMEM((plan_rows, LANES), jnp.float32),
            pltpu.VMEM((2 * BLK * LANES, SR * LANES), jnp.bfloat16),
            pltpu.VMEM((n_yz * CAP, rows, LANES), jnp.bfloat16),
            pltpu.SemaphoreType.DMA((2 * (len_x // BLK) + 5 + n_yz,)),
        ],
        compiler_params=pltpu.CompilerParams(vmem_limit_bytes=VMEM_BYTES - 8 * MIB),
        name="pack_shell",
    )(shell_owner, block_sources, block_targets, grid)

    moved = []
    for step in range(n_yz):
        pairs = [(t, n_yz + partner(t, step, n_yz)) for t in range(n_yz)]
        pairs = pairs + [(b, a) for a, b in pairs]
        moved.append(lax.ppermute(packed[step], ("dom", "yz"), pairs))

    staged = [
        jax.ShapeDtypeStruct(weights.shape, weights.dtype),
        jax.ShapeDtypeStruct((ncomp, plane, len_z), jnp.float32),
        jax.ShapeDtypeStruct((plan_rows, LANES), jnp.float32),
    ]
    staged_bytes = sum(x.size * x.dtype.itemsize for x in staged)
    room = pltpu.CompilerParams(vmem_limit_bytes=VMEM_BYTES - 17 * staged_bytes // 4)
    early_grid, wrap = pl.pallas_call(
        early_kernel,
        out_shape=[staged[1], jax.ShapeDtypeStruct(wrap.shape, wrap.dtype)],
        in_specs=[HB] * 2,
        out_specs=[VM, HB],
        scratch_shapes=[pltpu.SemaphoreType.DMA],
        input_output_aliases={1: 1},
        compiler_params=room,
        name="early_grid",
    )(carried, wrap)
    wrap = lax.ppermute(wrap, ("dom", "gx", "yz"), wrap_pairs(n_gx, n_yz))
    grid, plan = pl.pallas_call(
        stage_kernel,
        out_shape=staged[1:],
        in_specs=[HB] * 1,
        out_specs=[VM] * 2,
        scratch_shapes=[pltpu.SemaphoreType.DMA((2,))],
        compiler_params=room,
        cost_estimate=pl.CostEstimate(flops=0, bytes_accessed=4 * interp_weights.size, transcendentals=0),
        name="stage_operands",
    )(carried)

    filled, y_one, y_two, x_one, x_two = pl.pallas_call(
        functools.partial(fill_kernel, dims + (n_yz, slots, depth)),
        out_shape=[jax.ShapeDtypeStruct((cell_rows, len_z), jnp.float32), face_y, face_y, face_x, face_x],
        in_specs=[VM] * (4 + n_yz),
        out_specs=[VM] * 5,
        scratch_shapes=[
            pltpu.VMEM((2 * BLK * (slots * rows + BLK), LANES), jnp.float32),
            pltpu.SMEM((plan_rows, LANES), jnp.float32),
            pltpu.SemaphoreType.DMA,
        ],
        input_output_aliases={2: 0},
        compiler_params=pltpu.CompilerParams(vmem_limit_bytes=16 * MIB),
        name="fill_blocks",
    )(plan, weights, grid.reshape(cell_rows, len_z), early_grid.reshape(cell_rows, len_z), *moved)

    once_x, once_y = cycle(n_gx), cycle(n_yz)
    from_y_one = lax.ppermute(y_one, ("dom", "yz"), once_y)
    from_y_two = lax.ppermute(y_two, ("dom", "yz"), [(b, a) for a, b in once_y])
    from_x_one = lax.ppermute(x_one, ("dom", "gx"), once_x)
    from_x_two = lax.ppermute(x_two, ("dom", "gx"), [(b, a) for a, b in once_x])

    whole = jax.ShapeDtypeStruct((ncomp, len_x, len_y, len_z), jnp.float32)
    rim_x = jax.ShapeDtypeStruct((ncomp, len_y, len_z), jnp.float32)
    rim_y = jax.ShapeDtypeStruct((ncomp, len_x, len_z), jnp.float32)
    part, *rims = pl.pallas_call(
        functools.partial(inner_kernel, dims),
        out_shape=[whole, rim_x, rim_x, rim_y, rim_y],
        in_specs=[VM],
        out_specs=[HB] + [VM] * 4,
        scratch_shapes=[
            pltpu.VMEM((ncomp, len_x, len_y, len_z), jnp.float32),
            pltpu.SemaphoreType.DMA((len_x,)),
        ],
        compiler_params=pltpu.CompilerParams(vmem_limit_bytes=8 * MIB),
        cost_estimate=pl.CostEstimate(
            flops=300 * cell_rows * len_z, bytes_accessed=8 * cell_rows * len_z, transcendentals=0
        ),
        name="inner_faces",
    )(filled)

    updated = pl.pallas_call(
        functools.partial(edge_kernel, dims),
        out_shape=whole,
        in_specs=[HB] + [VM] * 13,
        out_specs=HB,
        scratch_shapes=[
            pltpu.VMEM((ncomp, len_y, len_z), jnp.float32),
            pltpu.VMEM((ncomp, len_y, len_z), jnp.float32),
            pltpu.VMEM((ncomp, len_x - 2, len_z), jnp.float32),
            pltpu.VMEM((ncomp, len_x - 2, len_z), jnp.float32),
            pltpu.SemaphoreType.DMA((4,)),
        ],
        input_output_aliases={0: 0},
        compiler_params=pltpu.CompilerParams(vmem_limit_bytes=8 * MIB),
        name="edge_faces",
    )(part, *rims, y_one, y_two, x_one, x_two, from_y_one, from_y_two, from_x_one, from_x_two, wrap.reshape(ncomp * len_y, len_z))
    return updated.reshape(1, ncomp, len_x, len_y, len_z)


def solution(mesh):
    placed = (
        P("dom", None, "gx", "yz", None),
        P("gx", None, None),
        P("gx", "yz", None, None),
        P("gx", "yz", None),
        P("gx", "yz", None, None, None, None),
    )
    return jax.shard_map(
        local,
        mesh=mesh,
        in_specs=placed,
        out_specs=P("dom", None, "gx", "yz", None),
        check_vma=False,
    )
```

```python
import functools

import jax
import jax.numpy as jnp
from jax import lax
from jax.experimental import pallas as pl
from jax.experimental.pallas import tpu as pltpu
from jax.sharding import PartitionSpec as P

BLK = 8
SR = 2
CAP = 2
LANES = 128
MIB = 2**20
VMEM_BYTES = 64 * MIB

HEAT_RATIO = 5.0 / 3.0
CORONA_RATIO = 0.04
HELIO_RATIO = 0.03

VM = pl.BlockSpec(memory_space=pltpu.VMEM)
HB = pl.BlockSpec(memory_space=pltpu.HBM)


def partner(index, step, count):
    if count & (count - 1) == 0:
        return index ^ step
    return (index + step) % count


def cycle(count):
    pairs = [(count + i, count + i + 1) for i in range(count - 1)] + [(2 * count - 1, count - 1)]
    return pairs + [(i + 1, i) for i in range(count - 1)] + [(0, count)]


def wrap_pairs(count, lines):
    def index(domain, column, line):
        return (domain * count + column) * lines + line

    pairs = []
    for t in range(lines):
        pairs.append((index(0, 0, t), index(0, count - 1, t)))
        pairs += [(index(0, g, t), index(1, g, t)) for g in range(1, count - 1)]
    pairs += [(index(1, g, t), index(1, g, t + 1)) for g in (0, count - 1) for t in range(0, lines - 1, 2)]
    return pairs + [(b, a) for a, b in pairs]


def pack_kernel(dims, owner_hbm, source_hbm, target_hbm, grid_hbm, *rest):
    ncomp, len_x, len_y, len_z, n_yz, shells, slots, depth = dims
    outs, carried, wrap = rest[:n_yz], rest[n_yz], rest[n_yz + 1]
    grid_ref, owner_ref, source_ref, target_ref, table, plan, spread, send, sems = rest[n_yz + 2 :]
    me = lax.axis_index("yz")
    plane = len_x * len_y
    n_bx, n_by, half = len_x // BLK, len_y // BLK, BLK // 2
    pitch = grid_ref.shape[1]
    flat = grid_ref.reshape(ncomp * pitch, len_z)
    onto = carried.at[pl.ds(0, ncomp)]
    slabs = [pl.ds(bx * BLK * len_y, BLK * len_y) for bx in range(n_bx)]
    grid_copies = [
        pltpu.make_async_copy(grid_hbm.at[:, slab, :], grid_ref.at[:, slab, :], sems.at[bx]) for bx, slab in enumerate(slabs)
    ]
    onward = [
        pltpu.make_async_copy(grid_ref.at[:, slab, :], onto.at[:, slab, :], sems.at[n_bx + bx])
        for bx, slab in enumerate(slabs)
    ]
    end = jnp.where(lax.axis_index("gx") == 0, 0, plane - len_y)
    first_sem = 2 * n_bx + 1
    wrap_copy = pltpu.make_async_copy(
        grid_ref.at[:, pl.ds(pl.multiple_of(end, BLK), len_y), :], wrap, sems.at[2 * n_bx]
    )
    copies = [
        pltpu.make_async_copy(owner_hbm, owner_ref, sems.at[first_sem]),
        pltpu.make_async_copy(source_hbm, source_ref, sems.at[first_sem + 1]),
        pltpu.make_async_copy(target_hbm, target_ref, sems.at[first_sem + 2]),
    ]

    @pl.when(lax.axis_index("dom") == 1)
    def _():
        for copy in copies:
            copy.start()
        for copy in grid_copies:
            copy.start()
        for copy in copies:
            copy.wait()
        position = jnp.int32(0)
        for t in range(n_yz):
            if n_yz & (n_yz - 1) == 0:
                step = t ^ me
            else:
                step = lax.rem(me - t + n_yz, n_yz)
            rank = jnp.int32(0)
            for b in range(shells):
                table[jnp.minimum(position, n_yz * CAP)] = step * CAP + jnp.minimum(rank, CAP - 1)
                mine = jnp.where(owner_ref[0, t, b] == me, 1, 0)
                position = position + mine
                rank = rank + mine
        for j in range(slots):
            for k in range(depth):
                entry = source_ref[0, 0, j, k]
                spot = jnp.where(entry >= 0, table[jnp.clip(entry, 0, n_yz * CAP)], -1)
                plan[j * depth + k : j * depth + k + 1, :] = jnp.full((1, LANES), spot.astype(jnp.float32))
            plan[slots * depth + j : slots * depth + j + 1, :] = jnp.full(
                (1, LANES), target_ref[0, 0, j].astype(jnp.float32)
            )
        told = pltpu.make_async_copy(plan, carried.at[ncomp, pl.ds(0, plan.shape[0])], sems.at[first_sem + 3])
        told.start()
        for arriving, leaving in zip(grid_copies, onward):
            arriving.wait()
            leaving.start()
        told.wait()
        for copy in onward:
            copy.wait()

    @pl.when(lax.axis_index("dom") == 0)
    def _():
        copies[0].start()
        for copy in grid_copies:
            copy.start()
        z_from = len_z - SR * BLK
        row_z = lax.broadcasted_iota(jnp.int32, (LANES, SR * LANES), 0) + (len_z - LANES)
        column = lax.broadcasted_iota(jnp.int32, (LANES, SR * LANES), 1)
        hit = row_z == z_from + column // LANES * BLK + column % BLK
        place = jnp.where(hit, column % LANES // BLK, -1)
        for m in range(2 * BLK):
            spread[m * LANES : (m + 1) * LANES, :] = jnp.where(place == m, 1.0, 0.0).astype(jnp.bfloat16)
        send[...] = jnp.zeros_like(send)
        copies[0].wait()
        spots = []
        for b in range(shells):
            owner = owner_ref[0, me, b]
            rank = jnp.int32(0)
            for other in range(b):
                rank = rank + jnp.where(owner_ref[0, me, other] == owner, 1, 0)
            if n_yz & (n_yz - 1) == 0:
                step = owner ^ me
            else:
                step = lax.rem(owner - me + n_yz, n_yz)
            spots.append(jnp.clip(step * CAP + rank, 0, n_yz * CAP - 1))
        rows = half * ncomp
        lines = []
        for bx in range(n_bx):
            grid_copies[bx].wait()
            onward[bx].start()
            line = []
            for ap in range(2):
                for cy in range(BLK):
                    pieces = []
                    for by in range(n_by):
                        for a2 in range(half):
                            first = (bx * BLK + a2 * 2 + ap) * len_y + by * BLK + cy
                            pieces.append(flat[pl.ds(first, ncomp, stride=pitch), :])
                    line.append(jnp.concatenate(pieces, axis=0).astype(jnp.bfloat16))
            lines.append(jnp.concatenate(line, axis=1))
        total = jnp.dot(jnp.concatenate(lines, axis=0), spread[...], preferred_element_type=jnp.float32)
        total = total.astype(jnp.bfloat16)
        for b in range(shells):
            column_block, br = b // SR, b % SR
            send[spots[b]] = total[
                column_block * rows : (column_block + 1) * rows, br * LANES : (br + 1) * LANES
            ]
        wrap_copy.start()
        sends = [
            pltpu.make_async_copy(send.at[pl.ds(step * CAP, CAP)], outs[step], sems.at[first_sem + 4 + step])
            for step in range(n_yz)
        ]
        for copy in sends:
            copy.start()
        for copy in [wrap_copy] + onward + sends:
            copy.wait()


def early(size):
    return (lax.axis_index("dom") == 0) & (lax.axis_index("gx") < size)


def early_kernel(carried, wrap_in, grid_ref, wrap_out, sem):
    @pl.when(early(1))
    def _():
        copy = pltpu.make_async_copy(carried.at[pl.ds(0, grid_ref.shape[0])], grid_ref, sem)
        copy.start()
        copy.wait()


def stage_kernel(carried, grid_ref, plan_ref, sems):
    ncomp, plan_rows = grid_ref.shape[0], plan_ref.shape[0]
    grid_copy = pltpu.make_async_copy(carried.at[pl.ds(0, ncomp)], grid_ref, sems.at[0])
    copies = [pltpu.make_async_copy(carried.at[ncomp, pl.ds(0, plan_rows)], plan_ref, sems.at[1]), grid_copy]

    @pl.when(lax.axis_index("dom") == 1)
    def _():
        for copy in copies:
            copy.start()
        for copy in copies:
            copy.wait()

    @pl.when((lax.axis_index("dom") == 0) & jnp.logical_not(early(1)))
    def _():
        grid_copy.start()
        grid_copy.wait()


def fill_kernel(dims, plan_vmem, weight_ref, grid_ref, early_ref, *rest):
    ncomp, len_x, len_y, len_z, n_yz, slots, depth = dims
    got = rest[:1] + rest[1:n_yz][::-1]
    filled, y_one, y_two, x_one, x_two, result, plan, sem = rest[n_yz:]
    half = BLK // 2
    rows = half * ncomp
    plane = len_x * len_y

    helio = lax.axis_index("dom") == 1
    ahead = early(1)

    @pl.when(ahead)
    def _():
        filled[...] = early_ref[...]

    @pl.when(jnp.logical_not(ahead))
    def _():
        filled[...] = grid_ref[...]

    @pl.when(helio)
    def _():
        copy = pltpu.make_async_copy(plan_vmem, plan, sem)
        copy.start()
        held = [
            got[step][slot].astype(jnp.float32)
            for step in range(n_yz)
            for slot in range(CAP)
        ]
        lines = []
        for j in range(slots):
            sources = []
            for k in range(depth):
                entry = j * depth + k
                spot = jnp.broadcast_to(plan_vmem[entry : entry + 1, :], (rows, LANES))
                block = jnp.zeros((rows, LANES), jnp.float32)
                for place, candidate in enumerate(held):
                    block = jnp.where(spot == float(place), candidate, block)
                sources += [block[a2 * ncomp : (a2 + 1) * ncomp, :] for a2 in range(half)]
            cells = jnp.concatenate(sources, axis=1).astype(jnp.bfloat16)
            dense = weight_ref[j * depth : (j + 1) * depth].reshape(depth * weight_ref.shape[1], weight_ref.shape[2])
            total = jnp.dot(cells, dense, preferred_element_type=jnp.float32)
            lines += [total[:, a2 * LANES : (a2 + 1) * LANES] for a2 in range(half)]
        lines = jnp.concatenate(lines, axis=0)
        top = lines.astype(jnp.bfloat16)
        rest = lines - top.astype(jnp.float32)
        middle = rest.astype(jnp.bfloat16)
        bottom = (rest - middle.astype(jnp.float32)).astype(jnp.bfloat16)
        lines = jnp.concatenate([top, middle, bottom], axis=0)
        count = slots * rows
        pitch = count + BLK
        from_lane = lax.broadcasted_iota(jnp.int32, (LANES, LANES), 0)
        to_lane = lax.broadcasted_iota(jnp.int32, (LANES, LANES), 1)
        same = from_lane % BLK == to_lane % BLK
        for m in range(2 * BLK):
            spread = jnp.where(same & (from_lane // BLK == m), 1.0, 0.0).astype(jnp.bfloat16)
            parts = jnp.dot(lines, spread, preferred_element_type=jnp.float32)
            result[m * pitch : m * pitch + count, :] = parts[:count] + parts[count : 2 * count] + parts[2 * count :]
        copy.wait()
        lane = lax.broadcasted_iota(jnp.int32, (BLK, LANES), 1)
        per_y, per_z = len_y // BLK, len_z // BLK
        for j in range(slots):
            target = plan[slots * depth + j, 0].astype(jnp.int32)

            @pl.when(target >= 0)
            def _():
                block_x = target // (per_y * per_z)
                block_y = target // per_z % per_y
                z_from = target % per_z * BLK
                inside = (lane >= z_from) & (lane < z_from + BLK)
                first = block_x * BLK * len_y + block_y * BLK
                for a in range(BLK):
                    spots = [
                        pl.ds(pl.multiple_of(first + c * plane + a * len_y, BLK), BLK) for c in range(ncomp)
                    ]
                    row = a % 2 * BLK * pitch + j * rows + a // 2 * ncomp
                    old = [filled[spot, :] for spot in spots]
                    new = [result[pl.ds(row + c, BLK, stride=pitch), :] for c in range(ncomp)]
                    for spot, before, after in zip(spots, old, new):
                        filled[spot, :] = jnp.where(inside, after, before)

    def faces(x_low, x_high, y_low, y_high):
        for c in range(ncomp):
            x_low[c * len_y : (c + 1) * len_y, :] = filled[c * plane : c * plane + len_y, :]
            x_high[c * len_y : (c + 1) * len_y, :] = filled[(c + 1) * plane - len_y : (c + 1) * plane, :]
            y_low[c * len_x : (c + 1) * len_x, :] = filled[pl.ds(c * plane, len_x, stride=len_y), :]
            y_high[c * len_x : (c + 1) * len_x, :] = filled[
                pl.ds(c * plane + len_y - 1, len_x, stride=len_y), :
            ]

    @pl.when(helio)
    def _():
        faces(x_two, x_one, y_two, y_one)

    @pl.when(jnp.logical_not(helio))
    def _():
        faces(x_one, x_two, y_one, y_two)


def primitives(cells):
    density, energy = cells[0], cells[7]
    momentum, magnetic = cells[1:4], cells[4:7]
    inverse = 1.0 / density
    velocity = [m * inverse for m in momentum]
    field_sq = magnetic[0] * magnetic[0] + magnetic[1] * magnetic[1] + magnetic[2] * magnetic[2]
    kinetic = momentum[0] * velocity[0] + momentum[1] * velocity[1] + momentum[2] * velocity[2]
    pressure = (HEAT_RATIO - 1.0) * (energy - 0.5 * kinetic - 0.5 * field_sq)
    total_pressure = pressure + 0.5 * field_sq
    dot = velocity[0] * magnetic[0] + velocity[1] * magnetic[1] + velocity[2] * magnetic[2]
    fast = jnp.sqrt((HEAT_RATIO * pressure + field_sq) * inverse)
    return velocity, total_pressure, energy + total_pressure, dot, fast


def flux_of(cells, prims, direction):
    velocity, total_pressure, enthalpy, dot, fast = prims
    momentum, magnetic = cells[1:4], cells[4:7]
    speed, field = velocity[direction], magnetic[direction]
    flux = [momentum[direction]]
    for other in range(3):
        term = momentum[other] * speed - magnetic[other] * field
        flux.append(term + total_pressure if other == direction else term)
    for other in range(3):
        if other == direction:
            flux.append(None)
        else:
            flux.append(speed * magnetic[other] - field * velocity[other])
    flux.append(enthalpy * speed - field * dot)
    return flux, jnp.abs(speed) + fast


def face_sum(low, high):
    fastest = jnp.maximum(low[2], high[2])
    out = []
    for u_low, u_high, f_low, f_high in zip(low[0], high[0], low[1], high[1]):
        face = fastest * (u_high - u_low)
        out.append(face if f_low is None else face - (f_low + f_high))
    return out


def inner_kernel(dims, filled, out, rim_x_low, rim_x_high, rim_y_low, rim_y_high, part, sems):
    ncomp, len_x, len_y, len_z = dims
    plane = len_x * len_y
    half_ratio = jnp.where(lax.axis_index("dom") == 0, 0.5 * CORONA_RATIO, 0.5 * HELIO_RATIO).astype(jnp.float32)
    shape = (len_y, LANES)
    row = lax.broadcasted_iota(jnp.int32, shape, 0)
    lane = lax.broadcasted_iota(jnp.int32, shape, 1)

    def load(x):
        return [filled[pl.ds(pl.multiple_of(c * plane + x * len_y, BLK), len_y), :] for c in range(ncomp)]

    def shift_up(values, axis, size):
        return [None if v is None else pltpu.roll(v, size - 1, axis) for v in values]

    def step(x, carry, last):
        cells, prims, flux_x, speed_x, low_x = carry
        if last:
            high_x = [jnp.zeros(shape, jnp.float32)] * ncomp
            next_carry = None
        else:
            next_cells = load(x + 1)
            next_prims = primitives(next_cells)
            next_flux, next_speed = flux_of(next_cells, next_prims, 0)
            high_x = face_sum((cells, flux_x, speed_x), (next_cells, next_flux, next_speed))
            next_carry = (next_cells, next_prims, next_flux, next_speed, high_x)
        total = [high - low for high, low in zip(high_x, low_x)]
        flux, speed = flux_of(cells, prims, 1)
        beside = (shift_up(cells, 0, len_y), shift_up(flux, 0, len_y), pltpu.roll(speed, len_y - 1, 0))
        for c, face in enumerate(face_sum((cells, flux, speed), beside)):
            face = jnp.where(row == len_y - 1, 0.0, face)
            total[c] = total[c] + (face - pltpu.roll(face, 1, 0))
        flux, speed = flux_of(cells, prims, 2)
        beside = (shift_up(cells, 1, LANES), shift_up(flux, 1, LANES), pltpu.roll(speed, LANES - 1, 1))
        for c, face in enumerate(face_sum((cells, flux, speed), beside)):
            own = jnp.zeros(shape, jnp.float32) if flux[c] is None else -2.0 * flux[c]
            face = jnp.where(lane == LANES - 1, own, face)
            below = jnp.where(lane == 0, own, pltpu.roll(face, 1, 1))
            total[c] = total[c] + (face - below)
        for c in range(ncomp):
            part[c, x] = cells[c] + half_ratio * total[c]
        return next_carry

    def line_copy(x):
        return pltpu.make_async_copy(part.at[:, x], out.at[:, x], sems.at[x])

    cells = load(0)
    prims = primitives(cells)
    flux, speed = flux_of(cells, prims, 0)
    flux[4] = None
    zero = [jnp.zeros(shape, jnp.float32)] * ncomp
    carry = (cells, prims, flux, speed, zero)

    def pack(carry):
        cells, prims, flux, speed, low = carry
        return cells, prims, [f for f in flux if f is not None], speed, low

    def unpack(carry):
        cells, prims, flux, speed, low = carry
        return cells, prims, flux[:4] + [None] + flux[4:], speed, low

    def line(x, carry):
        carry = pack(step(x, unpack(carry), False))

        @pl.when(x > 0)
        def _():
            line_copy(x).start()

        return carry

    carry = lax.fori_loop(0, len_x - 1, line, pack(carry), unroll=3)
    step(len_x - 1, unpack(carry), True)
    for c in range(ncomp):
        rim_x_low[c] = part[c, 0]
        rim_x_high[c] = part[c, len_x - 1]
        rim_y_low[c] = part[c, :, 0, :]
        rim_y_high[c] = part[c, :, len_y - 1, :]
    for x in range(1, len_x - 1):
        line_copy(x).wait()


def edge_kernel(dims, part, rim_x_low, rim_x_high, rim_y_low, rim_y_high, *rest):
    ncomp, len_x, len_y, len_z = dims
    y_one, y_two, x_one, x_two, from_y_one, from_y_two, from_x_one, from_x_two, wrap = rest[:9]
    out, row_x_low, row_x_high, row_y_low, row_y_high, sems = rest[9:]
    helio = lax.axis_index("dom") == 1
    half_ratio = jnp.where(helio, 0.5 * HELIO_RATIO, 0.5 * CORONA_RATIO).astype(jnp.float32)

    def state(cells, direction):
        flux, speed = flux_of(cells, primitives(cells), direction)
        return cells, flux, speed

    def faces(own_ref, other_ref, end, end_ref, direction, upper, size):
        own = [own_ref[c * size : (c + 1) * size, :] for c in range(ncomp)]
        other = [other_ref[c * size : (c + 1) * size, :] for c in range(ncomp)]
        at_end = own if end_ref is None else [end_ref[c * size : (c + 1) * size, :] for c in range(ncomp)]
        other = [jnp.where(end, u, v) for u, v in zip(at_end, other)]
        own, other = state(own, direction), state(other, direction)
        if upper:
            return [half_ratio * f for f in face_sum(own, other)]
        return [-half_ratio * f for f in face_sum(other, own)]

    def both(x_low, x_high, y_low, y_high, from_x_low, from_x_high, from_y_low, from_y_high, x_end):
        column, line = lax.axis_index("gx"), lax.axis_index("yz")
        low_end, high_end = line == 0, line == lax.axis_size("yz") - 1
        y_lows = faces(y_low, from_y_low, low_end, None, 1, False, len_x)
        y_highs = faces(y_high, from_y_high, high_end, None, 1, True, len_x)
        for c in range(ncomp):
            row_y_low[c] = (rim_y_low[c] + y_lows[c])[1 : len_x - 1]
            row_y_high[c] = (rim_y_high[c] + y_highs[c])[1 : len_x - 1]
        inner_x = pl.ds(1, len_x - 2)
        copies = [
            pltpu.make_async_copy(row_y_low, out.at[:, inner_x, 0], sems.at[0]),
            pltpu.make_async_copy(row_y_high, out.at[:, inner_x, len_y - 1], sems.at[1]),
        ]
        copies[0].start()
        copies[1].start()
        low_end, high_end = column == 0, column == lax.axis_size("gx") - 1
        x_lows = faces(x_low, from_x_low, low_end, x_end, 0, False, len_y)
        x_highs = faces(x_high, from_x_high, high_end, x_end, 0, True, len_y)
        for row, rim, changes, x, sem in (
            (row_x_low, rim_x_low, x_lows, 0, 2),
            (row_x_high, rim_x_high, x_highs, len_x - 1, 3),
        ):
            for c in range(ncomp):
                row[c] = rim[c] + changes[c]
                row[c, 0:1] = row[c, 0:1] + y_lows[c][x : x + 1]
                row[c, len_y - 1 : len_y] = row[c, len_y - 1 : len_y] + y_highs[c][x : x + 1]
            copies.append(pltpu.make_async_copy(row, out.at[:, x], sems.at[sem]))
            copies[-1].start()
        for copy in copies:
            copy.wait()

    @pl.when(helio)
    def _():
        both(x_two, x_one, y_two, y_one, from_x_one, from_x_two, from_y_one, from_y_two, None)

    @pl.when(jnp.logical_not(helio))
    def _():
        both(x_one, x_two, y_one, y_two, from_x_two, from_x_one, from_y_two, from_y_one, wrap)


def local(field_state, shell_owner, block_sources, block_targets, interp_weights):
    _, ncomp, len_x, len_y, len_z = field_state.shape
    n_gx, n_yz = lax.axis_size("gx"), lax.axis_size("yz")
    shells = shell_owner.shape[2]
    slots, depth = block_sources.shape[2:]
    volume = BLK * BLK * BLK
    cell_rows = ncomp * len_x * len_y
    grid = field_state.reshape(ncomp, len_x * len_y, len_z)
    weights = interp_weights.reshape(slots * depth, volume, volume)
    rows = BLK // 2 * ncomp
    dims = (ncomp, len_x, len_y, len_z)

    plan_rows = -(-slots * (depth + 1) // BLK) * BLK
    face_x = jax.ShapeDtypeStruct((ncomp * len_y, len_z), jnp.float32)
    face_y = jax.ShapeDtypeStruct((ncomp * len_x, len_z), jnp.float32)
    plane = len_x * len_y
    carried_planes = max(ncomp + 1, 16 * MIB // (4 * LANES * plane))
    *packed, carried, wrap = pl.pallas_call(
        functools.partial(pack_kernel, dims + (n_yz, shells, slots, depth)),
        out_shape=[jax.ShapeDtypeStruct((CAP, rows, LANES), jnp.bfloat16)] * n_yz
        + [
            jax.ShapeDtypeStruct((carried_planes, plane, len_z), jnp.float32),
            jax.ShapeDtypeStruct((ncomp, len_y, len_z), jnp.float32),
        ],
        in_specs=[HB] * 4,
        out_specs=[HB] * (n_yz + 2),
        scratch_shapes=[
            pltpu.VMEM((ncomp, plane + BLK, len_z), jnp.float32),
            pltpu.SMEM(shell_owner.shape, jnp.int32),
            pltpu.SMEM(block_sources.shape, jnp.int32),
            pltpu.SMEM(block_targets.shape, jnp.int32),
            pltpu.SMEM((n_yz * CAP + 1,), jnp.int32),
            pltpu.VMEM((plan_rows, LANES), jnp.float32),
            pltpu.VMEM((2 * BLK * LANES, SR * LANES), jnp.bfloat16),
            pltpu.VMEM((n_yz * CAP, rows, LANES), jnp.bfloat16),
            pltpu.SemaphoreType.DMA((2 * (len_x // BLK) + 5 + n_yz,)),
        ],
        compiler_params=pltpu.CompilerParams(vmem_limit_bytes=VMEM_BYTES - 8 * MIB),
        name="pack_shell",
    )(shell_owner, block_sources, block_targets, grid)

    moved = []
    for step in range(n_yz):
        pairs = [(t, n_yz + partner(t, step, n_yz)) for t in range(n_yz)]
        pairs = pairs + [(b, a) for a, b in pairs]
        moved.append(lax.ppermute(packed[step], ("dom", "yz"), pairs))

    staged = [
        jax.ShapeDtypeStruct(weights.shape, weights.dtype),
        jax.ShapeDtypeStruct((ncomp, plane, len_z), jnp.float32),
        jax.ShapeDtypeStruct((plan_rows, LANES), jnp.float32),
    ]
    staged_bytes = sum(x.size * x.dtype.itemsize for x in staged)
    room = pltpu.CompilerParams(vmem_limit_bytes=VMEM_BYTES - 17 * staged_bytes // 4)
    early_grid, wrap = pl.pallas_call(
        early_kernel,
        out_shape=[staged[1], jax.ShapeDtypeStruct(wrap.shape, wrap.dtype)],
        in_specs=[HB] * 2,
        out_specs=[VM, HB],
        scratch_shapes=[pltpu.SemaphoreType.DMA],
        input_output_aliases={1: 1},
        compiler_params=room,
        name="early_grid",
    )(carried, wrap)
    wrap = lax.ppermute(wrap, ("dom", "gx", "yz"), wrap_pairs(n_gx, n_yz))
    grid, plan = pl.pallas_call(
        stage_kernel,
        out_shape=staged[1:],
        in_specs=[HB] * 1,
        out_specs=[VM] * 2,
        scratch_shapes=[pltpu.SemaphoreType.DMA((2,))],
        compiler_params=room,
        cost_estimate=pl.CostEstimate(flops=0, bytes_accessed=4 * interp_weights.size, transcendentals=0),
        name="stage_operands",
    )(carried)

    filled, y_one, y_two, x_one, x_two = pl.pallas_call(
        functools.partial(fill_kernel, dims + (n_yz, slots, depth)),
        out_shape=[jax.ShapeDtypeStruct((cell_rows, len_z), jnp.float32), face_y, face_y, face_x, face_x],
        in_specs=[VM] * (4 + n_yz),
        out_specs=[VM] * 5,
        scratch_shapes=[
            pltpu.VMEM((2 * BLK * (slots * rows + BLK), LANES), jnp.float32),
            pltpu.SMEM((plan_rows, LANES), jnp.float32),
            pltpu.SemaphoreType.DMA,
        ],
        input_output_aliases={2: 0},
        compiler_params=pltpu.CompilerParams(vmem_limit_bytes=16 * MIB),
        name="fill_blocks",
    )(plan, weights, grid.reshape(cell_rows, len_z), early_grid.reshape(cell_rows, len_z), moved[0], *moved[:0:-1])

    once_x, once_y = cycle(n_gx), cycle(n_yz)
    from_y_one = lax.ppermute(y_one, ("dom", "yz"), once_y)
    from_y_two = lax.ppermute(y_two, ("dom", "yz"), [(b, a) for a, b in once_y])
    from_x_one = lax.ppermute(x_one, ("dom", "gx"), once_x)
    from_x_two = lax.ppermute(x_two, ("dom", "gx"), [(b, a) for a, b in once_x])

    whole = jax.ShapeDtypeStruct((ncomp, len_x, len_y, len_z), jnp.float32)
    rim_x = jax.ShapeDtypeStruct((ncomp, len_y, len_z), jnp.float32)
    rim_y = jax.ShapeDtypeStruct((ncomp, len_x, len_z), jnp.float32)
    part, *rims = pl.pallas_call(
        functools.partial(inner_kernel, dims),
        out_shape=[whole, rim_x, rim_x, rim_y, rim_y],
        in_specs=[VM],
        out_specs=[HB] + [VM] * 4,
        scratch_shapes=[
            pltpu.VMEM((ncomp, len_x, len_y, len_z), jnp.float32),
            pltpu.SemaphoreType.DMA((len_x,)),
        ],
        compiler_params=pltpu.CompilerParams(vmem_limit_bytes=8 * MIB),
        cost_estimate=pl.CostEstimate(
            flops=300 * cell_rows * len_z, bytes_accessed=8 * cell_rows * len_z, transcendentals=0
        ),
        name="inner_faces",
    )(filled)

    updated = pl.pallas_call(
        functools.partial(edge_kernel, dims),
        out_shape=whole,
        in_specs=[HB] + [VM] * 13,
        out_specs=HB,
        scratch_shapes=[
            pltpu.VMEM((ncomp, len_y, len_z), jnp.float32),
            pltpu.VMEM((ncomp, len_y, len_z), jnp.float32),
            pltpu.VMEM((ncomp, len_x - 2, len_z), jnp.float32),
            pltpu.VMEM((ncomp, len_x - 2, len_z), jnp.float32),
            pltpu.SemaphoreType.DMA((4,)),
        ],
        input_output_aliases={0: 0},
        compiler_params=pltpu.CompilerParams(vmem_limit_bytes=8 * MIB),
        name="edge_faces",
    )(part, *rims, y_one, y_two, x_one, x_two, from_y_one, from_y_two, from_x_one, from_x_two, wrap.reshape(ncomp * len_y, len_z))
    return updated.reshape(1, ncomp, len_x, len_y, len_z)


def solution(mesh):
    placed = (
        P("dom", None, "gx", "yz", None),
        P("gx", None, None),
        P("gx", "yz", None, None),
        P("gx", "yz", None),
        P("gx", "yz", None, None, None, None),
    )
    return jax.shard_map(
        local,
        mesh=mesh,
        in_specs=placed,
        out_specs=P("dom", None, "gx", "yz", None),
        check_vma=False,
    )
```
